32 devices in a mesh: rows: 4 (over z), cols: 8 (over y, x, core).
Axes of the slice: x: 2, y: 2, z: 4, core: 2. Of those that a mesh axis runs over, the one named last changes fastest.
Arguments:
- model_dir: float32 [65536, 128], P('cols'), may hold values from -6 to 6
- sens_blocks: bfloat16 [4, 3072, 128, 128], P('rows', 'cols'), may hold values from -0.09375 to 0.09375
- blk_row: int32 [4, 3072], P('rows', 'cols'), may hold values from 0 to 31, as said below
- blk_col: int32 [4, 3072], P('rows', 'cols'), may hold values from 0 to 63, as said below
- blk_count: int32 [4, 8], P('rows', 'cols'), may hold values from 48 to 384, as said below
- send_order: int32 [8, 64], P('cols'), may hold values from 0 to 63, each once within a row
- neighbors: int32 [4, 65536], P(None, 'cols'), may hold values from 0 to 65535, as said below
- face_weight: float32 [4, 65536], P(None, 'cols'), may hold values from 0.05 to 0.5
Outputs:
- data_image: float32 [16384, 128], P('rows')
- normal_product: float32 [65536, 128], P('cols')
The draws below stay inside these ranges and needn't reach their ends.
Inputs may be any that keep to these rules, and one draw needn't show every extreme that they name: Within one device's 384 slots the pairs (blk_row, blk_col) are all different. `blk_col`: paired with blk_row as stated there. The live slots of a device are its first blk_count slots; some device has all 384 live. `send_order`: each row is a permutation. `neighbors`: every neighbour lies within 64 of the cell's own number.
All inputs are finite; a program needn't handle non-finite values.
Results may differ from the reference program's by a relative error of at most 0.0029.
Values may be sent and summed in bfloat16 or wider, within the bound.
No kernel may reach another device: no remote copies, remote signals or barrier semaphores. Data moves between devices by JAX's collectives and lax.ppermute only.
A program may use at most 192 MiB of HBM per device.

```python
import math
import jax
import jax.numpy as jnp
from jax import lax

BLK = 128
NV = 128
RB_DEV = 32
NB_DEV = 64
KB = 384
RIM = 64
PER = 8
CB = 512
NCELL = 65536
ND = 16384
N_ROWS = 4
N_COLS = 8


def block_pairs(key):
    key_list = jax.random.split(jax.random.fold_in(key, 7), N_ROWS * N_COLS)

    def pick_one(subkey):
        return jax.random.permutation(subkey, RB_DEV * NB_DEV)[:KB]
    chosen = jax.vmap(pick_one)(key_list)
    return chosen.reshape(N_ROWS, N_COLS * KB).astype(jnp.int32)


def draw_blk_row(key, part):
    return block_pairs(key) // NB_DEV


def draw_blk_col(key, part):
    return block_pairs(key) % NB_DEV


def draw_blk_count(key, part):
    lowest = KB // 8
    first_draw = jax.random.randint(jax.random.fold_in(key, 3), (N_ROWS * N_COLS,), 0, KB + 1)
    second_draw = jax.random.randint(jax.random.fold_in(key, 4), (N_ROWS * N_COLS,), 0, KB + 1)
    counts = lowest + (KB - lowest) * first_draw * second_draw // (KB * KB)
    busiest = jax.random.randint(jax.random.fold_in(key, 5), (), 0, N_ROWS * N_COLS)
    counts = jnp.where(jnp.arange(N_ROWS * N_COLS) == busiest, KB, counts)
    return counts.reshape(N_ROWS, N_COLS).astype(jnp.int32)


def draw_neighbors(key, part):
    offsets = jax.random.randint(jax.random.fold_in(key, 9), (4, NCELL), -RIM, RIM + 1)
    own_index = jnp.arange(NCELL, dtype=jnp.int32)[None, :]
    return jnp.clip(own_index + offsets, 0, NCELL - 1).astype(jnp.int32)


def block_scale(rng, dims, pieces, least, largest):
    def one(axis_at, parts):
        heights = jax.random.uniform(jax.random.fold_in(jax.random.fold_in(rng, 6), axis_at), (parts,), jnp.float32, least / len(pieces), largest / len(pieces))
        return jnp.repeat(jnp.exp(heights), dims[axis_at] // parts).reshape((-1,) + (1,) * (len(dims) - axis_at - 1))

    level = one(*pieces[0])
    for cut in pieces[1:]:
        level = level * one(*cut)
    return level


def normal_values(rng, extent, spread, limit, cuts=(), kind=jnp.bfloat16):
    entries = spread * jax.random.normal(rng, extent, jnp.float32)
    if cuts:
        entries = entries * block_scale(rng, extent, cuts, -0.22, 0.18)
    return jnp.clip(entries, -limit, limit).astype(kind)


def setup_inputs(seed: int = 0) -> dict:
    arg_keys = jax.random.split(jax.random.key(seed), 9)
    return {
        "model_dir": normal_values(arg_keys[0], (NCELL, NV), 1.0, 6.0, ((0, 8),), jnp.float32),
        "sens_blocks": normal_values(arg_keys[1], (N_ROWS, N_COLS * KB, BLK, BLK), (BLK * KB * N_COLS // (3 * RB_DEV)) ** -0.5, 0.09375, ((0, 4), (1, 8))),
        "blk_row": draw_blk_row(jax.random.fold_in(arg_keys[8], 71), 0),
        "blk_col": draw_blk_col(jax.random.fold_in(arg_keys[8], 71), 0),
        "blk_count": draw_blk_count(jax.random.fold_in(arg_keys[8], 71), 0),
        "send_order": jax.vmap(lambda own: jax.random.permutation(own, NB_DEV))(jax.random.split(arg_keys[5], N_COLS)).reshape((N_COLS, NB_DEV)).astype(jnp.int32),
        "neighbors": draw_neighbors(jax.random.fold_in(arg_keys[8], 71), 0),
        "face_weight": jnp.clip(jnp.exp(math.log(0.5) - 2.3025851 * jax.random.uniform(arg_keys[7], (4, NCELL), jnp.float32) ** block_scale(arg_keys[7], (4, NCELL), ((1, 8),), -0.2, 0.2)), 0.05, 0.5),
    }


def haar_matrix(order_n):
    matrix = jnp.ones((1, 1), jnp.float32)
    factor = 1.0 / math.sqrt(2.0)
    while matrix.shape[0] < order_n:
        length = matrix.shape[0]
        upper_half = jnp.kron(matrix, jnp.array([[1.0, 1.0]], jnp.float32))
        lower_half = jnp.kron(jnp.eye(length, dtype=jnp.float32), jnp.array([[1.0, -1.0]], jnp.float32))
        matrix = jnp.concatenate([upper_half, lower_half], axis=0) * factor
    return matrix

def reference(model_dir, sens_blocks, blk_row, blk_col, blk_count, send_order, neighbors, face_weight):
    highest = lax.Precision.HIGHEST
    haar_basis = jnp.asarray(haar_matrix(BLK), jnp.float32)
    cell_blocks = model_dir.reshape(N_COLS, NB_DEV, BLK, NV)
    coeffs = jnp.einsum('ij,sbjn->sbin', haar_basis, cell_blocks, precision=highest).astype(jnp.bfloat16)
    ordered = jnp.take_along_axis(coeffs, send_order[:, :, None, None], axis=1)
    wavelet = ordered.reshape(N_COLS, N_COLS, PER, BLK, NV).transpose(1, 0, 2, 3, 4).reshape(CB, BLK, NV)
    slot_index = jnp.arange(KB).astype(jnp.int32)
    group_index = jnp.arange(N_COLS).astype(jnp.int32)
    adjoint_wave = jnp.zeros((CB, BLK, NV), jnp.float32)
    image_rows = []
    for row_group in range(N_ROWS):
        group_sens = sens_blocks[row_group]
        group_rows = blk_row[row_group]
        group_cols = blk_col[row_group]
        group_count = blk_count[row_group]

        def lists_of(col_group):
            first_slot = (col_group * KB).astype(jnp.int32)
            blocks_here = lax.dynamic_slice_in_dim(group_sens, first_slot, KB, 0).astype(jnp.float32)
            rows_here = lax.dynamic_slice_in_dim(group_rows, first_slot, KB, 0)
            cols_here = lax.dynamic_slice_in_dim(group_cols, first_slot, KB, 0)
            live_slot = slot_index < group_count[col_group]
            return (blocks_here, rows_here, cols_here, live_slot)

        def forward(col_group):
            blocks_here, rows_here, cols_here, live_slot = lists_of(col_group)
            picked = wavelet[cols_here + col_group * NB_DEV].astype(jnp.float32)
            terms = jnp.einsum('kij,kjn->kin', blocks_here, picked)
            terms = jnp.where(live_slot[:, None, None], terms, 0.0)
            return jax.ops.segment_sum(terms, rows_here, num_segments=RB_DEV)
        image_group = lax.optimization_barrier(jnp.sum(lax.map(forward, group_index), axis=0))
        image_half = image_group.astype(jnp.bfloat16)

        def adjoint(col_group):
            blocks_here, rows_here, cols_here, live_slot = lists_of(col_group)
            chosen = image_half[rows_here].astype(jnp.float32)
            terms = jnp.einsum('kij,kin->kjn', blocks_here, chosen)
            terms = jnp.where(live_slot[:, None, None], terms, 0.0)
            return jax.ops.segment_sum(terms, cols_here, num_segments=NB_DEV)
        adjoint_parts = lax.map(adjoint, group_index)
        adjoint_wave = adjoint_wave + adjoint_parts.reshape(CB, BLK, NV)
        image_rows.append(image_group)
    data_image = jnp.concatenate(image_rows, axis=0).reshape(ND, NV)
    by_source = adjoint_wave.reshape(N_COLS, N_COLS, PER, BLK, NV).transpose(1, 0, 2, 3, 4).reshape(N_COLS, NB_DEV, BLK, NV)
    inverse = jnp.argsort(send_order, axis=1).astype(jnp.int32)
    cell_side = jnp.take_along_axis(by_source, inverse[:, :, None, None], axis=1)
    adjoint_cells = jnp.einsum('ji,sbjn->sbin', haar_basis, cell_side, precision=highest).reshape(NCELL, NV)
    beside_all = model_dir[neighbors]
    smooth_term = lax.optimization_barrier(jnp.sum(face_weight[:, :, None] * (model_dir[None, :, :] - beside_all), axis=0))
    normal_product = adjoint_cells + smooth_term
    return (data_image, normal_product)
```

```python
import math

import jax
import jax.numpy as jnp
import numpy as np
from jax import lax
from jax.experimental import pallas as pl
from jax.experimental.pallas import tpu as pltpu
from jax.sharding import PartitionSpec as P

BLK = 128
RB_DEV = 32
RIM = 64
STEP = 16
MIB = 1 << 20


def haar_matrix(order_n):
    matrix = np.ones((1, 1))
    while matrix.shape[0] < order_n:
        length = matrix.shape[0]
        upper = np.kron(matrix, np.array([[1.0, 1.0]]))
        lower = np.kron(np.eye(length), np.array([[1.0, -1.0]]))
        matrix = np.concatenate([upper, lower], axis=0) / math.sqrt(2.0)
    return matrix


def split3(x):
    hi = x.astype(jnp.bfloat16)
    rest = x - hi.astype(jnp.float32)
    mid = rest.astype(jnp.bfloat16)
    low = (rest - mid.astype(jnp.float32)).astype(jnp.bfloat16)
    return jnp.concatenate([hi, mid, low], axis=0)


def analyze_body(place_ref, sign_ref, scale_ref, model_ref, out_ref):
    per_step = model_ref.shape[0]
    first = pl.program_id(0) * per_step
    for b in range(per_step):
        parts = split3(model_ref[b])
        raw = jnp.dot(sign_ref[...], parts, preferred_element_type=jnp.float32)
        out_ref[place_ref[first + b]] = (raw * scale_ref[...]).astype(jnp.bfloat16)


def analyze(place, model_blocks):
    blocks = model_blocks.shape[0]
    width = model_blocks.shape[2]
    per_step = 8
    haar = haar_matrix(BLK)
    scale = np.abs(haar).max(axis=1)
    sign = np.sign(haar)
    signs = jnp.asarray(np.concatenate([sign, sign, sign], axis=1), jnp.bfloat16)
    scales = jnp.asarray(np.broadcast_to(scale[:, None], (BLK, width)), jnp.float32)
    return pl.pallas_call(
        analyze_body,
        out_shape=jax.ShapeDtypeStruct((blocks, BLK, width), jnp.bfloat16),
        grid_spec=pltpu.PrefetchScalarGridSpec(
            num_scalar_prefetch=1,
            grid=(blocks // per_step,),
            in_specs=[
                pl.BlockSpec((BLK, 3 * BLK), lambda i, *_: (0, 0)),
                pl.BlockSpec((BLK, width), lambda i, *_: (0, 0)),
                pl.BlockSpec((per_step, BLK, width), lambda i, *_: (i, 0, 0)),
            ],
            out_specs=pl.BlockSpec((blocks, BLK, width), lambda i, *_: (0, 0, 0)),
        ),
        compiler_params=pltpu.CompilerParams(vmem_limit_bytes=24 * MIB),
        cost_estimate=pl.CostEstimate(
            flops=6 * blocks * BLK * BLK * width, bytes_accessed=6 * blocks * BLK * width,
            transcendentals=0,
        ),
        name="analyze",
    )(place, signs, scales, model_blocks)


def forward_body(rows_ref, cols_ref, count_ref, sens_ref, wave_ref, out_ref, acc_ref):
    step = pl.program_id(0)
    row_blocks = out_ref.shape[0]

    @pl.when(step == 0)
    def _():
        acc_ref[...] = jnp.zeros_like(acc_ref)

    @pl.when(step * STEP < count_ref[0])
    def _():
        for k in range(STEP):
            slot = step * STEP + k
            row = jnp.where(slot < count_ref[0], rows_ref[slot], row_blocks)
            acc_ref[row] += jnp.dot(
                sens_ref[k], wave_ref[cols_ref[slot]], preferred_element_type=jnp.float32
            )

    @pl.when(step == pl.num_programs(0) - 1)
    def _():
        out_ref[...] = acc_ref[:row_blocks].astype(out_ref.dtype)


def live_step(i, rows_ref, cols_ref, count_ref):
    return (jnp.minimum(i, (count_ref[0] - 1) // STEP), 0, 0)


def forward(rows, cols, count, sens, wave):
    slots = sens.shape[0]
    width = wave.shape[2]
    return pl.pallas_call(
        forward_body,
        out_shape=jax.ShapeDtypeStruct((RB_DEV, BLK, width), jnp.bfloat16),
        grid_spec=pltpu.PrefetchScalarGridSpec(
            num_scalar_prefetch=3,
            grid=(slots // STEP,),
            in_specs=[
                pl.BlockSpec((STEP, BLK, BLK), live_step),
                pl.BlockSpec(wave.shape, lambda i, *_: (0, 0, 0)),
            ],
            out_specs=pl.BlockSpec((RB_DEV, BLK, width), lambda i, *_: (0, 0, 0)),
            scratch_shapes=[pltpu.VMEM((RB_DEV + 1, BLK, width), jnp.float32)],
        ),
        compiler_params=pltpu.CompilerParams(vmem_limit_bytes=24 * MIB),
        cost_estimate=pl.CostEstimate(
            flops=2 * slots * BLK * BLK * width, bytes_accessed=2 * slots * BLK * BLK,
            transcendentals=0,
        ),
        name="forward",
    )(rows, cols, count, sens, wave)


def adjoint_body(rows_ref, cols_ref, count_ref, sens_ref, image_ref, out_ref, acc_ref):
    step = pl.program_id(0)
    parts, col_blocks, piece = out_ref.shape[:3]

    @pl.when(step == 0)
    def _():
        acc_ref[...] = jnp.zeros_like(acc_ref)

    @pl.when(step * STEP < count_ref[0])
    def _():
        for k in range(STEP):
            slot = step * STEP + k
            col = jnp.where(slot < count_ref[0], cols_ref[slot], col_blocks)
            acc_ref[col] += lax.dot_general(
                sens_ref[k], image_ref[rows_ref[slot]], (((0,), (0,)), ((), ())),
                preferred_element_type=jnp.float32,
            )

    @pl.when(step == pl.num_programs(0) - 1)
    def _():
        for r in range(parts):
            out_ref[r] = acc_ref[:col_blocks, r * piece : (r + 1) * piece].astype(out_ref.dtype)


def adjoint(rows, cols, count, sens, image, col_blocks, parts):
    slots = sens.shape[0]
    width = image.shape[2]
    piece = BLK // parts
    return pl.pallas_call(
        adjoint_body,
        out_shape=jax.ShapeDtypeStruct((parts, col_blocks, piece, width), jnp.bfloat16),
        grid_spec=pltpu.PrefetchScalarGridSpec(
            num_scalar_prefetch=3,
            grid=(slots // STEP,),
            in_specs=[
                pl.BlockSpec((STEP, BLK, BLK), live_step),
                pl.BlockSpec(image.shape, lambda i, *_: (0, 0, 0)),
            ],
            out_specs=pl.BlockSpec(
                (parts, col_blocks, piece, width), lambda i, *_: (0, 0, 0, 0)
            ),
            scratch_shapes=[pltpu.VMEM((col_blocks + 1, BLK, width), jnp.float32)],
        ),
        compiler_params=pltpu.CompilerParams(vmem_limit_bytes=24 * MIB),
        cost_estimate=pl.CostEstimate(
            flops=2 * slots * BLK * BLK * width, bytes_accessed=2 * slots * BLK * BLK,
            transcendentals=0,
        ),
        name="adjoint",
    )(rows, cols, count, sens, image)


def smooth_body(offset_ref, ext_ref, near_ref, weight_ref, out_ref):
    tiles = out_ref.shape[0] // BLK
    first = pl.program_id(0) * tiles
    span = lax.broadcasted_iota(jnp.int32, (2 * BLK, BLK), 0)
    center = lax.broadcasted_iota(jnp.int32, (2 * BLK, BLK), 1) + RIM
    for t in range(tiles):
        start = (first + t) * BLK
        cells = slice(t * BLK, (t + 1) * BLK)
        near = near_ref[:, cells] - (offset_ref[0] + start)
        face = weight_ref[:, cells]
        total = jnp.sum(face, axis=0, keepdims=True)
        mix = jnp.where(span == center, total, 0.0)
        for k in range(4):
            mix = mix - jnp.where(span == near[k : k + 1], face[k : k + 1], 0.0)
        window = ext_ref[pl.ds(pl.multiple_of(start, BLK), 2 * BLK), :]
        out_ref[cells, :] = lax.dot_general(
            mix, window, (((0,), (0,)), ((), ())),
            precision=lax.Precision.HIGHEST, preferred_element_type=jnp.float32,
        )


def smoothing(offset, extended, neighbors, face_weight):
    cells = neighbors.shape[1]
    width = extended.shape[1]
    per_step = 8 * BLK
    return pl.pallas_call(
        smooth_body,
        out_shape=jax.ShapeDtypeStruct((cells, width), jnp.float32),
        grid_spec=pltpu.PrefetchScalarGridSpec(
            num_scalar_prefetch=1,
            grid=(cells // per_step,),
            in_specs=[
                pl.BlockSpec(extended.shape, lambda i, *_: (0, 0)),
                pl.BlockSpec((4, per_step), lambda i, *_: (0, i)),
                pl.BlockSpec((4, per_step), lambda i, *_: (0, i)),
            ],
            out_specs=pl.BlockSpec((per_step, width), lambda i, *_: (i, 0)),
        ),
        compiler_params=pltpu.CompilerParams(vmem_limit_bytes=24 * MIB),
        cost_estimate=pl.CostEstimate(
            flops=24 * cells * BLK * width, bytes_accessed=16 * cells * width, transcendentals=0
        ),
        name="smoothing",
    )(offset, extended, neighbors, face_weight)


def finish_body(place_ref, basis_ref, wave_ref, smooth_ref, out_ref):
    per_step = out_ref.shape[0]
    first = pl.program_id(0) * per_step
    parts = wave_ref.shape[0]
    for b in range(per_step):
        at = place_ref[first + b]
        block = jnp.concatenate([wave_ref[r, at] for r in range(parts)], axis=0)
        both = jnp.concatenate([block, block], axis=0)
        out_ref[b] = smooth_ref[b] + jnp.dot(
            basis_ref[...], both, preferred_element_type=jnp.float32
        )


def finish(place, wave, smooth_blocks):
    blocks, _, width = smooth_blocks.shape
    per_step = 8
    basis = haar_matrix(BLK).T.astype(np.float32)
    high = basis.astype(jnp.bfloat16)
    low = (basis - high.astype(np.float32)).astype(jnp.bfloat16)
    basis2 = jnp.asarray(np.concatenate([high, low], axis=1))
    return pl.pallas_call(
        finish_body,
        out_shape=jax.ShapeDtypeStruct((blocks, BLK, width), jnp.float32),
        grid_spec=pltpu.PrefetchScalarGridSpec(
            num_scalar_prefetch=1,
            grid=(blocks // per_step,),
            in_specs=[
                pl.BlockSpec((BLK, 2 * BLK), lambda i, *_: (0, 0)),
                pl.BlockSpec(wave.shape, lambda i, *_: (0, 0, 0, 0)),
                pl.BlockSpec((per_step, BLK, width), lambda i, *_: (i, 0, 0)),
            ],
            out_specs=pl.BlockSpec((per_step, BLK, width), lambda i, *_: (i, 0, 0)),
        ),
        compiler_params=pltpu.CompilerParams(vmem_limit_bytes=24 * MIB),
        cost_estimate=pl.CostEstimate(
            flops=4 * blocks * BLK * BLK * width, bytes_accessed=10 * blocks * BLK * width,
            transcendentals=0,
        ),
        name="finish",
    )(place, basis2, wave, smooth_blocks)


def extend(block, axis, width):
    count = lax.axis_size(axis)
    forward_pairs = [(i, i + 1) for i in range(count - 1)]
    backward_pairs = [(target, source) for source, target in forward_pairs]
    low = lax.ppermute(block[block.shape[0] - width :], axis, forward_pairs)
    high = lax.ppermute(block[:width], axis, backward_pairs)
    return jnp.concatenate([low, block, high], axis=0)


def local(model_dir, sens_blocks, blk_row, blk_col, blk_count, send_order, neighbors, face_weight):
    cell_count, width = model_dir.shape
    blocks = cell_count // BLK
    col_devices = lax.axis_size("cols")
    row_devices = lax.axis_size("rows")
    per_peer = blocks // col_devices
    piece = BLK // row_devices
    model_blocks = model_dir.reshape(blocks, BLK, width)
    order = send_order[0]
    positions = lax.iota(jnp.int32, blocks)
    place = jnp.sum(
        jnp.where(order[None, :] == positions[:, None], positions[None, :], 0), axis=1
    )
    sens = sens_blocks[0]
    rows, cols, count = blk_row[0], blk_col[0], blk_count[0]

    outgoing = analyze(place, model_blocks)
    wave = lax.all_to_all(
        outgoing.reshape(col_devices, per_peer * BLK, width), "cols", 0, 0, tiled=True
    ).reshape(blocks, BLK, width)

    extended = extend(model_dir, "cols", RIM)
    offset = (lax.axis_index("cols") * cell_count - RIM).astype(jnp.int32).reshape(1)
    smooth = smoothing(offset, extended, neighbors, face_weight)

    partial_rows = forward(rows, cols, count, sens, wave)
    shares = lax.all_to_all(
        partial_rows.reshape(col_devices, -1, width), "cols", 0, 0, tiled=True
    )
    image_share = jnp.sum(shares.astype(jnp.float32), axis=0).astype(jnp.bfloat16)
    image_half = lax.all_gather(image_share, "cols", axis=0, tiled=True)
    data_image = image_half.astype(jnp.float32)

    partial_cols = adjoint(
        rows, cols, count, sens, image_half.reshape(RB_DEV, BLK, width), blocks, row_devices
    )
    pieces = lax.all_to_all(
        partial_cols.reshape(row_devices * col_devices, per_peer * piece, width),
        ("rows", "cols"), 0, 0, tiled=True,
    ).reshape(row_devices, blocks, piece, width)
    summed = jnp.sum(pieces.astype(jnp.float32), axis=0).astype(jnp.bfloat16)
    gathered = lax.all_gather(summed, "rows", axis=0, tiled=False)
    normal = finish(place, gathered, smooth.reshape(blocks, BLK, width))
    return (data_image, normal.reshape(cell_count, width))


def solution(mesh):
    placed = (
        P("cols", None),
        P("rows", "cols", None, None),
        P("rows", "cols"),
        P("rows", "cols"),
        P("rows", "cols"),
        P("cols", None),
        P(None, "cols"),
        P(None, "cols"),
    )
    return jax.shard_map(
        local,
        mesh=mesh,
        in_specs=placed,
        out_specs=(P("rows", None), P("cols", None)),
        check_vma=False,
    )
```

```python
import math

import jax
import jax.numpy as jnp
import numpy as np
from jax import lax
from jax.experimental import pallas as pl
from jax.experimental.pallas import tpu as pltpu
from jax.sharding import PartitionSpec as P

BLK = 128
RB_DEV = 32
RIM = 64
STEP = 16
CHUNKS = 4
MIB = 1 << 20
LARGE = 56 * MIB


def haar_matrix(order_n):
    matrix = np.ones((1, 1))
    while matrix.shape[0] < order_n:
        length = matrix.shape[0]
        upper = np.kron(matrix, np.array([[1.0, 1.0]]))
        lower = np.kron(np.eye(length), np.array([[1.0, -1.0]]))
        matrix = np.concatenate([upper, lower], axis=0) / math.sqrt(2.0)
    return matrix


def analyze_body(order_ref, sign_ref, scale_ref, model_ref, out_ref, block_ref, sems):
    per_step = out_ref.shape[0]
    step = pl.program_id(0)
    steps = model_ref.shape[0] // per_step

    def fetch(j):
        return pltpu.make_async_copy(
            model_ref.at[order_ref[0, j]], block_ref.at[j], sems.at[j // per_step]
        )

    @pl.when(step == 0)
    def _():
        for j in range(steps * per_step):
            fetch(j).start()

    for b in range(per_step):
        pltpu.make_async_copy(
            model_ref.at[0], block_ref.at[step * per_step + b], sems.at[step]
        ).wait()
    for b in range(per_step):
        x = block_ref[step * per_step + b]
        high = x.astype(jnp.bfloat16)
        low = (x - high.astype(jnp.float32)).astype(jnp.bfloat16)
        raw = jnp.dot(
            sign_ref[...], jnp.concatenate([high, low], axis=0),
            preferred_element_type=jnp.float32,
        )
        out_ref[b] = (raw * scale_ref[...]).astype(jnp.bfloat16)


def analyze(order, model_blocks):
    blocks = model_blocks.shape[0]
    width = model_blocks.shape[2]
    per_step = 8
    haar = haar_matrix(BLK)
    scale = np.abs(haar).max(axis=1)
    sign = np.sign(haar)
    signs = jnp.asarray(np.concatenate([sign, sign], axis=1), jnp.bfloat16)
    scales = jnp.asarray(np.broadcast_to(scale[:, None], (BLK, width)), jnp.float32)
    return pl.pallas_call(
        analyze_body,
        out_shape=jax.ShapeDtypeStruct((blocks, BLK, width), jnp.bfloat16),
        grid_spec=pltpu.PrefetchScalarGridSpec(
            num_scalar_prefetch=1,
            grid=(blocks // per_step,),
            in_specs=[
                pl.BlockSpec((BLK, 2 * BLK), lambda i, *_: (0, 0)),
                pl.BlockSpec((BLK, width), lambda i, *_: (0, 0)),
                pl.BlockSpec(memory_space=pl.ANY),
            ],
            out_specs=pl.BlockSpec((per_step, BLK, width), lambda i, *_: (i, 0, 0)),
            scratch_shapes=[
                pltpu.VMEM((blocks, BLK, width), jnp.float32),
                pltpu.SemaphoreType.DMA((blocks // per_step,)),
            ],
        ),
        compiler_params=pltpu.CompilerParams(vmem_limit_bytes=LARGE),
        cost_estimate=pl.CostEstimate(
            flops=4 * blocks * BLK * BLK * width, bytes_accessed=6 * blocks * BLK * width,
            transcendentals=0,
        ),
        name="analyze",
    )(order, signs, scales, model_blocks)


def forward_body(rows_ref, cols_ref, count_ref, sens_ref, wave_ref, out_ref, acc_ref):
    step = pl.program_id(0)
    row_blocks = out_ref.shape[0]

    @pl.when(step == 0)
    def _():
        acc_ref[...] = jnp.zeros_like(acc_ref)

    @pl.when(step * STEP < count_ref[0])
    def _():
        for k in range(STEP):
            slot = step * STEP + k
            row = jnp.where(slot < count_ref[0], rows_ref[slot], row_blocks)
            acc_ref[row] += jnp.dot(
                sens_ref[k], wave_ref[cols_ref[slot]], preferred_element_type=jnp.float32
            )

    @pl.when(step == pl.num_programs(0) - 1)
    def _():
        out_ref[...] = acc_ref[:row_blocks].astype(out_ref.dtype)


def live_step(i, rows_ref, cols_ref, count_ref):
    return (jnp.minimum(i, (count_ref[0] - 1) // STEP), 0, 0)


def forward(rows, cols, count, sens, wave):
    slots = sens.shape[0]
    width = wave.shape[2]
    return pl.pallas_call(
        forward_body,
        out_shape=jax.ShapeDtypeStruct((RB_DEV, BLK, width), jnp.bfloat16),
        grid_spec=pltpu.PrefetchScalarGridSpec(
            num_scalar_prefetch=3,
            grid=(slots // STEP,),
            in_specs=[
                pl.BlockSpec((STEP, BLK, BLK), live_step),
                pl.BlockSpec(wave.shape, lambda i, *_: (0, 0, 0)),
            ],
            out_specs=pl.BlockSpec((RB_DEV, BLK, width), lambda i, *_: (0, 0, 0)),
            scratch_shapes=[pltpu.VMEM((RB_DEV + 1, BLK, width), jnp.float32)],
        ),
        compiler_params=pltpu.CompilerParams(vmem_limit_bytes=LARGE),
        cost_estimate=pl.CostEstimate(
            flops=2 * slots * BLK * BLK * width, bytes_accessed=2 * slots * BLK * BLK,
            transcendentals=0,
        ),
        name="forward",
    )(rows, cols, count, sens, wave)


def adjoint_body(rows_ref, cols_ref, count_ref, sens_ref, image_ref, *refs):
    step = pl.program_id(0)
    out_refs, acc_ref = refs[:-1], refs[-1]
    col_blocks, piece = out_refs[0].shape[:2]

    @pl.when(step == 0)
    def _():
        acc_ref[...] = jnp.zeros_like(acc_ref)

    @pl.when(step * STEP < count_ref[0])
    def _():
        for k in range(STEP):
            slot = step * STEP + k
            col = jnp.where(slot < count_ref[0], cols_ref[slot], col_blocks)
            acc_ref[col] += lax.dot_general(
                sens_ref[k], image_ref[rows_ref[slot]], (((0,), (0,)), ((), ())),
                preferred_element_type=jnp.float32,
            )

    @pl.when(step == pl.num_programs(0) - 1)
    def _():
        for c, out_ref in enumerate(out_refs):
            out_ref[...] = acc_ref[:col_blocks, c * piece : (c + 1) * piece].astype(jnp.bfloat16)


def adjoint(rows, cols, count, sens, image, col_blocks):
    slots = sens.shape[0]
    width = image.shape[2]
    chunk = (col_blocks, BLK // CHUNKS, width)
    return pl.pallas_call(
        adjoint_body,
        out_shape=[jax.ShapeDtypeStruct(chunk, jnp.bfloat16)] * CHUNKS,
        grid_spec=pltpu.PrefetchScalarGridSpec(
            num_scalar_prefetch=3,
            grid=(slots // STEP,),
            in_specs=[
                pl.BlockSpec((STEP, BLK, BLK), live_step),
                pl.BlockSpec(image.shape, lambda i, *_: (0, 0, 0)),
            ],
            out_specs=[pl.BlockSpec(chunk, lambda i, *_: (0, 0, 0))] * CHUNKS,
            scratch_shapes=[pltpu.VMEM((col_blocks + 1, BLK, width), jnp.float32)],
        ),
        compiler_params=pltpu.CompilerParams(vmem_limit_bytes=LARGE),
        cost_estimate=pl.CostEstimate(
            flops=2 * slots * BLK * BLK * width, bytes_accessed=2 * slots * BLK * BLK,
            transcendentals=0,
        ),
        name="adjoint",
    )(rows, cols, count, sens, image)


def smooth_body(offset_ref, ext_ref, near_ref, weight_ref, out_ref):
    tiles = out_ref.shape[0] // BLK
    first = pl.program_id(0) * tiles
    span = lax.broadcasted_iota(jnp.int32, (2 * BLK, BLK), 0)
    center = lax.broadcasted_iota(jnp.int32, (2 * BLK, BLK), 1) + RIM
    for t in range(tiles):
        start = (first + t) * BLK
        cells = slice(t * BLK, (t + 1) * BLK)
        near = near_ref[:, cells] - (offset_ref[0] + start)
        face = weight_ref[:, cells]
        total = jnp.sum(face, axis=0, keepdims=True)
        mix = jnp.where(span == center, total, 0.0)
        for k in range(4):
            mix = mix - jnp.where(span == near[k : k + 1], face[k : k + 1], 0.0)
        window = ext_ref[pl.ds(pl.multiple_of(start, BLK), 2 * BLK), :]
        out_ref[cells, :] = lax.dot_general(
            mix, window, (((0,), (0,)), ((), ())),
            precision=lax.Precision.HIGHEST, preferred_element_type=jnp.float32,
        )


def smoothing(offset, extended, neighbors, face_weight):
    cells = neighbors.shape[1]
    width = extended.shape[1]
    per_step = 8 * BLK
    return pl.pallas_call(
        smooth_body,
        out_shape=jax.ShapeDtypeStruct((cells, width), jnp.float32),
        grid_spec=pltpu.PrefetchScalarGridSpec(
            num_scalar_prefetch=1,
            grid=(cells // per_step,),
            in_specs=[
                pl.BlockSpec(extended.shape, lambda i, *_: (0, 0)),
                pl.BlockSpec((4, per_step), lambda i, *_: (0, i)),
                pl.BlockSpec((4, per_step), lambda i, *_: (0, i)),
            ],
            out_specs=pl.BlockSpec((per_step, width), lambda i, *_: (i, 0)),
        ),
        compiler_params=pltpu.CompilerParams(vmem_limit_bytes=24 * MIB),
        cost_estimate=pl.CostEstimate(
            flops=24 * cells * BLK * width, bytes_accessed=16 * cells * width, transcendentals=0
        ),
        name="smoothing",
    )(offset, extended, neighbors, face_weight)


def finish_body(place_ref, basis_ref, *refs):
    wave_refs, smooth_ref, out_ref = refs[:-2], refs[-2], refs[-1]
    per_step = out_ref.shape[0]
    first = pl.program_id(0) * per_step
    for b in range(per_step):
        at = place_ref[first + b]
        pieces = [ref[at] for ref in wave_refs]
        both = jnp.concatenate(pieces + pieces, axis=0)
        out_ref[b] = smooth_ref[b] + jnp.dot(
            basis_ref[...], both, preferred_element_type=jnp.float32
        )


def finish(place, waves, smooth_blocks):
    blocks, _, width = smooth_blocks.shape
    per_step = 8
    basis = haar_matrix(BLK).T.astype(np.float32)
    high = basis.astype(jnp.bfloat16)
    low = (basis - high.astype(np.float32)).astype(jnp.bfloat16)
    basis2 = jnp.asarray(np.concatenate([high, low], axis=1))
    return pl.pallas_call(
        finish_body,
        out_shape=jax.ShapeDtypeStruct((blocks, BLK, width), jnp.float32),
        grid_spec=pltpu.PrefetchScalarGridSpec(
            num_scalar_prefetch=1,
            grid=(blocks // per_step,),
            in_specs=[
                pl.BlockSpec((BLK, 2 * BLK), lambda i, *_: (0, 0)),
                *[pl.BlockSpec(w.shape, lambda i, *_: (0, 0, 0)) for w in waves],
                pl.BlockSpec((per_step, BLK, width), lambda i, *_: (i, 0, 0)),
            ],
            out_specs=pl.BlockSpec((per_step, BLK, width), lambda i, *_: (i, 0, 0)),
        ),
        compiler_params=pltpu.CompilerParams(vmem_limit_bytes=LARGE),
        cost_estimate=pl.CostEstimate(
            flops=4 * blocks * BLK * BLK * width, bytes_accessed=10 * blocks * BLK * width,
            transcendentals=0,
        ),
        name="finish",
    )(place, basis2, *waves, smooth_blocks)


def merge_body(take_ref, got_ref, mine_ref, after_ref, out_ref, *, final):
    got, mine = got_ref[...], mine_ref[...]
    if final:
        out_ref[...] = jnp.where(take_ref[0] > 0, got, mine)
    else:
        out_ref[...] = (got.astype(jnp.float32) + mine.astype(jnp.float32)).astype(mine.dtype)


def merge(take, got, mine, after, final):
    return pl.pallas_call(
        lambda *refs: merge_body(*refs, final=final),
        out_shape=jax.ShapeDtypeStruct(mine.shape, mine.dtype),
        in_specs=[
            pl.BlockSpec(memory_space=pltpu.SMEM),
            pl.BlockSpec(memory_space=pltpu.VMEM),
            pl.BlockSpec(memory_space=pltpu.VMEM),
            pl.BlockSpec(memory_space=pl.ANY),
        ],
        out_specs=pl.BlockSpec(memory_space=pltpu.VMEM),
        compiler_params=pltpu.CompilerParams(vmem_limit_bytes=8 * MIB),
        cost_estimate=pl.CostEstimate(
            flops=mine.size, bytes_accessed=6 * mine.size, transcendentals=0
        ),
        name="merge",
    )(take, got, mine, after)


def line_sums(parts, axis, deliver):
    count = lax.axis_size(axis)
    half = count // 2
    me = lax.axis_index(axis)
    stages = []
    for hop in range(half - 1):
        stages.append(([(hop, hop + 1), (count - 1 - hop, count - 2 - hop)], False))
    stages.append(([(half - 1, half), (half, half - 1)], False))
    for hop in range(half - 1):
        left, right = half - 1 - hop, half + hop
        stages.append(([(left, left - 1), (right, right + 1)], True))
    state = list(parts)
    got = [lax.ppermute(part, axis, stages[0][0]) for part in parts]
    done = [None] * len(parts)
    after = parts[0]
    for time in range(len(parts) + len(stages) - 1):
        for s, (pairs, final) in enumerate(stages):
            k = time - s
            if not 0 <= k < len(parts):
                continue
            take = (me == pairs[0][1]) | (me == pairs[1][1])
            take = take.astype(jnp.int32).reshape(1)
            state[k] = after = merge(take, got[k], state[k], after, final)
            if s + 1 < len(stages):
                got[k] = lax.ppermute(state[k], axis, stages[s + 1][0])
            else:
                done[k] = deliver(state[k])
    return done


def extend(block, axis, width):
    count = lax.axis_size(axis)
    forward_pairs = [(i, i + 1) for i in range(count - 1)]
    backward_pairs = [(target, source) for source, target in forward_pairs]
    low = lax.ppermute(block[block.shape[0] - width :], axis, forward_pairs)
    high = lax.ppermute(block[:width], axis, backward_pairs)
    return jnp.concatenate([low, block, high], axis=0)


def local(model_dir, sens_blocks, blk_row, blk_col, blk_count, send_order, neighbors, face_weight):
    cell_count, width = model_dir.shape
    blocks = cell_count // BLK
    col_devices = lax.axis_size("cols")
    row_devices = lax.axis_size("rows")
    per_peer = blocks // col_devices
    piece = BLK // row_devices
    model_blocks = model_dir.reshape(blocks, BLK, width)
    order = send_order[0]
    positions = lax.iota(jnp.int32, blocks)
    place = jnp.sum(
        jnp.where(order[None, :] == positions[:, None], positions[None, :], 0), axis=1
    )
    sens = sens_blocks[0]
    rows, cols, count = blk_row[0], blk_col[0], blk_count[0]

    outgoing = analyze(send_order, model_blocks)
    wave = lax.all_to_all(
        outgoing.reshape(col_devices, per_peer * BLK, width), "cols", 0, 0, tiled=True
    ).reshape(blocks, BLK, width)

    model_late, _ = lax.optimization_barrier((model_dir, outgoing))
    extended = extend(model_late, "cols", RIM)
    offset = (lax.axis_index("cols") * cell_count - RIM).astype(jnp.int32).reshape(1)
    smooth = smoothing(offset, extended, neighbors, face_weight)
    wave, smooth = lax.optimization_barrier((wave, smooth))

    partial_rows = forward(rows, cols, count, sens, wave)
    shares = lax.all_to_all(
        partial_rows.reshape(col_devices, -1, width), "cols", 0, 0, tiled=True
    )
    image_share = jnp.sum(shares.astype(jnp.float32), axis=0).astype(jnp.bfloat16)
    image_half = lax.all_to_all(
        jnp.broadcast_to(image_share, shares.shape), "cols", 0, 0, tiled=True
    ).reshape(-1, width)
    data_image = image_half.astype(jnp.float32)

    partial_cols = adjoint(
        rows, cols, count, sens, image_half.reshape(RB_DEV, BLK, width), blocks
    )
    rows_each = BLK // CHUNKS

    def to_cells(chunk):
        back = lax.all_to_all(
            chunk.reshape(col_devices, per_peer * rows_each, width), "cols", 0, 0, tiled=True
        )
        return back.reshape(blocks, rows_each, width)

    returned = line_sums(partial_cols, "rows", to_cells)
    normal = finish(place, returned, smooth.reshape(blocks, BLK, width))
    return (data_image, normal.reshape(cell_count, width))


def solution(mesh):
    placed = (
        P("cols", None),
        P("rows", "cols", None, None),
        P("rows", "cols"),
        P("rows", "cols"),
        P("rows", "cols"),
        P("cols", None),
        P(None, "cols"),
        P(None, "cols"),
    )
    return jax.shard_map(
        local,
        mesh=mesh,
        in_specs=placed,
        out_specs=(P("rows", None), P("cols", None)),
        check_vma=False,
    )
```

```python
import math

import jax
import jax.numpy as jnp
import numpy as np
from jax import lax
from jax.experimental import pallas as pl
from jax.experimental.pallas import tpu as pltpu
from jax.sharding import PartitionSpec as P

BLK = 128
RB_DEV = 32
RIM = 64
STEP = 16
CHUNKS = 2
MIB = 1 << 20
SMALL = 24 * MIB
ANY_SPEC = pl.BlockSpec(memory_space=pl.ANY)
VMEM_SPEC = pl.BlockSpec(memory_space=pltpu.VMEM)
HBM_SPEC = pl.BlockSpec(memory_space=pltpu.HBM)
SMEM_SPEC = pl.BlockSpec(memory_space=pltpu.SMEM)


def haar_matrix(order_n):
    matrix = np.ones((1, 1))
    while matrix.shape[0] < order_n:
        length = matrix.shape[0]
        upper = np.kron(matrix, np.array([[1.0, 1.0]]))
        lower = np.kron(np.eye(length), np.array([[1.0, -1.0]]))
        matrix = np.concatenate([upper, lower], axis=0) / math.sqrt(2.0)
    return matrix


def analyze_body(order_ref, sign_ref, scale_ref, model_ref, out_ref, block_ref, sems):
    blocks = model_ref.shape[0]
    copies = [
        pltpu.make_async_copy(model_ref.at[order_ref[0, j]], block_ref.at[j], sems.at[j])
        for j in range(blocks)
    ]
    for copy in copies:
        copy.start()
    for j, copy in enumerate(copies):
        copy.wait()
        x = block_ref[j]
        high = x.astype(jnp.bfloat16)
        low = (x - high.astype(jnp.float32)).astype(jnp.bfloat16)
        raw = jnp.dot(
            sign_ref[...], jnp.concatenate([high, low], axis=0),
            preferred_element_type=jnp.float32,
        )
        out_ref[j] = (raw * scale_ref[...]).astype(jnp.bfloat16)


def analyze(order, model_blocks):
    blocks = model_blocks.shape[0]
    width = model_blocks.shape[2]
    haar = haar_matrix(BLK)
    scale = np.abs(haar).max(axis=1)
    sign = np.sign(haar)
    signs = jnp.asarray(np.concatenate([sign, sign], axis=1), jnp.bfloat16)
    scales = jnp.asarray(np.broadcast_to(scale[:, None], (BLK, width)), jnp.float32)
    return pl.pallas_call(
        analyze_body,
        out_shape=jax.ShapeDtypeStruct((blocks, BLK, width), jnp.bfloat16),
        in_specs=[SMEM_SPEC, VMEM_SPEC, VMEM_SPEC, ANY_SPEC],
        out_specs=VMEM_SPEC,
        scratch_shapes=[
            pltpu.VMEM((blocks, BLK, width), jnp.float32),
            pltpu.SemaphoreType.DMA((blocks,)),
        ],
        compiler_params=pltpu.CompilerParams(vmem_limit_bytes=56 * MIB),
        cost_estimate=pl.CostEstimate(
            flops=4 * blocks * BLK * BLK * width, bytes_accessed=6 * blocks * BLK * width,
            transcendentals=0,
        ),
        name="analyze",
    )(order, signs, scales, model_blocks)


def load_body(sens_ref, after_ref, out_ref, sems):
    pieces = sems.shape[0]
    each = sens_ref.shape[0] // pieces
    copies = [
        pltpu.make_async_copy(
            sens_ref.at[pl.ds(i * each, each)], out_ref.at[pl.ds(i * each, each)], sems.at[i]
        )
        for i in range(pieces)
    ]
    for copy in copies:
        copy.start()
    for copy in copies:
        copy.wait()


def load(sens, after):
    return pl.pallas_call(
        load_body,
        out_shape=pltpu.VMEM(sens.shape, sens.dtype),
        in_specs=[HBM_SPEC, HBM_SPEC],
        out_specs=VMEM_SPEC,
        scratch_shapes=[pltpu.SemaphoreType.DMA((16,))],
        compiler_params=pltpu.CompilerParams(vmem_limit_bytes=SMALL),
        cost_estimate=pl.CostEstimate(
            flops=0, bytes_accessed=4 * sens.size, transcendentals=0
        ),
        name="load",
    )(sens, after)


def forward_body(rows_ref, cols_ref, count_ref, sens_ref, wave_ref, out_ref, acc_ref):
    row_blocks = out_ref.shape[0]
    last = rows_ref.shape[0] - 1
    count = count_ref[0]
    acc_ref[...] = jnp.zeros_like(acc_ref)

    @pl.loop(0, (count + STEP - 1) // STEP)
    def _(step):
        for k in range(STEP):
            place = step * STEP + k
            slot = jnp.minimum(place, last)
            row = jnp.where(place < count, rows_ref[slot], row_blocks)
            acc_ref[row] += jnp.dot(
                sens_ref[slot], wave_ref[cols_ref[slot]], preferred_element_type=jnp.float32
            )

    out_ref[...] = acc_ref[:row_blocks].astype(out_ref.dtype)


def forward(rows, cols, count, sens, wave):
    slots = sens.shape[0]
    width = wave.shape[2]
    return pl.pallas_call(
        forward_body,
        out_shape=jax.ShapeDtypeStruct((RB_DEV, BLK, width), jnp.bfloat16),
        in_specs=[SMEM_SPEC, SMEM_SPEC, SMEM_SPEC, VMEM_SPEC, VMEM_SPEC],
        out_specs=VMEM_SPEC,
        scratch_shapes=[pltpu.VMEM((RB_DEV + 1, BLK, width), jnp.float32)],
        compiler_params=pltpu.CompilerParams(vmem_limit_bytes=SMALL),
        cost_estimate=pl.CostEstimate(
            flops=2 * slots * BLK * BLK * width, bytes_accessed=2 * slots * BLK * BLK,
            transcendentals=0,
        ),
        name="forward",
    )(rows, cols, count, sens, wave)


def adjoint_body(list_ref, bounds_ref, sens_ref, image_ref, out_ref, acc_ref, *, chunk, blocks):
    parts, cols, piece = out_ref.shape[:3]
    first, end = bounds_ref[chunk], bounds_ref[chunk + 1]
    last = list_ref.shape[0] - 1
    acc_ref[...] = jnp.zeros_like(acc_ref)

    @pl.loop(0, (end - first + STEP - 1) // STEP)
    def _(step):
        for k in range(STEP):
            place = first + step * STEP + k
            entry = list_ref[jnp.minimum(place, last)]
            col = jnp.where(place < end, entry % blocks, cols)
            row = (entry // blocks) % RB_DEV
            slot = entry // (blocks * RB_DEV)
            acc_ref[col] += lax.dot_general(
                sens_ref[slot], image_ref[row], (((0,), (0,)), ((), ())),
                preferred_element_type=jnp.float32,
            )

    for r in range(parts):
        out_ref[r] = acc_ref[:cols, r * piece : (r + 1) * piece].astype(out_ref.dtype)


def adjoint(listed, bounds, sens, image, chunk, chunks, blocks, parts):
    slots = sens.shape[0]
    width = image.shape[2]
    cols = blocks // chunks
    return pl.pallas_call(
        lambda *refs: adjoint_body(*refs, chunk=chunk, blocks=blocks),
        out_shape=jax.ShapeDtypeStruct((parts, cols, BLK // parts, width), jnp.bfloat16),
        in_specs=[SMEM_SPEC, SMEM_SPEC, VMEM_SPEC, VMEM_SPEC],
        out_specs=VMEM_SPEC,
        scratch_shapes=[pltpu.VMEM((cols + 1, BLK, width), jnp.float32)],
        compiler_params=pltpu.CompilerParams(vmem_limit_bytes=SMALL),
        cost_estimate=pl.CostEstimate(
            flops=2 * slots * BLK * BLK * width // chunks,
            bytes_accessed=2 * slots * BLK * BLK // chunks, transcendentals=0,
        ),
        name="adjoint",
    )(listed, bounds, sens, image)


def slot_list(rows, cols, count, blocks, per_peer, chunks):
    slots = rows.shape[0]
    each = per_peer // chunks
    slot = lax.iota(jnp.int32, slots)
    peer, q = cols // per_peer, cols % per_peer
    chunk = jnp.where(slot < count, q // each, chunks)
    entry = (slot * RB_DEV + rows) * blocks + peer * each + q % each
    key = chunk * slots + slot
    rank = jnp.sum((key[None, :] < key[:, None]).astype(jnp.int32), axis=1)
    listed = jnp.sum(jnp.where(rank[None, :] == slot[:, None], entry[None, :], 0), axis=1)
    starts = lax.iota(jnp.int32, chunks + 1)
    bounds = jnp.sum((chunk[None, :] < starts[:, None]).astype(jnp.int32), axis=1)
    return listed, bounds


def smooth_body(offset_ref, ext_ref, near_ref, weight_ref, out_ref):
    tiles = out_ref.shape[0] // BLK
    first = pl.program_id(0) * tiles
    span = lax.broadcasted_iota(jnp.int32, (2 * BLK, BLK), 0)
    center = lax.broadcasted_iota(jnp.int32, (2 * BLK, BLK), 1) + RIM
    for t in range(tiles):
        start = (first + t) * BLK
        cells = slice(t * BLK, (t + 1) * BLK)
        near = near_ref[:, cells] - (offset_ref[0] + start)
        face = weight_ref[:, cells]
        total = jnp.sum(face, axis=0, keepdims=True)
        mix = jnp.where(span == center, total, 0.0)
        for k in range(4):
            mix = mix - jnp.where(span == near[k : k + 1], face[k : k + 1], 0.0)
        window = ext_ref[pl.ds(pl.multiple_of(start, BLK), 2 * BLK), :]
        out_ref[cells, :] = lax.dot_general(
            mix, window, (((0,), (0,)), ((), ())),
            precision=lax.Precision.HIGHEST, preferred_element_type=jnp.float32,
        )


def smoothing(offset, extended, neighbors, face_weight):
    cells = neighbors.shape[1]
    width = extended.shape[1]
    per_step = 8 * BLK
    return pl.pallas_call(
        smooth_body,
        out_shape=jax.ShapeDtypeStruct((cells, width), jnp.float32),
        grid_spec=pltpu.PrefetchScalarGridSpec(
            num_scalar_prefetch=1,
            grid=(cells // per_step,),
            in_specs=[
                pl.BlockSpec(extended.shape, lambda i, *_: (0, 0)),
                pl.BlockSpec((4, per_step), lambda i, *_: (0, i)),
                pl.BlockSpec((4, per_step), lambda i, *_: (0, i)),
            ],
            out_specs=pl.BlockSpec((per_step, width), lambda i, *_: (i, 0)),
        ),
        compiler_params=pltpu.CompilerParams(vmem_limit_bytes=24 * MIB),
        cost_estimate=pl.CostEstimate(
            flops=24 * cells * BLK * width, bytes_accessed=16 * cells * width, transcendentals=0
        ),
        name="smoothing",
    )(offset, extended, neighbors, face_weight)


def finish_body(cells_ref, basis_ref, wave_ref, base_ref, out_ref, block_ref, got, put, *, chunk):
    parts, cols = wave_ref.shape[:2]
    fetches, stores = [], []
    for i in range(cols):
        cell = cells_ref[chunk * cols + i]
        fetches.append(pltpu.make_async_copy(base_ref.at[cell], block_ref.at[i], got.at[i]))
        stores.append(pltpu.make_async_copy(block_ref.at[i], out_ref.at[cell], put.at[i]))
    for fetch in fetches:
        fetch.start()
    for i in range(cols):
        pieces = [wave_ref[r, i] for r in range(parts)]
        both = jnp.concatenate(pieces + pieces, axis=0)
        value = jnp.dot(basis_ref[...], both, preferred_element_type=jnp.float32)
        fetches[i].wait()
        block_ref[i] += value
        stores[i].start()
    for store in stores:
        store.wait()


def finish(cells, wave, base, chunk):
    width = base.shape[2]
    cols = wave.shape[1]
    basis = haar_matrix(BLK).T.astype(np.float32)
    high = basis.astype(jnp.bfloat16)
    low = (basis - high.astype(np.float32)).astype(jnp.bfloat16)
    basis2 = jnp.asarray(np.concatenate([high, low], axis=1))
    return pl.pallas_call(
        lambda *refs: finish_body(*refs, chunk=chunk),
        out_shape=jax.ShapeDtypeStruct(base.shape, base.dtype),
        in_specs=[SMEM_SPEC, VMEM_SPEC, VMEM_SPEC, HBM_SPEC],
        out_specs=HBM_SPEC,
        input_output_aliases={3: 0},
        scratch_shapes=[
            pltpu.VMEM((cols, BLK, width), jnp.float32),
            pltpu.SemaphoreType.DMA((cols,)),
            pltpu.SemaphoreType.DMA((cols,)),
        ],
        compiler_params=pltpu.CompilerParams(vmem_limit_bytes=SMALL),
        cost_estimate=pl.CostEstimate(
            flops=4 * cols * BLK * BLK * width, bytes_accessed=10 * cols * BLK * width,
            transcendentals=0,
        ),
        name="finish",
    )(cells, basis2, wave, base)


def extend(block, axis, width):
    count = lax.axis_size(axis)
    forward_pairs = [(i, i + 1) for i in range(count - 1)]
    backward_pairs = [(target, source) for source, target in forward_pairs]
    low = lax.ppermute(block[block.shape[0] - width :], axis, forward_pairs)
    high = lax.ppermute(block[:width], axis, backward_pairs)
    return jnp.concatenate([low, block, high], axis=0)


def local(model_dir, sens_blocks, blk_row, blk_col, blk_count, send_order, neighbors, face_weight):
    cell_count, width = model_dir.shape
    blocks = cell_count // BLK
    col_devices = lax.axis_size("cols")
    row_devices = lax.axis_size("rows")
    per_peer = blocks // col_devices
    piece = BLK // row_devices
    model_blocks = model_dir.reshape(blocks, BLK, width)
    sens = sens_blocks[0]
    chunks = math.gcd(CHUNKS, per_peer)
    each = per_peer // chunks

    outgoing = analyze(send_order, model_blocks)
    wave = lax.all_to_all(
        outgoing.reshape(col_devices, per_peer * BLK, width), "cols", 0, 0, tiled=True
    ).reshape(blocks, BLK, width)
    held = load(sens, outgoing)
    blk_row, blk_col, blk_count, _ = lax.optimization_barrier(
        (blk_row, blk_col, blk_count, outgoing)
    )
    rows, cols, count = blk_row[0], blk_col[0], blk_count[0]
    listed, bounds = slot_list(rows, cols, count[0], blocks, per_peer, chunks)
    cells = send_order.reshape(col_devices, chunks, each).transpose(1, 0, 2).reshape(blocks)

    partial_rows = forward(rows, cols, count, held, wave)
    shares = lax.all_to_all(
        partial_rows.reshape(col_devices, -1, width), "cols", 0, 0, tiled=True
    )
    image_share = jnp.sum(shares.astype(jnp.float32), axis=0).astype(jnp.bfloat16)
    image_half = lax.all_to_all(
        jnp.broadcast_to(image_share, shares.shape), "cols", 0, 0, tiled=True
    ).reshape(-1, width)
    data_image = image_half.astype(jnp.float32)

    image_blocks = image_half.reshape(RB_DEV, BLK, width)
    gathered = []
    for chunk in range(chunks):
        part = adjoint(listed, bounds, held, image_blocks, chunk, chunks, blocks, row_devices)
        got = lax.all_to_all(
            part.reshape(row_devices * col_devices, each * piece, width),
            ("rows", "cols"), 0, 0, tiled=True,
        ).reshape(row_devices, col_devices * each, piece, width)
        total = jnp.sum(got.astype(jnp.float32), axis=0).astype(jnp.bfloat16)
        gathered.append(lax.all_gather(total, "rows", axis=0, tiled=False))
        if chunk == 0:
            model_late, _ = lax.optimization_barrier((model_dir, total))

    extended = extend(model_late, "cols", RIM)
    offset = (lax.axis_index("cols") * cell_count - RIM).astype(jnp.int32).reshape(1)
    normal = smoothing(offset, extended, neighbors, face_weight).reshape(blocks, BLK, width)
    for chunk, wave_back in enumerate(gathered):
        normal = finish(cells, wave_back, normal, chunk)
    return (data_image, normal.reshape(cell_count, width))


def solution(mesh):
    placed = (
        P("cols", None),
        P("rows", "cols", None, None),
        P("rows", "cols"),
        P("rows", "cols"),
        P("rows", "cols"),
        P("cols", None),
        P(None, "cols"),
        P(None, "cols"),
    )
    return jax.shard_map(
        local,
        mesh=mesh,
        in_specs=placed,
        out_specs=(P("rows", None), P("cols", None)),
        check_vma=False,
    )
```

```python
import math

import jax
import jax.numpy as jnp
import numpy as np
from jax import lax
from jax.experimental import pallas as pl
from jax.experimental.pallas import tpu as pltpu
from jax.sharding import PartitionSpec as P

BLK = 128
RB_DEV = 32
RIM = 64
STEP = 16
CHUNKS = 4
MIB = 1 << 20
SMALL = 16 * MIB
LARGE = 56 * MIB
ANY_SPEC = pl.BlockSpec(memory_space=pl.ANY)
VMEM_SPEC = pl.BlockSpec(memory_space=pltpu.VMEM)
SMEM_SPEC = pl.BlockSpec(memory_space=pltpu.SMEM)


def haar_matrix(order_n):
    matrix = np.ones((1, 1))
    while matrix.shape[0] < order_n:
        length = matrix.shape[0]
        upper = np.kron(matrix, np.array([[1.0, 1.0]]))
        lower = np.kron(np.eye(length), np.array([[1.0, -1.0]]))
        matrix = np.concatenate([upper, lower], axis=0) / math.sqrt(2.0)
    return matrix


def fetch(source, target, sems, pieces):
    each = source.shape[0] // pieces
    parts = [pl.ds(i * each, each) for i in range(pieces)]
    return [
        pltpu.make_async_copy(source.at[part], target.at[part], sems.at[i])
        for i, part in enumerate(parts)
    ]


def start_all(copies):
    for copy in copies:
        copy.start()


def wait_all(copies):
    for copy in copies:
        copy.wait()


def analyze_body(order_ref, model_ref, out_ref, block_ref, coeff_ref, got, put):
    blocks, _, width = model_ref.shape
    steps = put.shape[0]
    each = blocks // steps
    loads = fetch(model_ref, block_ref, got, got.shape[0])
    start_all(loads)
    row = lax.broadcasted_iota(jnp.int32, (BLK, BLK), 0)
    col = lax.broadcasted_iota(jnp.int32, (BLK, BLK), 1)
    level = jnp.ones_like(row)
    scale = jnp.full((BLK, width), BLK**-0.5, jnp.float32)
    wide_row = lax.broadcasted_iota(jnp.int32, (BLK, width), 0)
    size = 2
    while size < BLK:
        level = jnp.where(row >= size, size, level)
        scale = jnp.where(wide_row >= size, (size / BLK) ** 0.5, scale)
        size *= 2
    span = BLK // level
    inside = col - (row - level) * span
    sign = jnp.where(inside * 2 < span, 1.0, -1.0)
    sign = jnp.where((inside >= 0) & (inside < span), sign, 0.0)
    sign = jnp.where(row == 0, 1.0, sign).astype(jnp.bfloat16)
    both_signs = jnp.concatenate([sign, sign], axis=1)
    stores = fetch(coeff_ref, out_ref, put, steps)
    wait_all(loads)
    for step in range(steps):
        for j in range(step * each, (step + 1) * each):
            x = block_ref[order_ref[0, j]]
            high = x.astype(jnp.bfloat16)
            low = (x - high.astype(jnp.float32)).astype(jnp.bfloat16)
            raw = jnp.dot(
                both_signs, jnp.concatenate([high, low], axis=0),
                preferred_element_type=jnp.float32,
            )
            coeff_ref[j] = (raw * scale).astype(jnp.bfloat16)
        stores[step].start()
    wait_all(stores)


def analyze(order, model_blocks):
    blocks, _, width = model_blocks.shape
    return pl.pallas_call(
        analyze_body,
        out_shape=jax.ShapeDtypeStruct((blocks, BLK, width), jnp.bfloat16),
        in_specs=[SMEM_SPEC, ANY_SPEC],
        out_specs=ANY_SPEC,
        scratch_shapes=[
            pltpu.VMEM((blocks, BLK, width), jnp.float32),
            pltpu.VMEM((blocks, BLK, width), jnp.bfloat16),
            pltpu.SemaphoreType.DMA((16,)),
            pltpu.SemaphoreType.DMA((4,)),
        ],
        compiler_params=pltpu.CompilerParams(vmem_limit_bytes=LARGE),
        cost_estimate=pl.CostEstimate(
            flops=4 * blocks * BLK * BLK * width, bytes_accessed=6 * blocks * BLK * width,
            transcendentals=0,
        ),
        name="analyze",
    )(order, model_blocks)


def slot_loop(count, sens_ref, block_ref, sems, others, work):
    steps = sems.shape[0]
    each = sens_ref.shape[0] // steps

    def block_copy(step):
        part = pl.ds(step * each, each)
        return pltpu.make_async_copy(sens_ref.at[part], block_ref.at[part], sems.at[step])

    start_all(others)
    needed = (count + each - 1) // each

    @pl.loop(0, needed)
    def _(step):
        block_copy(step).start()

    wait_all(others)

    @pl.loop(0, needed)
    def _(step):
        block_copy(step).wait()
        for k in range(each):
            slot = step * each + k
            work(slot, block_ref[slot], slot < count)


def forward_body(rows_ref, cols_ref, count_ref, sens_ref, wave_ref, out_ref,
                 block_ref, held_ref, acc_ref, half_ref, sems, got, put):
    row_blocks = out_ref.shape[0]
    acc_ref[...] = jnp.zeros_like(acc_ref)

    def work(slot, block, live):
        row = jnp.where(live, rows_ref[0, slot], row_blocks)
        acc_ref[row] += jnp.dot(
            block, held_ref[cols_ref[0, slot]], preferred_element_type=jnp.float32
        )

    waves = fetch(wave_ref, held_ref, got, got.shape[0])
    slot_loop(count_ref[0, 0], sens_ref, block_ref, sems, waves, work)
    half_ref[...] = acc_ref[:row_blocks].astype(half_ref.dtype)
    stores = fetch(half_ref, out_ref, put, put.shape[0])
    start_all(stores)
    wait_all(stores)


def forward(rows, cols, count, sens, wave):
    slots = sens.shape[0]
    width = wave.shape[2]
    return pl.pallas_call(
        forward_body,
        out_shape=jax.ShapeDtypeStruct((RB_DEV, BLK, width), jnp.bfloat16),
        in_specs=[SMEM_SPEC, SMEM_SPEC, SMEM_SPEC, ANY_SPEC, ANY_SPEC],
        out_specs=ANY_SPEC,
        scratch_shapes=[
            pltpu.VMEM(sens.shape, sens.dtype),
            pltpu.VMEM(wave.shape, wave.dtype),
            pltpu.VMEM((RB_DEV + 1, BLK, width), jnp.float32),
            pltpu.VMEM((RB_DEV, BLK, width), jnp.bfloat16),
            pltpu.SemaphoreType.DMA((slots // STEP,)),
            pltpu.SemaphoreType.DMA((8,)),
            pltpu.SemaphoreType.DMA((4,)),
        ],
        compiler_params=pltpu.CompilerParams(vmem_limit_bytes=LARGE),
        cost_estimate=pl.CostEstimate(
            flops=2 * slots * BLK * BLK * width, bytes_accessed=2 * slots * BLK * BLK,
            transcendentals=0,
        ),
        name="forward",
    )(rows, cols, count, sens, wave)


def adjoint_body(rows_ref, cols_ref, count_ref, sens_ref, image_ref, after_ref, *refs, per_peer):
    chunks = len(refs) - 7
    out_refs = refs[:chunks]
    block_ref, held_ref, acc_ref, half_ref, sems, got, put = refs[chunks:]
    cols = acc_ref.shape[0] - 1
    peers, each = cols // per_peer, per_peer // chunks
    acc_ref[...] = jnp.zeros_like(acc_ref)

    def work(slot, block, live):
        col = jnp.where(live, cols_ref[0, slot], cols)
        acc_ref[col] += lax.dot_general(
            block, held_ref[rows_ref[0, slot]], (((0,), (0,)), ((), ())),
            preferred_element_type=jnp.float32,
        )

    images = fetch(image_ref, held_ref, got, got.shape[0])
    slot_loop(count_ref[0, 0], sens_ref, block_ref, sems, images, work)
    stores = []
    for chunk, out_ref in enumerate(out_refs):
        for peer in range(peers):
            first = peer * per_peer + chunk * each
            half_ref[chunk, peer * each : (peer + 1) * each] = acc_ref[
                first : first + each
            ].astype(half_ref.dtype)
        stores.append(pltpu.make_async_copy(half_ref.at[chunk], out_ref, put.at[chunk]))
        stores[-1].start()
    wait_all(stores)


def adjoint(rows, cols, count, sens, image, after, blocks, per_peer, chunks):
    slots = sens.shape[0]
    width = image.shape[2]
    chunk = (blocks // chunks, BLK, width)
    return pl.pallas_call(
        lambda *refs: adjoint_body(*refs, per_peer=per_peer),
        out_shape=[jax.ShapeDtypeStruct(chunk, jnp.bfloat16)] * chunks,
        in_specs=[SMEM_SPEC, SMEM_SPEC, SMEM_SPEC, ANY_SPEC, ANY_SPEC, ANY_SPEC],
        out_specs=[ANY_SPEC] * chunks,
        scratch_shapes=[
            pltpu.VMEM(sens.shape, sens.dtype),
            pltpu.VMEM(image.shape, image.dtype),
            pltpu.VMEM((blocks + 1, BLK, width), jnp.float32),
            pltpu.VMEM((chunks, *chunk), jnp.bfloat16),
            pltpu.SemaphoreType.DMA((slots // STEP,)),
            pltpu.SemaphoreType.DMA((4,)),
            pltpu.SemaphoreType.DMA((chunks,)),
        ],
        compiler_params=pltpu.CompilerParams(vmem_limit_bytes=LARGE),
        cost_estimate=pl.CostEstimate(
            flops=2 * slots * BLK * BLK * width, bytes_accessed=2 * slots * BLK * BLK,
            transcendentals=0,
        ),
        name="adjoint",
    )(rows, cols, count, sens, image, after)


def smooth_body(offset_ref, low_ref, model_ref, high_ref, near_ref, weight_ref, after_ref,
                out_ref, ext_ref, value_ref, got, ends, put):
    cells = model_ref.shape[0]
    steps = put.shape[0]
    tiles = cells // BLK // steps
    each = cells // got.shape[0]
    loads = [
        pltpu.make_async_copy(
            model_ref.at[pl.ds(i * each, each)], ext_ref.at[pl.ds(RIM + i * each, each)], got.at[i]
        )
        for i in range(got.shape[0])
    ]
    loads.append(pltpu.make_async_copy(low_ref, ext_ref.at[pl.ds(0, RIM)], ends.at[0]))
    loads.append(
        pltpu.make_async_copy(high_ref, ext_ref.at[pl.ds(RIM + cells, RIM)], ends.at[1])
    )
    start_all(loads)
    wait_all(loads)
    span = lax.broadcasted_iota(jnp.int32, (2 * BLK, BLK), 0)
    center = lax.broadcasted_iota(jnp.int32, (2 * BLK, BLK), 1) + RIM

    def store(step):
        part = pl.ds(step * tiles * BLK, tiles * BLK)
        return pltpu.make_async_copy(value_ref.at[part], out_ref.at[part], put.at[step])

    @pl.loop(0, steps)
    def _(step):
        for t in range(tiles):
            start = pl.multiple_of((step * tiles + t) * BLK, BLK)
            near = near_ref[:, pl.ds(start, BLK)] - (offset_ref[0] + start)
            face = weight_ref[:, pl.ds(start, BLK)]
            mix = jnp.where(span == center, jnp.sum(face, axis=0, keepdims=True), 0.0)
            for k in range(4):
                mix = mix - jnp.where(span == near[k : k + 1], face[k : k + 1], 0.0)
            window = ext_ref[pl.ds(start, 2 * BLK), :]
            mix_high = mix.astype(jnp.bfloat16)
            mix_low = (mix - mix_high.astype(jnp.float32)).astype(jnp.bfloat16)
            near_high = window.astype(jnp.bfloat16)
            near_low = (window - near_high.astype(jnp.float32)).astype(jnp.bfloat16)
            value_ref[pl.ds(start, BLK), :] = lax.dot_general(
                jnp.concatenate([mix_high, mix_high, mix_low], axis=0),
                jnp.concatenate([near_high, near_low, near_high], axis=0),
                (((0,), (0,)), ((), ())), preferred_element_type=jnp.float32,
            )
        store(step).start()

    for step in range(steps):
        store(step).wait()


def smoothing(offset, low, model, high, neighbors, face_weight, after):
    cells, width = model.shape
    return pl.pallas_call(
        smooth_body,
        out_shape=jax.ShapeDtypeStruct((cells, width), jnp.float32),
        in_specs=[SMEM_SPEC, ANY_SPEC, ANY_SPEC, ANY_SPEC, VMEM_SPEC, VMEM_SPEC, ANY_SPEC],
        out_specs=ANY_SPEC,
        scratch_shapes=[
            pltpu.VMEM((cells + 2 * RIM, width), jnp.float32),
            pltpu.VMEM((cells, width), jnp.float32),
            pltpu.SemaphoreType.DMA((16,)),
            pltpu.SemaphoreType.DMA((2,)),
            pltpu.SemaphoreType.DMA((8,)),
        ],
        compiler_params=pltpu.CompilerParams(vmem_limit_bytes=LARGE),
        cost_estimate=pl.CostEstimate(
            flops=24 * cells * BLK * width, bytes_accessed=16 * cells * width, transcendentals=0
        ),
        name="smoothing",
    )(offset, low, model, high, neighbors, face_weight, after)


def finish_body(take_ref, cells_ref, basis_ref, got_ref, mine_ref, base_ref, after_ref,
                out_ref, token_ref, block_ref, got, put, *, chunk):
    cols = got_ref.shape[0]
    fetches, stores = [], []
    for i in range(cols):
        cell = cells_ref[chunk * cols + i]
        fetches.append(pltpu.make_async_copy(base_ref.at[cell], block_ref.at[i], got.at[i]))
        stores.append(pltpu.make_async_copy(block_ref.at[i], out_ref.at[cell], put.at[i]))
    start_all(fetches)
    wait_all(fetches)
    for i in range(cols):
        wave = jnp.where(take_ref[0] > 0, got_ref[i], mine_ref[i])
        both = jnp.concatenate([wave, wave], axis=0)
        block_ref[i] += jnp.dot(basis_ref[...], both, preferred_element_type=jnp.float32)
    start_all(stores)
    token_ref[...] = jnp.zeros_like(token_ref)
    wait_all(stores)


def finish(take, cells, got, mine, base, after, chunk):
    cols, _, width = got.shape
    basis = haar_matrix(BLK).T.astype(np.float32)
    high = basis.astype(jnp.bfloat16)
    low = (basis - high.astype(np.float32)).astype(jnp.bfloat16)
    basis2 = jnp.asarray(np.concatenate([high, low], axis=1))
    return pl.pallas_call(
        lambda *refs: finish_body(*refs, chunk=chunk),
        out_shape=[
            jax.ShapeDtypeStruct(base.shape, base.dtype),
            jax.ShapeDtypeStruct((8, BLK), jnp.float32),
        ],
        in_specs=[SMEM_SPEC, SMEM_SPEC, VMEM_SPEC, VMEM_SPEC, VMEM_SPEC, ANY_SPEC, ANY_SPEC],
        out_specs=[ANY_SPEC, VMEM_SPEC],
        input_output_aliases={5: 0},
        scratch_shapes=[
            pltpu.VMEM((cols, BLK, width), jnp.float32),
            pltpu.SemaphoreType.DMA((cols,)),
            pltpu.SemaphoreType.DMA((cols,)),
        ],
        compiler_params=pltpu.CompilerParams(vmem_limit_bytes=SMALL),
        cost_estimate=pl.CostEstimate(
            flops=4 * cols * BLK * BLK * width, bytes_accessed=10 * cols * BLK * width,
            transcendentals=0,
        ),
        name="finish",
    )(take, cells, basis2, got, mine, base, after)


def merge_body(got_ref, mine_ref, after_ref, out_ref):
    total = got_ref[...].astype(jnp.float32) + mine_ref[...].astype(jnp.float32)
    out_ref[...] = total.astype(out_ref.dtype)


def merge(got, mine, after):
    return pl.pallas_call(
        merge_body,
        out_shape=jax.ShapeDtypeStruct(mine.shape, mine.dtype),
        in_specs=[VMEM_SPEC, VMEM_SPEC, ANY_SPEC],
        out_specs=VMEM_SPEC,
        compiler_params=pltpu.CompilerParams(vmem_limit_bytes=SMALL),
        cost_estimate=pl.CostEstimate(
            flops=mine.size, bytes_accessed=6 * mine.size, transcendentals=0
        ),
        name="merge",
    )(got, mine, after)


def line_sums(parts, axis, deliver):
    count = lax.axis_size(axis)
    half = count // 2
    me = lax.axis_index(axis)
    stages = []
    for hop in range(half - 1):
        stages.append(([(hop, hop + 1), (count - 1 - hop, count - 2 - hop)], False))
    stages.append(([(half - 1, half), (half, half - 1)], False))
    for hop in range(half - 1):
        left, right = half - 1 - hop, half + hop
        stages.append(([(left, left - 1), (right, right + 1)], True))
    state = list(parts)
    got = [lax.ppermute(part, axis, stages[0][0]) for part in parts]
    after = parts[0]
    for time in range(len(parts) + len(stages) - 1):
        for s, (pairs, outwards) in enumerate(stages):
            k = time - s
            if not 0 <= k < len(parts):
                continue
            last = s + 1 == len(stages)
            if outwards:
                take = (me == pairs[0][1]) | (me == pairs[1][1])
                take = take.astype(jnp.int32).reshape(1)
                if last:
                    after = deliver(k, take, got[k], state[k], after)
                else:
                    state[k] = jnp.where(take[0] > 0, got[k], state[k])
            else:
                state[k] = after = merge(got[k], state[k], after)
                if last:
                    after = deliver(k, jnp.zeros((1,), jnp.int32), state[k], state[k], after)
            if not last:
                got[k] = lax.ppermute(state[k], axis, stages[s + 1][0])


def halo(block, axis, width):
    count = lax.axis_size(axis)
    forward_pairs = [(i, i + 1) for i in range(count - 1)]
    backward_pairs = [(target, source) for source, target in forward_pairs]
    low = lax.ppermute(block[block.shape[0] - width :], axis, forward_pairs)
    high = lax.ppermute(block[:width], axis, backward_pairs)
    return low, high


def local(model_dir, sens_blocks, blk_row, blk_col, blk_count, send_order, neighbors, face_weight):
    cell_count, width = model_dir.shape
    blocks = cell_count // BLK
    col_devices = lax.axis_size("cols")
    per_peer = blocks // col_devices
    model_blocks = model_dir.reshape(blocks, BLK, width)
    sens = sens_blocks[0]
    chunks = math.gcd(CHUNKS, per_peer)
    each = per_peer // chunks

    outgoing = analyze(send_order, model_blocks)
    wave = lax.all_to_all(
        outgoing.reshape(col_devices, per_peer * BLK, width), "cols", 0, 0, tiled=True
    ).reshape(blocks, BLK, width)

    model_late, order_late, _ = lax.optimization_barrier((model_dir, send_order, outgoing))
    low, high = halo(model_late, "cols", RIM)
    offset = (lax.axis_index("cols") * cell_count - RIM).astype(jnp.int32).reshape(1)
    cells = order_late.reshape(col_devices, chunks, each).transpose(1, 0, 2).reshape(blocks)

    partial_rows = forward(blk_row, blk_col, blk_count, sens, wave)
    shares = lax.all_to_all(
        partial_rows.reshape(col_devices, -1, width), "cols", 0, 0, tiled=True
    )
    smooth = smoothing(offset, low, model_dir, high, neighbors, face_weight, partial_rows)
    image_share = jnp.sum(shares.astype(jnp.float32), axis=0).astype(jnp.bfloat16)
    image_half = lax.all_to_all(
        jnp.broadcast_to(image_share, shares.shape), "cols", 0, 0, tiled=True
    ).reshape(-1, width)
    data_image = image_half.astype(jnp.float32)

    partial_cols = adjoint(
        blk_row, blk_col, blk_count, sens, image_half.reshape(RB_DEV, BLK, width), smooth,
        blocks, per_peer, chunks,
    )
    returned = [
        lax.all_to_all(
            part.reshape(col_devices, each * BLK, width), "cols", 0, 0, tiled=True
        ).reshape(col_devices * each, BLK, width)
        for part in partial_cols
    ]
    normal = smooth.reshape(blocks, BLK, width)

    def deliver(chunk, take, got, mine, after):
        nonlocal normal
        normal, token = finish(take, cells, got, mine, normal, after, chunk)
        return token

    line_sums(returned, "rows", deliver)
    return (data_image, normal.reshape(cell_count, width))


def solution(mesh):
    placed = (
        P("cols", None),
        P("rows", "cols", None, None),
        P("rows", "cols"),
        P("rows", "cols"),
        P("rows", "cols"),
        P("cols", None),
        P(None, "cols"),
        P(None, "cols"),
    )
    return jax.shard_map(
        local,
        mesh=mesh,
        in_specs=placed,
        out_specs=(P("rows", None), P("cols", None)),
        check_vma=False,
    )
```

```python
import math

import jax
import jax.numpy as jnp
import numpy as np
from jax import lax
from jax.experimental import pallas as pl
from jax.experimental.pallas import tpu as pltpu
from jax.sharding import PartitionSpec as P

BLK = 128
RB_DEV = 32
RIM = 64
STEP = 16
MIB = 1 << 20
SMALL = 16 * MIB
LARGE = 56 * MIB
ANY_SPEC = pl.BlockSpec(memory_space=pl.ANY)
VMEM_SPEC = pl.BlockSpec(memory_space=pltpu.VMEM)
SMEM_SPEC = pl.BlockSpec(memory_space=pltpu.SMEM)


def haar_matrix(order_n):
    matrix = np.ones((1, 1))
    while matrix.shape[0] < order_n:
        length = matrix.shape[0]
        upper = np.kron(matrix, np.array([[1.0, 1.0]]))
        lower = np.kron(np.eye(length), np.array([[1.0, -1.0]]))
        matrix = np.concatenate([upper, lower], axis=0) / math.sqrt(2.0)
    return matrix


def fetch(source, target, sems, pieces):
    each = source.shape[0] // pieces
    parts = [pl.ds(i * each, each) for i in range(pieces)]
    return [
        pltpu.make_async_copy(source.at[part], target.at[part], sems.at[i])
        for i, part in enumerate(parts)
    ]


def gather_pieces(pieces, held_ref, me, sems):
    each = pieces[0].shape[0]
    return [
        pltpu.make_async_copy(
            piece, held_ref.at[pl.ds((me ^ offset) * each, each)], sems.at[offset]
        )
        for offset, piece in enumerate(pieces)
    ]


def far_first(count):
    return sorted(range(count), key=lambda offset: (-bin(offset >> 1).count("1"), offset))


def start_all(copies):
    for copy in copies:
        copy.start()


def wait_all(copies):
    for copy in copies:
        copy.wait()


def analyze_body(me_ref, order_ref, model_ref, *refs):
    out_refs, (block_ref, coeff_ref, got, put) = refs[:-4], refs[-4:]
    width = model_ref.shape[2]
    per_peer = out_refs[0].shape[0]
    me = me_ref[0]
    loads = fetch(model_ref, block_ref, got, got.shape[0])
    start_all(loads)
    row = lax.broadcasted_iota(jnp.int32, (BLK, BLK), 0)
    col = lax.broadcasted_iota(jnp.int32, (BLK, BLK), 1)
    level = jnp.ones_like(row)
    scale = jnp.full((BLK, width), BLK**-0.5, jnp.float32)
    wide_row = lax.broadcasted_iota(jnp.int32, (BLK, width), 0)
    size = 2
    while size < BLK:
        level = jnp.where(row >= size, size, level)
        scale = jnp.where(wide_row >= size, (size / BLK) ** 0.5, scale)
        size *= 2
    span = BLK // level
    inside = col - (row - level) * span
    sign = jnp.where(inside * 2 < span, 1.0, -1.0)
    sign = jnp.where((inside >= 0) & (inside < span), sign, 0.0)
    sign = jnp.where(row == 0, 1.0, sign).astype(jnp.bfloat16)
    both_signs = jnp.concatenate([sign, sign], axis=1)
    wait_all(loads)
    stores = []
    for offset in far_first(len(out_refs)):
        peer = (me ^ offset) * per_peer
        for q in range(per_peer):
            x = block_ref[order_ref[0, peer + q]]
            high = x.astype(jnp.bfloat16)
            low = (x - high.astype(jnp.float32)).astype(jnp.bfloat16)
            raw = jnp.dot(
                both_signs, jnp.concatenate([high, low], axis=0),
                preferred_element_type=jnp.float32,
            )
            coeff_ref[offset, q] = (raw * scale).astype(jnp.bfloat16)
        stores.append(
            pltpu.make_async_copy(coeff_ref.at[offset], out_refs[offset], put.at[offset])
        )
        stores[-1].start()
    wait_all(stores)


def analyze(me, order, model_blocks, peers):
    blocks, _, width = model_blocks.shape
    piece = (blocks // peers, BLK, width)
    return pl.pallas_call(
        analyze_body,
        out_shape=[jax.ShapeDtypeStruct(piece, jnp.bfloat16)] * peers,
        in_specs=[SMEM_SPEC, SMEM_SPEC, ANY_SPEC],
        out_specs=[ANY_SPEC] * peers,
        scratch_shapes=[
            pltpu.VMEM((blocks, BLK, width), jnp.float32),
            pltpu.VMEM((peers, *piece), jnp.bfloat16),
            pltpu.SemaphoreType.DMA((16,)),
            pltpu.SemaphoreType.DMA((peers,)),
        ],
        compiler_params=pltpu.CompilerParams(vmem_limit_bytes=LARGE),
        cost_estimate=pl.CostEstimate(
            flops=4 * blocks * BLK * BLK * width, bytes_accessed=6 * blocks * BLK * width,
            transcendentals=0,
        ),
        name="analyze",
    )(me, order, model_blocks)


def slot_loop(count, sens_ref, block_ref, sems, others, work):
    steps = sems.shape[0]
    each = sens_ref.shape[0] // steps

    def block_copy(step):
        part = pl.ds(step * each, each)
        return pltpu.make_async_copy(sens_ref.at[part], block_ref.at[part], sems.at[step])

    start_all(others)
    needed = (count + each - 1) // each

    @pl.loop(0, needed)
    def _(step):
        block_copy(step).start()

    wait_all(others)

    @pl.loop(0, needed)
    def _(step):
        block_copy(step).wait()
        for k in range(each):
            slot = step * each + k
            work(slot, block_ref[slot], slot < count)


def forward_body(me_ref, rows_ref, cols_ref, count_ref, sens_ref, *refs):
    peers = (len(refs) - 10) // 2
    wave_refs, out_refs = refs[:peers], refs[peers + 3 : 2 * peers + 3]
    block_ref, held_ref, acc_ref, half_ref, sems, got, put = refs[2 * peers + 3 :]
    row_blocks = acc_ref.shape[0] - 1
    each = row_blocks // peers
    me = me_ref[0]
    acc_ref[...] = jnp.zeros_like(acc_ref)

    def work(slot, block, live):
        row = jnp.where(live, rows_ref[0, slot], row_blocks)
        acc_ref[row] += jnp.dot(
            block, held_ref[cols_ref[0, slot]], preferred_element_type=jnp.float32
        )

    waves = gather_pieces(wave_refs, held_ref, me, got)
    slot_loop(count_ref[0, 0], sens_ref, block_ref, sems, waves, work)
    stores = []
    for offset, out_ref in enumerate(out_refs):
        part = acc_ref[pl.ds((me ^ offset) * each, each)]
        half_ref[offset] = part.astype(half_ref.dtype)
        stores.append(pltpu.make_async_copy(half_ref.at[offset], out_ref, put.at[offset]))
        stores[-1].start()
    wait_all(stores)


def forward(me, rows, cols, count, sens, waves, after):
    slots = sens.shape[0]
    peers = len(waves)
    per_peer, _, width = waves[0].shape
    piece = (RB_DEV // peers, BLK, width)
    assert len(after) == 3
    return pl.pallas_call(
        forward_body,
        out_shape=[jax.ShapeDtypeStruct(piece, jnp.bfloat16)] * peers,
        in_specs=[SMEM_SPEC] * 4 + [ANY_SPEC] * (1 + peers + 3),
        out_specs=[ANY_SPEC] * peers,
        scratch_shapes=[
            pltpu.VMEM(sens.shape, sens.dtype),
            pltpu.VMEM((peers * per_peer, BLK, width), jnp.bfloat16),
            pltpu.VMEM((RB_DEV + 1, BLK, width), jnp.float32),
            pltpu.VMEM((peers, *piece), jnp.bfloat16),
            pltpu.SemaphoreType.DMA((slots // STEP,)),
            pltpu.SemaphoreType.DMA((peers,)),
            pltpu.SemaphoreType.DMA((peers,)),
        ],
        compiler_params=pltpu.CompilerParams(vmem_limit_bytes=LARGE),
        cost_estimate=pl.CostEstimate(
            flops=2 * slots * BLK * BLK * width, bytes_accessed=2 * slots * BLK * BLK,
            transcendentals=0,
        ),
        name="forward",
    )(me, rows, cols, count, sens, *waves, *after)


def adjoint_body(me_ref, rows_ref, cols_ref, count_ref, sens_ref, *refs):
    peers = (len(refs) - 10) // 2
    image_refs, out_refs = refs[:peers], refs[peers + 1 : 2 * peers + 1]
    image_out_ref = refs[2 * peers + 1]
    block_ref, held_ref, acc_ref, half_ref, sems, got, put, whole = refs[2 * peers + 2 :]
    col_blocks = acc_ref.shape[0] - 1
    each = col_blocks // peers
    me = me_ref[0]
    acc_ref[...] = jnp.zeros_like(acc_ref)

    def work(slot, block, live):
        col = jnp.where(live, cols_ref[0, slot], col_blocks)
        acc_ref[col] += lax.dot_general(
            block, held_ref[rows_ref[0, slot]], (((0,), (0,)), ((), ())),
            preferred_element_type=jnp.float32,
        )

    images = gather_pieces(image_refs, held_ref, me, got)
    slot_loop(count_ref[0, 0], sens_ref, block_ref, sems, images, work)
    stores = fetch(held_ref, image_out_ref, whole, whole.shape[0])
    start_all(stores)
    for offset, out_ref in enumerate(out_refs):
        part = acc_ref[pl.ds((me ^ offset) * each, each)]
        half_ref[offset] = part.astype(half_ref.dtype)
        stores.append(pltpu.make_async_copy(half_ref.at[offset], out_ref, put.at[offset]))
        stores[-1].start()
    wait_all(stores)


def adjoint(me, rows, cols, count, sens, images, after, blocks):
    slots = sens.shape[0]
    peers = len(images)
    width = images[0].shape[2]
    piece = (blocks // peers, BLK, width)
    image = (RB_DEV, BLK, width)
    outs = pl.pallas_call(
        adjoint_body,
        out_shape=[jax.ShapeDtypeStruct(piece, jnp.bfloat16)] * peers
        + [jax.ShapeDtypeStruct(image, jnp.bfloat16)],
        in_specs=[SMEM_SPEC] * 4 + [ANY_SPEC] * (1 + peers + 1),
        out_specs=[ANY_SPEC] * (peers + 1),
        scratch_shapes=[
            pltpu.VMEM(sens.shape, sens.dtype),
            pltpu.VMEM(image, jnp.bfloat16),
            pltpu.VMEM((blocks + 1, BLK, width), jnp.float32),
            pltpu.VMEM((peers, *piece), jnp.bfloat16),
            pltpu.SemaphoreType.DMA((slots // STEP,)),
            pltpu.SemaphoreType.DMA((peers,)),
            pltpu.SemaphoreType.DMA((peers,)),
            pltpu.SemaphoreType.DMA((4,)),
        ],
        compiler_params=pltpu.CompilerParams(vmem_limit_bytes=LARGE),
        cost_estimate=pl.CostEstimate(
            flops=2 * slots * BLK * BLK * width, bytes_accessed=2 * slots * BLK * BLK,
            transcendentals=0,
        ),
        name="adjoint",
    )(me, rows, cols, count, sens, *images, after)
    return outs[:peers], outs[peers]


def tile_value(near, face, window):
    span = lax.broadcasted_iota(jnp.int32, (2 * BLK, BLK), 0)
    center = lax.broadcasted_iota(jnp.int32, (2 * BLK, BLK), 1) + RIM
    mix = jnp.where(span == center, jnp.sum(face, axis=0, keepdims=True), 0.0)
    for k in range(4):
        mix = mix - jnp.where(span == near[k : k + 1], face[k : k + 1], 0.0)
    mix_high = mix.astype(jnp.bfloat16)
    mix_low = (mix - mix_high.astype(jnp.float32)).astype(jnp.bfloat16)
    near_high = window.astype(jnp.bfloat16)
    near_low = (window - near_high.astype(jnp.float32)).astype(jnp.bfloat16)
    return lax.dot_general(
        jnp.concatenate([mix_high, mix_high, mix_low], axis=0),
        jnp.concatenate([near_high, near_low, near_high], axis=0),
        (((0,), (0,)), ((), ())), preferred_element_type=jnp.float32,
    )


def smooth_body(offset_ref, model_ref, near_ref, weight_ref, after_ref,
                out_ref, ext_ref, value_ref, got, put):
    cells, width = model_ref.shape
    steps = put.shape[0]
    tiles = cells // BLK // steps
    each = cells // got.shape[0]
    loads = [
        pltpu.make_async_copy(
            model_ref.at[pl.ds(i * each, each)], ext_ref.at[pl.ds(RIM + i * each, each)], got.at[i]
        )
        for i in range(got.shape[0])
    ]
    start_all(loads)
    ext_ref[:RIM] = jnp.zeros((RIM, width), jnp.float32)
    ext_ref[RIM + cells :] = jnp.zeros((RIM, width), jnp.float32)
    wait_all(loads)

    def store(step):
        part = pl.ds(step * tiles * BLK, tiles * BLK)
        return pltpu.make_async_copy(value_ref.at[part], out_ref.at[part], put.at[step])

    @pl.loop(0, steps)
    def _(step):
        for t in range(tiles):
            start = pl.multiple_of((step * tiles + t) * BLK, BLK)
            near = near_ref[:, pl.ds(start, BLK)] - (offset_ref[0] + start)
            face = weight_ref[:, pl.ds(start, BLK)]
            window = ext_ref[pl.ds(start, 2 * BLK), :]
            value_ref[pl.ds(start, BLK), :] = tile_value(near, face, window)
        store(step).start()

    for step in range(steps):
        store(step).wait()


def smoothing(offset, model, neighbors, face_weight, after):
    cells, width = model.shape
    return pl.pallas_call(
        smooth_body,
        out_shape=jax.ShapeDtypeStruct((cells, width), jnp.float32),
        in_specs=[SMEM_SPEC, ANY_SPEC, VMEM_SPEC, VMEM_SPEC, ANY_SPEC],
        out_specs=ANY_SPEC,
        scratch_shapes=[
            pltpu.VMEM((cells + 2 * RIM, width), jnp.float32),
            pltpu.VMEM((cells, width), jnp.float32),
            pltpu.SemaphoreType.DMA((16,)),
            pltpu.SemaphoreType.DMA((8,)),
        ],
        compiler_params=pltpu.CompilerParams(vmem_limit_bytes=LARGE),
        cost_estimate=pl.CostEstimate(
            flops=24 * cells * BLK * width, bytes_accessed=16 * cells * width, transcendentals=0
        ),
        name="smoothing",
    )(offset, model, neighbors, face_weight, after)


def edges_body(offset_ref, low_ref, model_ref, high_ref, near_ref, weight_ref, base_ref, after_ref,
               out_ref, window_ref, value_ref, got, put):
    cells = model_ref.shape[0]
    inner = 2 * BLK - RIM
    starts = (0, cells - BLK)
    loads = [
        pltpu.make_async_copy(low_ref, window_ref.at[0, pl.ds(0, RIM)], got.at[0]),
        pltpu.make_async_copy(
            model_ref.at[pl.ds(0, inner)], window_ref.at[0, pl.ds(RIM, inner)], got.at[1]
        ),
        pltpu.make_async_copy(
            model_ref.at[pl.ds(cells - inner, inner)], window_ref.at[1, pl.ds(0, inner)], got.at[2]
        ),
        pltpu.make_async_copy(high_ref, window_ref.at[1, pl.ds(inner, RIM)], got.at[3]),
    ]
    start_all(loads)
    wait_all(loads)
    stores = []
    for i, start in enumerate(starts):
        near = near_ref[:, start : start + BLK] - (offset_ref[0] + start)
        value_ref[i] = tile_value(near, weight_ref[:, start : start + BLK], window_ref[i])
        stores.append(
            pltpu.make_async_copy(value_ref.at[i], out_ref.at[pl.ds(start, BLK)], put.at[i])
        )
    start_all(stores)
    wait_all(stores)


def edges(offset, low, model, high, neighbors, face_weight, base, after):
    width = model.shape[1]
    return pl.pallas_call(
        edges_body,
        out_shape=jax.ShapeDtypeStruct(base.shape, base.dtype),
        in_specs=[SMEM_SPEC, ANY_SPEC, ANY_SPEC, ANY_SPEC, VMEM_SPEC, VMEM_SPEC, ANY_SPEC, ANY_SPEC],
        out_specs=ANY_SPEC,
        input_output_aliases={6: 0},
        scratch_shapes=[
            pltpu.VMEM((2, 2 * BLK, width), jnp.float32),
            pltpu.VMEM((2, BLK, width), jnp.float32),
            pltpu.SemaphoreType.DMA((4,)),
            pltpu.SemaphoreType.DMA((2,)),
        ],
        compiler_params=pltpu.CompilerParams(vmem_limit_bytes=SMALL),
        cost_estimate=pl.CostEstimate(
            flops=24 * 2 * BLK * BLK * width, bytes_accessed=32 * BLK * width, transcendentals=0
        ),
        name="edges",
    )(offset, low, model, high, neighbors, face_weight, base, after)


def finish_body(me_ref, take_ref, order_ref, basis_ref, got_ref, mine_ref, base_ref, after_ref,
                out_ref, token_ref, block_ref, value_ref, got, put, *, offsets):
    cols = got_ref.shape[0]
    per_peer = cols // len(offsets)
    fetches, stores = [], []
    for i in range(cols):
        offset = offsets[i // per_peer]
        cell = order_ref[0, (me_ref[0] ^ offset) * per_peer + i % per_peer]
        fetches.append(pltpu.make_async_copy(base_ref.at[cell], block_ref.at[i], got.at[i]))
        stores.append(pltpu.make_async_copy(block_ref.at[i], out_ref.at[cell], put.at[i]))
    start_all(fetches)
    for i in range(cols):
        wave = jnp.where(take_ref[0] > 0, got_ref[i], mine_ref[i])
        both = jnp.concatenate([wave, wave], axis=0)
        value_ref[i] = jnp.dot(basis_ref[...], both, preferred_element_type=jnp.float32)
    wait_all(fetches)
    block_ref[...] += value_ref[...]
    start_all(stores)
    token_ref[...] = jnp.zeros_like(token_ref)
    wait_all(stores)


def finish(me, take, order, got, mine, base, after, offsets):
    cols, _, width = got.shape
    basis = haar_matrix(BLK).T.astype(np.float32)
    high = basis.astype(jnp.bfloat16)
    low = (basis - high.astype(np.float32)).astype(jnp.bfloat16)
    basis2 = jnp.asarray(np.concatenate([high, low], axis=1))
    return pl.pallas_call(
        lambda *refs: finish_body(*refs, offsets=offsets),
        out_shape=[
            jax.ShapeDtypeStruct(base.shape, base.dtype),
            jax.ShapeDtypeStruct((8, BLK), jnp.float32),
        ],
        in_specs=[SMEM_SPEC] * 3 + [VMEM_SPEC] * 3 + [ANY_SPEC] * 2,
        out_specs=[ANY_SPEC, VMEM_SPEC],
        input_output_aliases={6: 0},
        scratch_shapes=[
            pltpu.VMEM((cols, BLK, width), jnp.float32),
            pltpu.VMEM((cols, BLK, width), jnp.float32),
            pltpu.SemaphoreType.DMA((cols,)),
            pltpu.SemaphoreType.DMA((cols,)),
        ],
        compiler_params=pltpu.CompilerParams(vmem_limit_bytes=SMALL),
        cost_estimate=pl.CostEstimate(
            flops=4 * cols * BLK * BLK * width, bytes_accessed=10 * cols * BLK * width,
            transcendentals=0,
        ),
        name="finish",
    )(me, take, order, basis2, got, mine, base, after)


def merge_body(got_ref, mine_ref, after_ref, out_ref):
    total = got_ref[...].astype(jnp.float32) + mine_ref[...].astype(jnp.float32)
    out_ref[...] = total.astype(out_ref.dtype)


def merge(got, mine, after):
    return pl.pallas_call(
        merge_body,
        out_shape=jax.ShapeDtypeStruct(mine.shape, mine.dtype),
        in_specs=[VMEM_SPEC, VMEM_SPEC, ANY_SPEC],
        out_specs=VMEM_SPEC,
        compiler_params=pltpu.CompilerParams(vmem_limit_bytes=SMALL),
        cost_estimate=pl.CostEstimate(
            flops=mine.size, bytes_accessed=6 * mine.size, transcendentals=0
        ),
        name="merge",
    )(got, mine, after)


def line_sums(parts, axis, deliver):
    count = lax.axis_size(axis)
    half = count // 2
    me = lax.axis_index(axis)
    stages = []
    for hop in range(half - 1):
        stages.append(([(hop, hop + 1), (count - 1 - hop, count - 2 - hop)], False))
    stages.append(([(half - 1, half), (half, half - 1)], False))
    for hop in range(half - 1):
        left, right = half - 1 - hop, half + hop
        stages.append(([(left, left - 1), (right, right + 1)], True))
    state = list(parts)
    got = [lax.ppermute(part, axis, stages[0][0]) for part in parts]
    after = parts[0]
    for time in range(len(parts) + len(stages) - 1):
        for s, (pairs, outwards) in enumerate(stages):
            k = time - s
            if not 0 <= k < len(parts):
                continue
            last = s + 1 == len(stages)
            if outwards:
                take = (me == pairs[0][1]) | (me == pairs[1][1])
                take = take.astype(jnp.int32).reshape(1)
                if last:
                    after = deliver(k, take, got[k], state[k], after)
                else:
                    state[k] = jnp.where(take[0] > 0, got[k], state[k])
            else:
                state[k] = after = merge(got[k], state[k], after)
                if last:
                    after = deliver(k, jnp.zeros((1,), jnp.int32), state[k], state[k], after)
            if not last:
                got[k] = lax.ppermute(state[k], axis, stages[s + 1][0])


def halo(block, axis, width):
    count = lax.axis_size(axis)
    forward_pairs = [(i, i + 1) for i in range(count - 1)]
    backward_pairs = [(target, source) for source, target in forward_pairs]
    low = lax.ppermute(block[block.shape[0] - width :], axis, forward_pairs)
    high = lax.ppermute(block[:width], axis, backward_pairs)
    return low, high


def swap(piece, axis, offset):
    return lax.ppermute(piece, axis, [(c, c ^ offset) for c in range(lax.axis_size(axis))])


def exchange(pieces, axis):
    got = list(pieces)
    for offset in far_first(len(pieces)):
        if offset:
            got[offset] = swap(pieces[offset], axis, offset)
    return got


def local(model_dir, sens_blocks, blk_row, blk_col, blk_count, send_order, neighbors, face_weight):
    cell_count, width = model_dir.shape
    blocks = cell_count // BLK
    peers = lax.axis_size("cols")
    col = lax.axis_index("cols").astype(jnp.int32)
    me = col.reshape(1)
    offset = (col * cell_count - RIM).reshape(1)
    sens = sens_blocks[0]

    outgoing = analyze(me, send_order, model_dir.reshape(blocks, BLK, width), peers)
    waves = exchange(outgoing, "cols")
    smooth = smoothing(offset, model_dir, neighbors, face_weight, outgoing[0])
    model_late, _ = lax.optimization_barrier((model_dir, outgoing[0]))
    low, high = halo(model_late, "cols", RIM)

    partial_rows = forward(me, blk_row, blk_col, blk_count, sens, waves, (smooth, low, high))
    shares = exchange(partial_rows, "cols")
    smooth = edges(
        offset, low, model_dir, high, neighbors, face_weight, smooth, partial_rows[0]
    )
    total = sum(share.astype(jnp.float32) for share in shares)
    image_share = total.astype(jnp.bfloat16)
    images = exchange([image_share] * peers, "cols")

    partial_cols, image = adjoint(
        me, blk_row, blk_col, blk_count, sens, images, smooth, blocks
    )
    data_image = image.reshape(RB_DEV * BLK, width).astype(jnp.float32)
    groups = [[0], [1]] + [[o, o + 1] for o in range(2, peers, 2)]
    chunks = []
    for group in groups:
        got = [swap(partial_cols[o], "cols", o) if o else partial_cols[o] for o in group]
        chunks.append(got[0] if len(got) == 1 else jnp.concatenate(got, axis=0))
    normal = smooth.reshape(blocks, BLK, width)

    def deliver(chunk, take, got, mine, after):
        nonlocal normal
        normal, token = finish(me, take, send_order, got, mine, normal, after, groups[chunk])
        return token

    line_sums(chunks, "rows", deliver)
    return (data_image, normal.reshape(cell_count, width))


def solution(mesh):
    placed = (
        P("cols", None),
        P("rows", "cols", None, None),
        P("rows", "cols"),
        P("rows", "cols"),
        P("rows", "cols"),
        P("cols", None),
        P(None, "cols"),
        P(None, "cols"),
    )
    return jax.shard_map(
        local,
        mesh=mesh,
        in_specs=placed,
        out_specs=(P("rows", None), P("cols", None)),
        check_vma=False,
    )
```

```python
import math

import jax
import jax.numpy as jnp
import numpy as np
from jax import lax
from jax.experimental import pallas as pl
from jax.experimental.pallas import tpu as pltpu
from jax.sharding import PartitionSpec as P

BLK = 128
RB_DEV = 32
RIM = 64
STEP = 16
MIB = 1 << 20
SMALL = 16 * MIB
LARGE = 56 * MIB
ANY_SPEC = pl.BlockSpec(memory_space=pl.ANY)
VMEM_SPEC = pl.BlockSpec(memory_space=pltpu.VMEM)
SMEM_SPEC = pl.BlockSpec(memory_space=pltpu.SMEM)


def haar_matrix(order_n):
    matrix = np.ones((1, 1))
    while matrix.shape[0] < order_n:
        length = matrix.shape[0]
        upper = np.kron(matrix, np.array([[1.0, 1.0]]))
        lower = np.kron(np.eye(length), np.array([[1.0, -1.0]]))
        matrix = np.concatenate([upper, lower], axis=0) / math.sqrt(2.0)
    return matrix


def fetch(source, target, sems, pieces):
    each = source.shape[0] // pieces
    parts = [pl.ds(i * each, each) for i in range(pieces)]
    return [
        pltpu.make_async_copy(source.at[part], target.at[part], sems.at[i])
        for i, part in enumerate(parts)
    ]


def gather_pieces(sources, held_ref, me, sems):
    each = held_ref.shape[0] // len(sources)
    return [
        pltpu.make_async_copy(
            ref.at[pl.ds(first * each, each)],
            held_ref.at[pl.ds((me ^ offset) * each, each)],
            sems.at[offset],
        )
        for offset, (ref, first) in enumerate(sources)
    ]


def piece_stores(source, offset, even_refs, odd_ref, sems):
    each = odd_ref.shape[0] // (sems.shape[0] // 2)
    if offset % 2:
        target = odd_ref.at[pl.ds((offset // 2) * each, each)]
    else:
        target = even_refs[offset // 2]
    return pltpu.make_async_copy(source, target, sems.at[offset])


def start_all(copies):
    for copy in copies:
        copy.start()


def wait_all(copies):
    for copy in copies:
        copy.wait()


def analyze_body(me_ref, order_ref, model_ref, *refs):
    even_refs, (odd_ref, block_ref, coeff_ref, got, put) = refs[:-5], refs[-5:]
    width = model_ref.shape[2]
    per_peer = even_refs[0].shape[0]
    peers = put.shape[0]
    me = me_ref[0]
    loads = fetch(model_ref, block_ref, got, got.shape[0])
    start_all(loads)
    row = lax.broadcasted_iota(jnp.int32, (BLK, BLK), 0)
    col = lax.broadcasted_iota(jnp.int32, (BLK, BLK), 1)
    level = jnp.ones_like(row)
    scale = jnp.full((BLK, width), BLK**-0.5, jnp.float32)
    wide_row = lax.broadcasted_iota(jnp.int32, (BLK, width), 0)
    size = 2
    while size < BLK:
        level = jnp.where(row >= size, size, level)
        scale = jnp.where(wide_row >= size, (size / BLK) ** 0.5, scale)
        size *= 2
    span = BLK // level
    inside = col - (row - level) * span
    sign = jnp.where(inside * 2 < span, 1.0, -1.0)
    sign = jnp.where((inside >= 0) & (inside < span), sign, 0.0)
    sign = jnp.where(row == 0, 1.0, sign).astype(jnp.bfloat16)
    both_signs = jnp.concatenate([sign, sign], axis=1)
    wait_all(loads)
    stores = []
    for offset in [*range(1, peers, 2), *range(peers - 2, -1, -2)]:
        peer = (me ^ offset) * per_peer
        for q in range(per_peer):
            x = block_ref[order_ref[0, peer + q]]
            high = x.astype(jnp.bfloat16)
            low = (x - high.astype(jnp.float32)).astype(jnp.bfloat16)
            raw = jnp.dot(
                both_signs, jnp.concatenate([high, low], axis=0),
                preferred_element_type=jnp.float32,
            )
            coeff_ref[offset, q] = (raw * scale).astype(jnp.bfloat16)
        stores.append(piece_stores(coeff_ref.at[offset], offset, even_refs, odd_ref, put))
        stores[-1].start()
    wait_all(stores)


def piece_shapes(piece, peers, dtype):
    half = peers // 2
    return [jax.ShapeDtypeStruct(piece, dtype)] * half + [
        jax.ShapeDtypeStruct((half * piece[0], *piece[1:]), dtype)
    ]


def analyze(me, order, model_blocks, peers):
    blocks, _, width = model_blocks.shape
    piece = (blocks // peers, BLK, width)
    return pl.pallas_call(
        analyze_body,
        out_shape=piece_shapes(piece, peers, jnp.bfloat16),
        in_specs=[SMEM_SPEC, SMEM_SPEC, ANY_SPEC],
        out_specs=[ANY_SPEC] * (peers // 2 + 1),
        scratch_shapes=[
            pltpu.VMEM((blocks, BLK, width), jnp.float32),
            pltpu.VMEM((peers, *piece), jnp.bfloat16),
            pltpu.SemaphoreType.DMA((16,)),
            pltpu.SemaphoreType.DMA((peers,)),
        ],
        compiler_params=pltpu.CompilerParams(vmem_limit_bytes=LARGE),
        cost_estimate=pl.CostEstimate(
            flops=4 * blocks * BLK * BLK * width, bytes_accessed=6 * blocks * BLK * width,
            transcendentals=0,
        ),
        name="analyze",
    )(me, order, model_blocks)


def slot_loop(count, sens_ref, block_ref, sems, others, work):
    steps = sems.shape[0]
    each = sens_ref.shape[0] // steps

    def block_copy(step):
        part = pl.ds(step * each, each)
        return pltpu.make_async_copy(sens_ref.at[part], block_ref.at[part], sems.at[step])

    start_all(others)
    needed = (count + each - 1) // each

    @pl.loop(0, needed)
    def _(step):
        block_copy(step).start()

    wait_all(others)

    @pl.loop(0, needed)
    def _(step):
        block_copy(step).wait()
        for k in range(each):
            slot = step * each + k
            work(slot, block_ref[slot], slot < count)


def forward_body(me_ref, rows_ref, cols_ref, count_ref, sens_ref, *refs):
    peers = len(refs) - 9
    wave_refs, (even_ref, odd_ref) = refs[:peers], refs[peers + 1 : peers + 3]
    block_ref, held_ref, acc_ref, sems, got, put = refs[peers + 3 :]
    row_blocks = acc_ref.shape[0] - 1
    each = row_blocks // peers
    me = me_ref[0]
    acc_ref[...] = jnp.zeros_like(acc_ref)

    def work(slot, block, live):
        row = jnp.where(live, rows_ref[0, slot], row_blocks)
        acc_ref[row] += jnp.dot(
            block, held_ref[cols_ref[0, slot]], preferred_element_type=jnp.float32
        )

    waves = gather_pieces([(ref, 0) for ref in wave_refs], held_ref, me, got)
    slot_loop(count_ref[0, 0], sens_ref, block_ref, sems, waves, work)
    stores = []
    for offset in [*range(1, peers, 2), *range(0, peers, 2)]:
        target = odd_ref if offset % 2 else even_ref
        stores.append(
            pltpu.make_async_copy(
                acc_ref.at[pl.ds((me ^ offset) * each, each)],
                target.at[pl.ds((offset // 2) * each, each)],
                put.at[offset],
            )
        )
    start_all(stores)
    wait_all(stores)


def forward(me, rows, cols, count, sens, waves, after):
    slots = sens.shape[0]
    peers = len(waves)
    blocks, width = after[1], sens.shape[2]
    half = (RB_DEV // 2, BLK, width)
    return pl.pallas_call(
        forward_body,
        out_shape=[jax.ShapeDtypeStruct(half, jnp.float32)] * 2,
        in_specs=[SMEM_SPEC] * 4 + [ANY_SPEC] * (1 + peers + 1),
        out_specs=[ANY_SPEC] * 2,
        scratch_shapes=[
            pltpu.VMEM(sens.shape, sens.dtype),
            pltpu.VMEM((blocks, BLK, width), jnp.bfloat16),
            pltpu.VMEM((RB_DEV + 1, BLK, width), jnp.float32),
            pltpu.SemaphoreType.DMA((slots // STEP,)),
            pltpu.SemaphoreType.DMA((peers,)),
            pltpu.SemaphoreType.DMA((peers,)),
        ],
        compiler_params=pltpu.CompilerParams(vmem_limit_bytes=LARGE),
        cost_estimate=pl.CostEstimate(
            flops=2 * slots * BLK * BLK * width, bytes_accessed=2 * slots * BLK * BLK,
            transcendentals=0,
        ),
        name="forward",
    )(me, rows, cols, count, sens, *waves, after[0])


def adjoint_body(me_ref, rows_ref, cols_ref, count_ref, sens_ref, even_in_ref, odd_in_ref,
                 after_ref, *refs):
    even_refs, (odd_ref, image_ref) = refs[:-10], refs[-10:-8]
    block_ref, held_ref, acc_ref, half_ref, sems, got, put, whole = refs[-8:]
    peers = put.shape[0]
    col_blocks = acc_ref.shape[0] - 1
    each = col_blocks // peers
    me = me_ref[0]
    acc_ref[...] = jnp.zeros_like(acc_ref)

    def work(slot, block, live):
        col = jnp.where(live, cols_ref[0, slot], col_blocks)
        acc_ref[col] += lax.dot_general(
            block, held_ref[rows_ref[0, slot]], (((0,), (0,)), ((), ())),
            preferred_element_type=jnp.float32,
        )

    sources = [(odd_in_ref if o % 2 else even_in_ref, o // 2) for o in range(peers)]
    images = gather_pieces(sources, held_ref, me, got)
    slot_loop(count_ref[0, 0], sens_ref, block_ref, sems, images, work)
    stores = []
    for offset in [0, *range(1, peers, 2), *range(2, peers, 2)]:
        part = acc_ref[pl.ds((me ^ offset) * each, each)]
        half_ref[offset] = part.astype(half_ref.dtype)
        stores.append(piece_stores(half_ref.at[offset], offset, even_refs, odd_ref, put))
        stores[-1].start()
    stores.extend(fetch(held_ref, image_ref, whole, whole.shape[0]))
    start_all(stores[peers:])
    wait_all(stores)


def adjoint(me, rows, cols, count, sens, even, odd, after, blocks, peers):
    slots = sens.shape[0]
    width = even.shape[2]
    piece = (blocks // peers, BLK, width)
    image = (RB_DEV, BLK, width)
    outs = pl.pallas_call(
        adjoint_body,
        out_shape=piece_shapes(piece, peers, jnp.bfloat16)
        + [jax.ShapeDtypeStruct(image, jnp.bfloat16)],
        in_specs=[SMEM_SPEC] * 4 + [ANY_SPEC] * 4,
        out_specs=[ANY_SPEC] * (peers // 2 + 2),
        scratch_shapes=[
            pltpu.VMEM(sens.shape, sens.dtype),
            pltpu.VMEM(image, jnp.bfloat16),
            pltpu.VMEM((blocks + 1, BLK, width), jnp.float32),
            pltpu.VMEM((peers, *piece), jnp.bfloat16),
            pltpu.SemaphoreType.DMA((slots // STEP,)),
            pltpu.SemaphoreType.DMA((peers,)),
            pltpu.SemaphoreType.DMA((peers,)),
            pltpu.SemaphoreType.DMA((4,)),
        ],
        compiler_params=pltpu.CompilerParams(vmem_limit_bytes=LARGE),
        cost_estimate=pl.CostEstimate(
            flops=2 * slots * BLK * BLK * width, bytes_accessed=2 * slots * BLK * BLK,
            transcendentals=0,
        ),
        name="adjoint",
    )(me, rows, cols, count, sens, even, odd, after)
    return outs[:-2], outs[-2], outs[-1]


def join_body(own_ref, other_ref, after_ref, out_ref, *, place):
    each = own_ref.shape[0]
    out_ref[:each] = own_ref[...]
    out_ref[each:] = other_ref[place * each : (place + 1) * each]


def join(own, other, place, after):
    each = own.shape[0]
    return pl.pallas_call(
        lambda *refs: join_body(*refs, place=place),
        out_shape=jax.ShapeDtypeStruct((2 * each, *own.shape[1:]), own.dtype),
        in_specs=[VMEM_SPEC, VMEM_SPEC, ANY_SPEC],
        out_specs=VMEM_SPEC,
        compiler_params=pltpu.CompilerParams(vmem_limit_bytes=SMALL),
        cost_estimate=pl.CostEstimate(
            flops=0, bytes_accessed=8 * own.size, transcendentals=0
        ),
        name="join",
    )(own, other, after)


def tile_value(near, face, window):
    span = lax.broadcasted_iota(jnp.int32, (2 * BLK, BLK), 0)
    center = lax.broadcasted_iota(jnp.int32, (2 * BLK, BLK), 1) + RIM
    mix = jnp.where(span == center, jnp.sum(face, axis=0, keepdims=True), 0.0)
    for k in range(4):
        mix = mix - jnp.where(span == near[k : k + 1], face[k : k + 1], 0.0)
    mix_high = mix.astype(jnp.bfloat16)
    mix_low = (mix - mix_high.astype(jnp.float32)).astype(jnp.bfloat16)
    near_high = window.astype(jnp.bfloat16)
    near_low = (window - near_high.astype(jnp.float32)).astype(jnp.bfloat16)
    return lax.dot_general(
        jnp.concatenate([mix_high, mix_high, mix_low], axis=0),
        jnp.concatenate([near_high, near_low, near_high], axis=0),
        (((0,), (0,)), ((), ())), preferred_element_type=jnp.float32,
    )


def smooth_body(offset_ref, model_ref, near_ref, weight_ref, after_ref,
                out_ref, ext_ref, value_ref, got, put):
    cells, width = model_ref.shape
    steps = put.shape[0]
    tiles = cells // BLK // steps
    each = cells // got.shape[0]
    loads = [
        pltpu.make_async_copy(
            model_ref.at[pl.ds(i * each, each)], ext_ref.at[pl.ds(RIM + i * each, each)], got.at[i]
        )
        for i in range(got.shape[0])
    ]
    start_all(loads)
    ext_ref[:RIM] = jnp.zeros((RIM, width), jnp.float32)
    ext_ref[RIM + cells :] = jnp.zeros((RIM, width), jnp.float32)
    wait_all(loads)

    def store(step):
        part = pl.ds(step * tiles * BLK, tiles * BLK)
        return pltpu.make_async_copy(value_ref.at[part], out_ref.at[part], put.at[step])

    @pl.loop(0, steps)
    def _(step):
        for t in range(tiles):
            start = pl.multiple_of((step * tiles + t) * BLK, BLK)
            near = near_ref[:, pl.ds(start, BLK)] - (offset_ref[0] + start)
            face = weight_ref[:, pl.ds(start, BLK)]
            window = ext_ref[pl.ds(start, 2 * BLK), :]
            value_ref[pl.ds(start, BLK), :] = tile_value(near, face, window)
        store(step).start()

    for step in range(steps):
        store(step).wait()


def smoothing(offset, model, neighbors, face_weight, after):
    cells, width = model.shape
    return pl.pallas_call(
        smooth_body,
        out_shape=jax.ShapeDtypeStruct((cells, width), jnp.float32),
        in_specs=[SMEM_SPEC, ANY_SPEC, VMEM_SPEC, VMEM_SPEC, ANY_SPEC],
        out_specs=ANY_SPEC,
        scratch_shapes=[
            pltpu.VMEM((cells + 2 * RIM, width), jnp.float32),
            pltpu.VMEM((cells, width), jnp.float32),
            pltpu.SemaphoreType.DMA((16,)),
            pltpu.SemaphoreType.DMA((8,)),
        ],
        compiler_params=pltpu.CompilerParams(vmem_limit_bytes=LARGE),
        cost_estimate=pl.CostEstimate(
            flops=24 * cells * BLK * width, bytes_accessed=16 * cells * width, transcendentals=0
        ),
        name="smoothing",
    )(offset, model, neighbors, face_weight, after)


def edges_body(offset_ref, low_ref, model_ref, high_ref, near_ref, weight_ref, base_ref, after_ref,
               out_ref, window_ref, value_ref, got, put):
    cells = model_ref.shape[0]
    inner = 2 * BLK - RIM
    starts = (0, cells - BLK)
    loads = [
        pltpu.make_async_copy(low_ref, window_ref.at[0, pl.ds(0, RIM)], got.at[0]),
        pltpu.make_async_copy(
            model_ref.at[pl.ds(0, inner)], window_ref.at[0, pl.ds(RIM, inner)], got.at[1]
        ),
        pltpu.make_async_copy(
            model_ref.at[pl.ds(cells - inner, inner)], window_ref.at[1, pl.ds(0, inner)], got.at[2]
        ),
        pltpu.make_async_copy(high_ref, window_ref.at[1, pl.ds(inner, RIM)], got.at[3]),
    ]
    start_all(loads)
    wait_all(loads)
    stores = []
    for i, start in enumerate(starts):
        near = near_ref[:, start : start + BLK] - (offset_ref[0] + start)
        value_ref[i] = tile_value(near, weight_ref[:, start : start + BLK], window_ref[i])
        stores.append(
            pltpu.make_async_copy(value_ref.at[i], out_ref.at[pl.ds(start, BLK)], put.at[i])
        )
    start_all(stores)
    wait_all(stores)


def edges(offset, low, model, high, neighbors, face_weight, base, after):
    width = model.shape[1]
    return pl.pallas_call(
        edges_body,
        out_shape=jax.ShapeDtypeStruct(base.shape, base.dtype),
        in_specs=[SMEM_SPEC, ANY_SPEC, ANY_SPEC, ANY_SPEC, VMEM_SPEC, VMEM_SPEC, ANY_SPEC, ANY_SPEC],
        out_specs=ANY_SPEC,
        input_output_aliases={6: 0},
        scratch_shapes=[
            pltpu.VMEM((2, 2 * BLK, width), jnp.float32),
            pltpu.VMEM((2, BLK, width), jnp.float32),
            pltpu.SemaphoreType.DMA((4,)),
            pltpu.SemaphoreType.DMA((2,)),
        ],
        compiler_params=pltpu.CompilerParams(vmem_limit_bytes=SMALL),
        cost_estimate=pl.CostEstimate(
            flops=24 * 2 * BLK * BLK * width, bytes_accessed=32 * BLK * width, transcendentals=0
        ),
        name="edges",
    )(offset, low, model, high, neighbors, face_weight, base, after)


def finish_body(me_ref, take_ref, order_ref, basis_ref, got_ref, mine_ref, base_ref, after_ref,
                out_ref, token_ref, block_ref, value_ref, got, put, *, offsets):
    cols = got_ref.shape[0]
    per_peer = cols // len(offsets)
    fetches, stores = [], []
    for i in range(cols):
        offset = offsets[i // per_peer]
        cell = order_ref[0, (me_ref[0] ^ offset) * per_peer + i % per_peer]
        fetches.append(pltpu.make_async_copy(base_ref.at[cell], block_ref.at[i], got.at[i]))
        stores.append(pltpu.make_async_copy(block_ref.at[i], out_ref.at[cell], put.at[i]))
    start_all(fetches)
    for i in range(cols):
        wave = jnp.where(take_ref[0] > 0, got_ref[i], mine_ref[i])
        both = jnp.concatenate([wave, wave], axis=0)
        value_ref[i] = jnp.dot(basis_ref[...], both, preferred_element_type=jnp.float32)
    wait_all(fetches)
    block_ref[...] += value_ref[...]
    start_all(stores)
    token_ref[...] = jnp.zeros_like(token_ref)
    wait_all(stores)


def finish(me, take, order, got, mine, base, after, offsets):
    cols, _, width = got.shape
    basis = haar_matrix(BLK).T.astype(np.float32)
    high = basis.astype(jnp.bfloat16)
    low = (basis - high.astype(np.float32)).astype(jnp.bfloat16)
    basis2 = jnp.asarray(np.concatenate([high, low], axis=1))
    return pl.pallas_call(
        lambda *refs: finish_body(*refs, offsets=offsets),
        out_shape=[
            jax.ShapeDtypeStruct(base.shape, base.dtype),
            jax.ShapeDtypeStruct((8, BLK), jnp.float32),
        ],
        in_specs=[SMEM_SPEC] * 3 + [VMEM_SPEC] * 3 + [ANY_SPEC] * 2,
        out_specs=[ANY_SPEC, VMEM_SPEC],
        input_output_aliases={6: 0},
        scratch_shapes=[
            pltpu.VMEM((cols, BLK, width), jnp.float32),
            pltpu.VMEM((cols, BLK, width), jnp.float32),
            pltpu.SemaphoreType.DMA((cols,)),
            pltpu.SemaphoreType.DMA((cols,)),
        ],
        compiler_params=pltpu.CompilerParams(vmem_limit_bytes=SMALL),
        cost_estimate=pl.CostEstimate(
            flops=4 * cols * BLK * BLK * width, bytes_accessed=10 * cols * BLK * width,
            transcendentals=0,
        ),
        name="finish",
    )(me, take, order, basis2, got, mine, base, after)


def merge_body(got_ref, mine_ref, after_ref, out_ref):
    total = got_ref[...].astype(jnp.float32) + mine_ref[...].astype(jnp.float32)
    out_ref[...] = total.astype(out_ref.dtype)


def merge(got, mine, after):
    return pl.pallas_call(
        merge_body,
        out_shape=jax.ShapeDtypeStruct(mine.shape, mine.dtype),
        in_specs=[VMEM_SPEC, VMEM_SPEC, ANY_SPEC],
        out_specs=VMEM_SPEC,
        compiler_params=pltpu.CompilerParams(vmem_limit_bytes=SMALL),
        cost_estimate=pl.CostEstimate(
            flops=mine.size, bytes_accessed=6 * mine.size, transcendentals=0
        ),
        name="merge",
    )(got, mine, after)


def line_sums(count_parts, make, axis, deliver):
    count = lax.axis_size(axis)
    half = count // 2
    me = lax.axis_index(axis)
    stages = []
    for hop in range(half - 1):
        stages.append(([(hop, hop + 1), (count - 1 - hop, count - 2 - hop)], False))
    stages.append(([(half - 1, half), (half, half - 1)], False))
    for hop in range(half - 1):
        left, right = half - 1 - hop, half + hop
        stages.append(([(left, left - 1), (right, right + 1)], True))
    state, got = [], []

    def add_part(after):
        if len(state) < count_parts:
            state.append(make(len(state), after))
            got.append(lax.ppermute(state[-1], axis, stages[0][0]))

    for _ in range(3):
        add_part(None)
    after = state[0]
    for time in range(count_parts + len(stages) - 1):
        for s, (pairs, outwards) in enumerate(stages):
            k = time - s
            if not 0 <= k < count_parts:
                continue
            last = s + 1 == len(stages)
            if outwards:
                take = (me == pairs[0][1]) | (me == pairs[1][1])
                take = take.astype(jnp.int32).reshape(1)
                if last:
                    after = deliver(k, take, got[k], state[k], after)
                else:
                    state[k] = jnp.where(take[0] > 0, got[k], state[k])
            else:
                state[k] = after = merge(got[k], state[k], after)
                if last:
                    after = deliver(k, jnp.zeros((1,), jnp.int32), state[k], state[k], after)
            if not last:
                got[k] = lax.ppermute(state[k], axis, stages[s + 1][0])
            if s == 0:
                add_part(after)


def halo(block, axis, width):
    count = lax.axis_size(axis)
    forward_pairs = [(i, i + 1) for i in range(count - 1)]
    backward_pairs = [(target, source) for source, target in forward_pairs]
    low = lax.ppermute(block[block.shape[0] - width :], axis, forward_pairs)
    high = lax.ppermute(block[:width], axis, backward_pairs)
    return low, high


def swap(piece, axis, offset):
    return lax.ppermute(piece, axis, [(c, c ^ offset) for c in range(lax.axis_size(axis))])


def local(model_dir, sens_blocks, blk_row, blk_col, blk_count, send_order, neighbors, face_weight):
    cell_count, width = model_dir.shape
    blocks = cell_count // BLK
    peers = lax.axis_size("cols")
    half = peers // 2
    per_peer = blocks // peers
    col = lax.axis_index("cols").astype(jnp.int32)
    me = col.reshape(1)
    offset = (col * cell_count - RIM).reshape(1)
    sens = sens_blocks[0]
    evens = range(1, half)

    *own, odd = analyze(me, send_order, model_dir.reshape(blocks, BLK, width), peers)
    partner = swap(odd, "cols", 1)
    direct = {j: swap(own[j], "cols", 2 * j) for j in reversed(evens)}
    passed = {
        j: swap(partner[j * per_peer : (j + 1) * per_peer], "cols", 2 * j)
        for j in reversed(evens)
    }
    waves = [own[0], partner]
    for j in evens:
        waves += [direct[j], passed[j]]
    smooth = smoothing(offset, model_dir, neighbors, face_weight, partner)

    even_rows, odd_rows = forward(
        me, blk_row, blk_col, blk_count, sens, waves, (smooth, blocks)
    )
    pair = (even_rows + swap(odd_rows, "cols", 1)).reshape(half, -1, BLK, width)
    to_send = pair.astype(jnp.bfloat16)
    shares = [swap(to_send[j], "cols", 2 * j) for j in evens]
    total = pair[0] + sum(share.astype(jnp.float32) for share in shares)
    image_share = total.astype(jnp.bfloat16)
    even_image = jnp.concatenate(
        [image_share] + [swap(image_share, "cols", 2 * j) for j in evens], axis=0
    )
    odd_image = swap(even_image, "cols", 1)

    own, odd, image = adjoint(
        me, blk_row, blk_col, blk_count, sens, even_image, odd_image, smooth, blocks, peers
    )
    data_image = image.reshape(RB_DEV * BLK, width).astype(jnp.float32)
    partner = swap(odd, "cols", 1)
    groups = [[0], [1]] + [[2 * j, 2 * j + 1] for j in evens]

    def make(chunk, after):
        if chunk == 0:
            return own[0]
        if chunk == 1:
            return partner[:per_peer]
        j = chunk - 1
        both = join(own[j], partner, j, own[0] if after is None else after)
        return swap(both, "cols", 2 * j)

    model_late, _ = lax.optimization_barrier((model_dir, own[0]))
    low, high = halo(model_late, "cols", RIM)
    smooth = edges(offset, low, model_dir, high, neighbors, face_weight, smooth, own[0])
    normal = smooth.reshape(blocks, BLK, width)

    def deliver(chunk, take, got, mine, after):
        nonlocal normal
        normal, token = finish(me, take, send_order, got, mine, normal, after, groups[chunk])
        return token

    line_sums(len(groups), make, "rows", deliver)
    return (data_image, normal.reshape(cell_count, width))


def solution(mesh):
    placed = (
        P("cols", None),
        P("rows", "cols", None, None),
        P("rows", "cols"),
        P("rows", "cols"),
        P("rows", "cols"),
        P("cols", None),
        P(None, "cols"),
        P(None, "cols"),
    )
    return jax.shard_map(
        local,
        mesh=mesh,
        in_specs=placed,
        out_specs=(P("rows", None), P("cols", None)),
        check_vma=False,
    )
```

```python
import math

import jax
import jax.numpy as jnp
import numpy as np
from jax import lax
from jax.experimental import pallas as pl
from jax.experimental.pallas import tpu as pltpu
from jax.sharding import PartitionSpec as P

BLK = 128
RB_DEV = 32
RIM = 64
STEP = 16
MIB = 1 << 20
SMALL = 16 * MIB
LARGE = 56 * MIB
ANY_SPEC = pl.BlockSpec(memory_space=pl.ANY)
VMEM_SPEC = pl.BlockSpec(memory_space=pltpu.VMEM)
SMEM_SPEC = pl.BlockSpec(memory_space=pltpu.SMEM)


def haar_matrix(order_n):
    matrix = np.ones((1, 1))
    while matrix.shape[0] < order_n:
        length = matrix.shape[0]
        upper = np.kron(matrix, np.array([[1.0, 1.0]]))
        lower = np.kron(np.eye(length), np.array([[1.0, -1.0]]))
        matrix = np.concatenate([upper, lower], axis=0) / math.sqrt(2.0)
    return matrix


def fetch(source, target, sems, pieces):
    each = source.shape[0] // pieces
    parts = [pl.ds(i * each, each) for i in range(pieces)]
    return [
        pltpu.make_async_copy(source.at[part], target.at[part], sems.at[i])
        for i, part in enumerate(parts)
    ]


def gather_pieces(sources, held_ref, me, sems):
    each = held_ref.shape[0] // len(sources)
    return [
        pltpu.make_async_copy(
            ref.at[pl.ds(first * each, each)],
            held_ref.at[pl.ds((me ^ offset) * each, each)],
            sems.at[offset],
        )
        for offset, (ref, first) in enumerate(sources)
    ]


def piece_stores(source, offset, even_refs, odd_ref, sems):
    each = odd_ref.shape[0] // (sems.shape[0] // 2)
    if offset % 2:
        target = odd_ref.at[pl.ds((offset // 2) * each, each)]
    else:
        target = even_refs[offset // 2].at[pl.ds(0, each)]
    return pltpu.make_async_copy(source, target, sems.at[offset])


def start_all(copies):
    for copy in copies:
        copy.start()


def wait_all(copies):
    for copy in copies:
        copy.wait()


def analyze_body(me_ref, order_ref, model_ref, *refs):
    even_refs, (odd_ref, block_ref, coeff_ref, got, put) = refs[:-5], refs[-5:]
    width = model_ref.shape[2]
    per_peer = even_refs[0].shape[0]
    peers = put.shape[0]
    me = me_ref[0]
    loads = fetch(model_ref, block_ref, got, got.shape[0])
    start_all(loads)
    row = lax.broadcasted_iota(jnp.int32, (BLK, BLK), 0)
    col = lax.broadcasted_iota(jnp.int32, (BLK, BLK), 1)
    level = jnp.ones_like(row)
    scale = jnp.full((BLK, width), BLK**-0.5, jnp.float32)
    wide_row = lax.broadcasted_iota(jnp.int32, (BLK, width), 0)
    size = 2
    while size < BLK:
        level = jnp.where(row >= size, size, level)
        scale = jnp.where(wide_row >= size, (size / BLK) ** 0.5, scale)
        size *= 2
    span = BLK // level
    inside = col - (row - level) * span
    sign = jnp.where(inside * 2 < span, 1.0, -1.0)
    sign = jnp.where((inside >= 0) & (inside < span), sign, 0.0)
    sign = jnp.where(row == 0, 1.0, sign).astype(jnp.bfloat16)
    both_signs = jnp.concatenate([sign, sign], axis=1)
    wait_all(loads)
    stores = []
    for offset in [*range(1, peers, 2), *range(peers - 2, -1, -2)]:
        peer = (me ^ offset) * per_peer
        for q in range(per_peer):
            x = block_ref[order_ref[0, peer + q]]
            high = x.astype(jnp.bfloat16)
            low = (x - high.astype(jnp.float32)).astype(jnp.bfloat16)
            raw = jnp.dot(
                both_signs, jnp.concatenate([high, low], axis=0),
                preferred_element_type=jnp.float32,
            )
            coeff_ref[offset, q] = (raw * scale).astype(jnp.bfloat16)
        stores.append(piece_stores(coeff_ref.at[offset], offset, even_refs, odd_ref, put))
        stores[-1].start()
    wait_all(stores)


def piece_shapes(piece, peers, dtype):
    half = peers // 2
    return [jax.ShapeDtypeStruct(piece, dtype)] * half + [
        jax.ShapeDtypeStruct((half * piece[0], *piece[1:]), dtype)
    ]


def analyze(me, order, model_blocks, peers):
    blocks, _, width = model_blocks.shape
    piece = (blocks // peers, BLK, width)
    return pl.pallas_call(
        analyze_body,
        out_shape=piece_shapes(piece, peers, jnp.bfloat16),
        in_specs=[SMEM_SPEC, SMEM_SPEC, ANY_SPEC],
        out_specs=[ANY_SPEC] * (peers // 2 + 1),
        scratch_shapes=[
            pltpu.VMEM((blocks, BLK, width), jnp.float32),
            pltpu.VMEM((peers, *piece), jnp.bfloat16),
            pltpu.SemaphoreType.DMA((16,)),
            pltpu.SemaphoreType.DMA((peers,)),
        ],
        compiler_params=pltpu.CompilerParams(vmem_limit_bytes=LARGE),
        cost_estimate=pl.CostEstimate(
            flops=4 * blocks * BLK * BLK * width, bytes_accessed=6 * blocks * BLK * width,
            transcendentals=0,
        ),
        name="analyze",
    )(me, order, model_blocks)


def slot_loop(count, sens_ref, block_ref, sems, others, acc_ref, work):
    steps = sems.shape[0]
    each = sens_ref.shape[0] // steps

    def block_copy(step):
        part = pl.ds(step * each, each)
        return pltpu.make_async_copy(sens_ref.at[part], block_ref.at[part], sems.at[step])

    start_all(others)
    needed = (count + each - 1) // each

    @pl.loop(0, needed)
    def _(step):
        block_copy(step).start()

    acc_ref[...] = jnp.zeros_like(acc_ref)
    wait_all(others)

    @pl.loop(0, needed)
    def _(step):
        block_copy(step).wait()
        for k in range(each):
            slot = step * each + k
            work(slot, block_ref[slot], slot < count)


def forward_body(me_ref, rows_ref, cols_ref, count_ref, sens_ref, *refs):
    peers = len(refs) - 9
    wave_refs, (even_ref, odd_ref) = refs[:peers], refs[peers + 1 : peers + 3]
    block_ref, held_ref, acc_ref, sems, got, put = refs[peers + 3 :]
    row_blocks = acc_ref.shape[0] - 1
    each = row_blocks // peers
    me = me_ref[0]
    def work(slot, block, live):
        row = jnp.where(live, rows_ref[0, slot], row_blocks)
        acc_ref[row] += jnp.dot(
            block, held_ref[cols_ref[0, slot]], preferred_element_type=jnp.float32
        )

    waves = gather_pieces([(ref, 0) for ref in wave_refs], held_ref, me, got)
    slot_loop(count_ref[0, 0], sens_ref, block_ref, sems, waves, acc_ref, work)
    stores = []
    for offset in [*range(1, peers, 2), *range(0, peers, 2)]:
        target = odd_ref if offset % 2 else even_ref
        stores.append(
            pltpu.make_async_copy(
                acc_ref.at[pl.ds((me ^ offset) * each, each)],
                target.at[pl.ds((offset // 2) * each, each)],
                put.at[offset],
            )
        )
    start_all(stores)
    wait_all(stores)


def forward(me, rows, cols, count, sens, waves, after):
    slots = sens.shape[0]
    peers = len(waves)
    blocks, width = after[1], sens.shape[2]
    half = (RB_DEV // 2, BLK, width)
    return pl.pallas_call(
        forward_body,
        out_shape=[jax.ShapeDtypeStruct(half, jnp.float32)] * 2,
        in_specs=[SMEM_SPEC] * 4 + [ANY_SPEC] * (1 + peers + 1),
        out_specs=[ANY_SPEC] * 2,
        scratch_shapes=[
            pltpu.VMEM(sens.shape, sens.dtype),
            pltpu.VMEM((blocks, BLK, width), jnp.bfloat16),
            pltpu.VMEM((RB_DEV + 1, BLK, width), jnp.float32),
            pltpu.SemaphoreType.DMA((slots // STEP,)),
            pltpu.SemaphoreType.DMA((peers,)),
            pltpu.SemaphoreType.DMA((peers,)),
        ],
        compiler_params=pltpu.CompilerParams(vmem_limit_bytes=LARGE),
        cost_estimate=pl.CostEstimate(
            flops=2 * slots * BLK * BLK * width, bytes_accessed=2 * slots * BLK * BLK,
            transcendentals=0,
        ),
        name="forward",
    )(me, rows, cols, count, sens, *waves, after[0])


def adjoint_body(me_ref, rows_ref, cols_ref, count_ref, sens_ref, even_in_ref, odd_in_ref,
                 after_ref, *refs):
    even_refs, (odd_ref, image_ref) = refs[:-10], refs[-10:-8]
    block_ref, held_ref, acc_ref, half_ref, sems, got, put, whole = refs[-8:]
    peers = put.shape[0]
    col_blocks = acc_ref.shape[0] - 1
    each = col_blocks // peers
    me = me_ref[0]
    def work(slot, block, live):
        col = jnp.where(live, cols_ref[0, slot], col_blocks)
        acc_ref[col] += lax.dot_general(
            block, held_ref[rows_ref[0, slot]], (((0,), (0,)), ((), ())),
            preferred_element_type=jnp.float32,
        )

    sources = [(odd_in_ref if o % 2 else even_in_ref, o // 2) for o in range(peers)]
    images = gather_pieces(sources, held_ref, me, got)
    slot_loop(count_ref[0, 0], sens_ref, block_ref, sems, images, acc_ref, work)
    stores = []
    for offset in [0, *range(1, peers, 2), *range(2, peers, 2)]:
        part = acc_ref[pl.ds((me ^ offset) * each, each)]
        half_ref[offset] = part.astype(half_ref.dtype)
        stores.append(piece_stores(half_ref.at[offset], offset, even_refs, odd_ref, put))
        stores[-1].start()
    stores.extend(fetch(held_ref, image_ref, whole, whole.shape[0]))
    start_all(stores[peers:])
    wait_all(stores)


def adjoint(me, rows, cols, count, sens, even, odd, after, blocks, peers):
    slots = sens.shape[0]
    width = even.shape[2]
    piece = (blocks // peers, BLK, width)
    image = (RB_DEV, BLK, width)
    outs = pl.pallas_call(
        adjoint_body,
        out_shape=[jax.ShapeDtypeStruct(piece, jnp.bfloat16)]
        + [jax.ShapeDtypeStruct((2 * piece[0], *piece[1:]), jnp.bfloat16)] * (peers // 2 - 1)
        + piece_shapes(piece, peers, jnp.bfloat16)[-1:]
        + [jax.ShapeDtypeStruct(image, jnp.bfloat16)],
        in_specs=[SMEM_SPEC] * 4 + [ANY_SPEC] * 4,
        out_specs=[ANY_SPEC] * (peers // 2 + 2),
        scratch_shapes=[
            pltpu.VMEM(sens.shape, sens.dtype),
            pltpu.VMEM(image, jnp.bfloat16),
            pltpu.VMEM((blocks + 1, BLK, width), jnp.float32),
            pltpu.VMEM((peers, *piece), jnp.bfloat16),
            pltpu.SemaphoreType.DMA((slots // STEP,)),
            pltpu.SemaphoreType.DMA((peers,)),
            pltpu.SemaphoreType.DMA((peers,)),
            pltpu.SemaphoreType.DMA((4,)),
        ],
        compiler_params=pltpu.CompilerParams(vmem_limit_bytes=LARGE),
        cost_estimate=pl.CostEstimate(
            flops=2 * slots * BLK * BLK * width, bytes_accessed=2 * slots * BLK * BLK,
            transcendentals=0,
        ),
        name="adjoint",
    )(me, rows, cols, count, sens, even, odd, after)
    return outs[:-2], outs[-2], outs[-1]


def join_body(*refs):
    count = (len(refs) - 3) // 2
    other_ref, out_refs, sems = refs[count], refs[count + 2 : -1], refs[-1]
    each = out_refs[0].shape[0] // 2
    copies = [
        pltpu.make_async_copy(
            other_ref.at[pl.ds((i + 1) * each, each)], out_ref.at[pl.ds(each, each)], sems.at[i]
        )
        for i, out_ref in enumerate(out_refs)
    ]
    start_all(copies)
    wait_all(copies)


def join(own, other, after):
    count = len(own)
    return pl.pallas_call(
        join_body,
        out_shape=[jax.ShapeDtypeStruct(x.shape, x.dtype) for x in own],
        in_specs=[ANY_SPEC] * (count + 2),
        out_specs=[ANY_SPEC] * count,
        input_output_aliases={i: i for i in range(count)},
        scratch_shapes=[pltpu.SemaphoreType.DMA((count,))],
        compiler_params=pltpu.CompilerParams(vmem_limit_bytes=SMALL),
        cost_estimate=pl.CostEstimate(
            flops=0, bytes_accessed=4 * other.size, transcendentals=0
        ),
        name="join",
    )(*own, other, after)


def tile_value(near, face, window):
    span = lax.broadcasted_iota(jnp.int32, (2 * BLK, BLK), 0)
    center = lax.broadcasted_iota(jnp.int32, (2 * BLK, BLK), 1) + RIM
    mix = jnp.where(span == center, jnp.sum(face, axis=0, keepdims=True), 0.0)
    for k in range(4):
        mix = mix - jnp.where(span == near[k : k + 1], face[k : k + 1], 0.0)
    mix_high = mix.astype(jnp.bfloat16)
    mix_low = (mix - mix_high.astype(jnp.float32)).astype(jnp.bfloat16)
    near_high = window.astype(jnp.bfloat16)
    near_low = (window - near_high.astype(jnp.float32)).astype(jnp.bfloat16)
    return lax.dot_general(
        jnp.concatenate([mix_high, mix_high, mix_low], axis=0),
        jnp.concatenate([near_high, near_low, near_high], axis=0),
        (((0,), (0,)), ((), ())), preferred_element_type=jnp.float32,
    )


def smooth_body(offset_ref, model_ref, near_ref, weight_ref, after_ref,
                out_ref, ext_ref, value_ref, got, put):
    cells, width = model_ref.shape
    steps = put.shape[0]
    tiles = cells // BLK // steps
    each = cells // got.shape[0]
    loads = [
        pltpu.make_async_copy(
            model_ref.at[pl.ds(i * each, each)], ext_ref.at[pl.ds(RIM + i * each, each)], got.at[i]
        )
        for i in range(got.shape[0])
    ]
    start_all(loads)
    ext_ref[:RIM] = jnp.zeros((RIM, width), jnp.float32)
    ext_ref[RIM + cells :] = jnp.zeros((RIM, width), jnp.float32)
    wait_all(loads)

    def store(step):
        part = pl.ds(step * tiles * BLK, tiles * BLK)
        return pltpu.make_async_copy(value_ref.at[part], out_ref.at[part], put.at[step])

    @pl.loop(0, steps)
    def _(step):
        for t in range(tiles):
            start = pl.multiple_of((step * tiles + t) * BLK, BLK)
            near = near_ref[:, pl.ds(start, BLK)] - (offset_ref[0] + start)
            face = weight_ref[:, pl.ds(start, BLK)]
            window = ext_ref[pl.ds(start, 2 * BLK), :]
            value_ref[pl.ds(start, BLK), :] = tile_value(near, face, window)
        store(step).start()

    for step in range(steps):
        store(step).wait()


def smoothing(offset, model, neighbors, face_weight, after):
    cells, width = model.shape
    return pl.pallas_call(
        smooth_body,
        out_shape=jax.ShapeDtypeStruct((cells, width), jnp.float32),
        in_specs=[SMEM_SPEC, ANY_SPEC, VMEM_SPEC, VMEM_SPEC, ANY_SPEC],
        out_specs=ANY_SPEC,
        scratch_shapes=[
            pltpu.VMEM((cells + 2 * RIM, width), jnp.float32),
            pltpu.VMEM((cells, width), jnp.float32),
            pltpu.SemaphoreType.DMA((16,)),
            pltpu.SemaphoreType.DMA((8,)),
        ],
        compiler_params=pltpu.CompilerParams(vmem_limit_bytes=LARGE),
        cost_estimate=pl.CostEstimate(
            flops=24 * cells * BLK * width, bytes_accessed=16 * cells * width, transcendentals=0
        ),
        name="smoothing",
    )(offset, model, neighbors, face_weight, after)


def edges_body(offset_ref, low_ref, model_ref, high_ref, near_ref, weight_ref, base_ref, after_ref,
               out_ref, window_ref, value_ref, got, put):
    cells = model_ref.shape[0]
    inner = 2 * BLK - RIM
    starts = (0, cells - BLK)
    loads = [
        pltpu.make_async_copy(low_ref, window_ref.at[0, pl.ds(0, RIM)], got.at[0]),
        pltpu.make_async_copy(
            model_ref.at[pl.ds(0, inner)], window_ref.at[0, pl.ds(RIM, inner)], got.at[1]
        ),
        pltpu.make_async_copy(
            model_ref.at[pl.ds(cells - inner, inner)], window_ref.at[1, pl.ds(0, inner)], got.at[2]
        ),
        pltpu.make_async_copy(high_ref, window_ref.at[1, pl.ds(inner, RIM)], got.at[3]),
    ]
    start_all(loads)
    wait_all(loads)
    stores = []
    for i, start in enumerate(starts):
        near = near_ref[:, start : start + BLK] - (offset_ref[0] + start)
        value_ref[i] = tile_value(near, weight_ref[:, start : start + BLK], window_ref[i])
        stores.append(
            pltpu.make_async_copy(value_ref.at[i], out_ref.at[pl.ds(start, BLK)], put.at[i])
        )
    start_all(stores)
    wait_all(stores)


def edges(offset, low, model, high, neighbors, face_weight, base, after):
    width = model.shape[1]
    return pl.pallas_call(
        edges_body,
        out_shape=jax.ShapeDtypeStruct(base.shape, base.dtype),
        in_specs=[SMEM_SPEC, ANY_SPEC, ANY_SPEC, ANY_SPEC, VMEM_SPEC, VMEM_SPEC, ANY_SPEC, ANY_SPEC],
        out_specs=ANY_SPEC,
        input_output_aliases={6: 0},
        scratch_shapes=[
            pltpu.VMEM((2, 2 * BLK, width), jnp.float32),
            pltpu.VMEM((2, BLK, width), jnp.float32),
            pltpu.SemaphoreType.DMA((4,)),
            pltpu.SemaphoreType.DMA((2,)),
        ],
        compiler_params=pltpu.CompilerParams(vmem_limit_bytes=SMALL),
        cost_estimate=pl.CostEstimate(
            flops=24 * 2 * BLK * BLK * width, bytes_accessed=32 * BLK * width, transcendentals=0
        ),
        name="edges",
    )(offset, low, model, high, neighbors, face_weight, base, after)


def finish_body(me_ref, take_ref, order_ref, basis_ref, got_ref, mine_ref, base_ref, after_ref,
                out_ref, token_ref, block_ref, value_ref, got, put, *, offsets):
    cols = got_ref.shape[0]
    per_peer = cols // len(offsets)
    fetches, stores = [], []
    for i in range(cols):
        offset = offsets[i // per_peer]
        cell = order_ref[0, (me_ref[0] ^ offset) * per_peer + i % per_peer]
        fetches.append(pltpu.make_async_copy(base_ref.at[cell], block_ref.at[i], got.at[i]))
        stores.append(pltpu.make_async_copy(block_ref.at[i], out_ref.at[cell], put.at[i]))
    start_all(fetches)
    for i in range(cols):
        wave = jnp.where(take_ref[0] > 0, got_ref[i], mine_ref[i])
        both = jnp.concatenate([wave, wave], axis=0)
        value_ref[i] = jnp.dot(basis_ref[...], both, preferred_element_type=jnp.float32)
    wait_all(fetches)
    block_ref[...] += value_ref[...]
    start_all(stores)
    token_ref[...] = jnp.zeros_like(token_ref)
    wait_all(stores)


def finish(me, take, order, got, mine, base, after, offsets):
    cols, _, width = got.shape
    basis = haar_matrix(BLK).T.astype(np.float32)
    high = basis.astype(jnp.bfloat16)
    low = (basis - high.astype(np.float32)).astype(jnp.bfloat16)
    basis2 = jnp.asarray(np.concatenate([high, low], axis=1))
    return pl.pallas_call(
        lambda *refs: finish_body(*refs, offsets=offsets),
        out_shape=[
            jax.ShapeDtypeStruct(base.shape, base.dtype),
            jax.ShapeDtypeStruct((8, BLK), jnp.float32),
        ],
        in_specs=[SMEM_SPEC] * 3 + [VMEM_SPEC] * 3 + [ANY_SPEC] * 2,
        out_specs=[ANY_SPEC, VMEM_SPEC],
        input_output_aliases={6: 0},
        scratch_shapes=[
            pltpu.VMEM((cols, BLK, width), jnp.float32),
            pltpu.VMEM((cols, BLK, width), jnp.float32),
            pltpu.SemaphoreType.DMA((cols,)),
            pltpu.SemaphoreType.DMA((cols,)),
        ],
        compiler_params=pltpu.CompilerParams(vmem_limit_bytes=SMALL),
        cost_estimate=pl.CostEstimate(
            flops=4 * cols * BLK * BLK * width, bytes_accessed=10 * cols * BLK * width,
            transcendentals=0,
        ),
        name="finish",
    )(me, take, order, basis2, got, mine, base, after)


def merge_body(got_ref, mine_ref, after_ref, out_ref):
    total = got_ref[...].astype(jnp.float32) + mine_ref[...].astype(jnp.float32)
    out_ref[...] = total.astype(out_ref.dtype)


def merge(got, mine, after):
    return pl.pallas_call(
        merge_body,
        out_shape=jax.ShapeDtypeStruct(mine.shape, mine.dtype),
        in_specs=[VMEM_SPEC, VMEM_SPEC, ANY_SPEC],
        out_specs=VMEM_SPEC,
        compiler_params=pltpu.CompilerParams(vmem_limit_bytes=SMALL),
        cost_estimate=pl.CostEstimate(
            flops=mine.size, bytes_accessed=6 * mine.size, transcendentals=0
        ),
        name="merge",
    )(got, mine, after)


def line_sums(count_parts, make, axis, deliver):
    count = lax.axis_size(axis)
    half = count // 2
    me = lax.axis_index(axis)
    stages = []
    for hop in range(half - 1):
        stages.append(([(hop, hop + 1), (count - 1 - hop, count - 2 - hop)], False))
    stages.append(([(half - 1, half), (half, half - 1)], False))
    for hop in range(half - 1):
        left, right = half - 1 - hop, half + hop
        stages.append(([(left, left - 1), (right, right + 1)], True))
    state = [make(k, None) for k in range(2)]
    got = [lax.ppermute(part, axis, stages[0][0]) for part in state]
    after = state[0]
    for time in range(count_parts + len(stages) - 1):
        for s, (pairs, outwards) in enumerate(stages):
            k = time - s
            if not 0 <= k < count_parts:
                continue
            last = s + 1 == len(stages)
            if outwards:
                take = (me == pairs[0][1]) | (me == pairs[1][1])
                take = take.astype(jnp.int32).reshape(1)
                if last:
                    after = deliver(k, take, got[k], state[k], after)
                else:
                    state[k] = jnp.where(take[0] > 0, got[k], state[k])
            else:
                state[k] = after = merge(got[k], state[k], after)
                if last:
                    after = deliver(k, jnp.zeros((1,), jnp.int32), state[k], state[k], after)
            if not last:
                got[k] = lax.ppermute(state[k], axis, stages[s + 1][0])
            if s == 0 and k == 0:
                for later in range(2, count_parts):
                    state.append(make(later, after))
                    got.append(lax.ppermute(state[-1], axis, stages[0][0]))


def halo(block, axis, width):
    count = lax.axis_size(axis)
    forward_pairs = [(i, i + 1) for i in range(count - 1)]
    backward_pairs = [(target, source) for source, target in forward_pairs]
    low = lax.ppermute(block[block.shape[0] - width :], axis, forward_pairs)
    high = lax.ppermute(block[:width], axis, backward_pairs)
    return low, high


def swap(piece, axis, offset):
    return lax.ppermute(piece, axis, [(c, c ^ offset) for c in range(lax.axis_size(axis))])


def local(model_dir, sens_blocks, blk_row, blk_col, blk_count, send_order, neighbors, face_weight):
    cell_count, width = model_dir.shape
    blocks = cell_count // BLK
    peers = lax.axis_size("cols")
    half = peers // 2
    per_peer = blocks // peers
    col = lax.axis_index("cols").astype(jnp.int32)
    me = col.reshape(1)
    offset = (col * cell_count - RIM).reshape(1)
    sens = sens_blocks[0]
    evens = range(1, half)

    *own, odd = analyze(me, send_order, model_dir.reshape(blocks, BLK, width), peers)
    partner = swap(odd, "cols", 1)
    direct = {j: swap(own[j], "cols", 2 * j) for j in reversed(evens)}
    passed = {
        j: swap(partner[j * per_peer : (j + 1) * per_peer], "cols", 2 * j)
        for j in reversed(evens)
    }
    waves = [own[0], partner]
    for j in evens:
        waves += [direct[j], passed[j]]
    smooth = smoothing(offset, model_dir, neighbors, face_weight, partner)

    even_rows, odd_rows = forward(
        me, blk_row, blk_col, blk_count, sens, waves, (smooth, blocks)
    )
    pair = (even_rows + swap(odd_rows, "cols", 1)).reshape(half, -1, BLK, width)
    to_send = pair.astype(jnp.bfloat16)
    shares = [swap(to_send[j], "cols", 2 * j) for j in evens]
    total = pair[0] + sum(share.astype(jnp.float32) for share in shares)
    image_share = total.astype(jnp.bfloat16)
    even_image = jnp.concatenate(
        [image_share] + [swap(image_share, "cols", 2 * j) for j in evens], axis=0
    )
    odd_image = swap(even_image, "cols", 1)
    model_late, _ = lax.optimization_barrier((model_dir, to_send))
    low, high = halo(model_late, "cols", RIM)
    smooth = edges(offset, low, model_dir, high, neighbors, face_weight, smooth, to_send)

    own, odd, image = adjoint(
        me, blk_row, blk_col, blk_count, sens, even_image, odd_image, smooth, blocks, peers
    )
    data_image = image.reshape(RB_DEV * BLK, width).astype(jnp.float32)
    partner = swap(odd, "cols", 1)
    groups = [[0], [1]] + [[2 * j, 2 * j + 1] for j in evens]

    joined = []

    def make(chunk, after):
        if chunk == 0:
            return own[0]
        if chunk == 1:
            return partner[:per_peer]
        if not joined:
            joined.extend(join(own[1:], partner, after))
        return swap(joined[chunk - 2], "cols", 2 * (chunk - 1))

    normal = smooth.reshape(blocks, BLK, width)

    def deliver(chunk, take, got, mine, after):
        nonlocal normal
        normal, token = finish(me, take, send_order, got, mine, normal, after, groups[chunk])
        return token

    line_sums(len(groups), make, "rows", deliver)
    return (data_image, normal.reshape(cell_count, width))


def solution(mesh):
    placed = (
        P("cols", None),
        P("rows", "cols", None, None),
        P("rows", "cols"),
        P("rows", "cols"),
        P("rows", "cols"),
        P("cols", None),
        P(None, "cols"),
        P(None, "cols"),
    )
    return jax.shard_map(
        local,
        mesh=mesh,
        in_specs=placed,
        out_specs=(P("rows", None), P("cols", None)),
        check_vma=False,
    )
```

```python
import math

import jax
import jax.numpy as jnp
import numpy as np
from jax import lax
from jax.experimental import pallas as pl
from jax.experimental.pallas import tpu as pltpu
from jax.sharding import PartitionSpec as P

BLK = 128
RB_DEV = 32
RIM = 64
STEP = 16
MIB = 1 << 20
SMALL = 16 * MIB
LARGE = 56 * MIB
ANY_SPEC = pl.BlockSpec(memory_space=pl.ANY)
VMEM_SPEC = pl.BlockSpec(memory_space=pltpu.VMEM)
SMEM_SPEC = pl.BlockSpec(memory_space=pltpu.SMEM)


def haar_matrix(order_n):
    matrix = np.ones((1, 1))
    while matrix.shape[0] < order_n:
        length = matrix.shape[0]
        upper = np.kron(matrix, np.array([[1.0, 1.0]]))
        lower = np.kron(np.eye(length), np.array([[1.0, -1.0]]))
        matrix = np.concatenate([upper, lower], axis=0) / math.sqrt(2.0)
    return matrix


def fetch(source, target, sems, pieces):
    each = source.shape[0] // pieces
    parts = [pl.ds(i * each, each) for i in range(pieces)]
    return [
        pltpu.make_async_copy(source.at[part], target.at[part], sems.at[i])
        for i, part in enumerate(parts)
    ]


def gather_pieces(sources, held_ref, me, sems):
    each = held_ref.shape[0] // len(sources)
    return [
        pltpu.make_async_copy(
            ref.at[pl.ds(first, each)],
            held_ref.at[pl.ds((me ^ offset) * each, each)],
            sems.at[offset],
        )
        for offset, (ref, first) in enumerate(sources)
    ]


def piece_stores(source, offset, even_refs, odd_ref, sems):
    each = source.shape[0]
    stride = odd_ref.shape[0] // (sems.shape[0] // 2)
    if offset % 2:
        target = odd_ref.at[pl.ds((offset // 2) * stride, each)]
    else:
        target = even_refs[offset // 2].at[pl.ds(0, each)]
    return pltpu.make_async_copy(source, target, sems.at[offset])


def start_all(copies):
    for copy in copies:
        copy.start()


def wait_all(copies):
    for copy in copies:
        copy.wait()


def analyze_body(me_ref, order_ref, model_ref, *refs):
    even_refs, (odd_ref, block_ref, coeff_ref, got, put) = refs[:-5], refs[-5:]
    width = model_ref.shape[2]
    per_peer = even_refs[0].shape[0]
    peers = put.shape[0]
    me = me_ref[0]
    loads = fetch(model_ref, block_ref, got, got.shape[0])
    start_all(loads)
    row = lax.broadcasted_iota(jnp.int32, (BLK, BLK), 0)
    col = lax.broadcasted_iota(jnp.int32, (BLK, BLK), 1)
    level = jnp.ones_like(row)
    scale = jnp.full((BLK, width), BLK**-0.5, jnp.float32)
    wide_row = lax.broadcasted_iota(jnp.int32, (BLK, width), 0)
    size = 2
    while size < BLK:
        level = jnp.where(row >= size, size, level)
        scale = jnp.where(wide_row >= size, (size / BLK) ** 0.5, scale)
        size *= 2
    span = BLK // level
    inside = col - (row - level) * span
    sign = jnp.where(inside * 2 < span, 1.0, -1.0)
    sign = jnp.where((inside >= 0) & (inside < span), sign, 0.0)
    sign = jnp.where(row == 0, 1.0, sign).astype(jnp.bfloat16)
    both_signs = jnp.concatenate([sign, sign], axis=1)
    wait_all(loads)
    stores = []
    ends = []
    for rows in (block_ref[model_ref.shape[0] - 1, BLK - RIM :], block_ref[0, :RIM]):
        high = rows.astype(jnp.bfloat16)
        low = (rows - high.astype(jnp.float32)).astype(jnp.bfloat16)
        ends.append(jnp.concatenate([high, low], axis=0))
    for offset in [*range(1, peers, 2), *range(peers - 2, -1, -2)]:
        peer = (me ^ offset) * per_peer
        for q in range(per_peer):
            x = block_ref[order_ref[0, peer + q]]
            high = x.astype(jnp.bfloat16)
            low = (x - high.astype(jnp.float32)).astype(jnp.bfloat16)
            raw = jnp.dot(
                both_signs, jnp.concatenate([high, low], axis=0),
                preferred_element_type=jnp.float32,
            )
            coeff_ref[offset, q] = (raw * scale).astype(jnp.bfloat16)
        length = per_peer
        if offset % 2:
            coeff_ref[offset, per_peer] = jnp.where(me ^ offset == me + 1, ends[0], ends[1])
            length += 1
        source = coeff_ref.at[offset, pl.ds(0, length)]
        stores.append(piece_stores(source, offset, even_refs, odd_ref, put))
        stores[-1].start()
    wait_all(stores)


def piece_shapes(piece, peers, dtype, more=0):
    half = peers // 2
    return [jax.ShapeDtypeStruct(piece, dtype)] * half + [
        jax.ShapeDtypeStruct((half * (piece[0] + more), *piece[1:]), dtype)
    ]


def analyze(me, order, model_blocks, peers):
    blocks, _, width = model_blocks.shape
    piece = (blocks // peers, BLK, width)
    return pl.pallas_call(
        analyze_body,
        out_shape=piece_shapes(piece, peers, jnp.bfloat16, 1),
        in_specs=[SMEM_SPEC, SMEM_SPEC, ANY_SPEC],
        out_specs=[ANY_SPEC] * (peers // 2 + 1),
        scratch_shapes=[
            pltpu.VMEM((blocks, BLK, width), jnp.float32),
            pltpu.VMEM((peers, piece[0] + 1, *piece[1:]), jnp.bfloat16),
            pltpu.SemaphoreType.DMA((16,)),
            pltpu.SemaphoreType.DMA((peers,)),
        ],
        compiler_params=pltpu.CompilerParams(vmem_limit_bytes=LARGE),
        cost_estimate=pl.CostEstimate(
            flops=4 * blocks * BLK * BLK * width, bytes_accessed=6 * blocks * BLK * width,
            transcendentals=0,
        ),
        name="analyze",
    )(me, order, model_blocks)


def slot_loop(count, sens_ref, block_ref, sems, others, acc_ref, work):
    steps = sems.shape[0]
    each = sens_ref.shape[0] // steps

    def block_copy(step):
        part = pl.ds(step * each, each)
        return pltpu.make_async_copy(sens_ref.at[part], block_ref.at[part], sems.at[step])

    start_all(others)
    needed = (count + each - 1) // each

    @pl.loop(0, needed)
    def _(step):
        block_copy(step).start()

    acc_ref[...] = jnp.zeros_like(acc_ref)
    wait_all(others)

    @pl.loop(0, needed)
    def _(step):
        block_copy(step).wait()
        for k in range(each):
            slot = step * each + k
            work(slot, block_ref[slot], slot < count)


def forward_body(me_ref, rows_ref, cols_ref, count_ref, sens_ref, *refs):
    peers = len(refs) - 9
    wave_refs, (even_ref, odd_ref) = refs[:peers], refs[peers + 1 : peers + 3]
    block_ref, held_ref, acc_ref, sems, got, put = refs[peers + 3 :]
    row_blocks = acc_ref.shape[0] - 1
    each = row_blocks // peers
    me = me_ref[0]
    def work(slot, block, live):
        row = jnp.where(live, rows_ref[0, slot], row_blocks)
        acc_ref[row] += jnp.dot(
            block, held_ref[cols_ref[0, slot]], preferred_element_type=jnp.float32
        )

    waves = gather_pieces([(ref, 0) for ref in wave_refs], held_ref, me, got)
    slot_loop(count_ref[0, 0], sens_ref, block_ref, sems, waves, acc_ref, work)
    stores = []
    for offset in [*range(1, peers, 2), *range(0, peers, 2)]:
        target = odd_ref if offset % 2 else even_ref
        stores.append(
            pltpu.make_async_copy(
                acc_ref.at[pl.ds((me ^ offset) * each, each)],
                target.at[pl.ds((offset // 2) * each, each)],
                put.at[offset],
            )
        )
    start_all(stores)
    wait_all(stores)


def forward(me, rows, cols, count, sens, waves, after):
    slots = sens.shape[0]
    peers = len(waves)
    blocks, width = after[1], sens.shape[2]
    half = (RB_DEV // 2, BLK, width)
    return pl.pallas_call(
        forward_body,
        out_shape=[jax.ShapeDtypeStruct(half, jnp.float32)] * 2,
        in_specs=[SMEM_SPEC] * 4 + [ANY_SPEC] * (1 + peers + 1),
        out_specs=[ANY_SPEC] * 2,
        scratch_shapes=[
            pltpu.VMEM(sens.shape, sens.dtype),
            pltpu.VMEM((blocks, BLK, width), jnp.bfloat16),
            pltpu.VMEM((RB_DEV + 1, BLK, width), jnp.float32),
            pltpu.SemaphoreType.DMA((slots // STEP,)),
            pltpu.SemaphoreType.DMA((peers,)),
            pltpu.SemaphoreType.DMA((peers,)),
        ],
        compiler_params=pltpu.CompilerParams(vmem_limit_bytes=LARGE),
        cost_estimate=pl.CostEstimate(
            flops=2 * slots * BLK * BLK * width, bytes_accessed=2 * slots * BLK * BLK,
            transcendentals=0,
        ),
        name="forward",
    )(me, rows, cols, count, sens, *waves, after[0])


def adjoint_body(me_ref, rows_ref, cols_ref, count_ref, sens_ref, even_in_ref, odd_in_ref,
                 after_ref, *refs):
    even_refs, (odd_ref, image_ref) = refs[:-10], refs[-10:-8]
    block_ref, held_ref, acc_ref, half_ref, sems, got, put, whole = refs[-8:]
    peers = put.shape[0]
    col_blocks = acc_ref.shape[0] - 1
    each = col_blocks // peers
    me = me_ref[0]
    def work(slot, block, live):
        col = jnp.where(live, cols_ref[0, slot], col_blocks)
        acc_ref[col] += lax.dot_general(
            block, held_ref[rows_ref[0, slot]], (((0,), (0,)), ((), ())),
            preferred_element_type=jnp.float32,
        )

    each_in = held_ref.shape[0] // peers
    sources = [
        (odd_in_ref if o % 2 else even_in_ref, o // 2 * each_in) for o in range(peers)
    ]
    images = gather_pieces(sources, held_ref, me, got)
    slot_loop(count_ref[0, 0], sens_ref, block_ref, sems, images, acc_ref, work)
    stores = []
    for offset in [0, *range(1, peers, 2), *range(2, peers, 2)]:
        part = acc_ref[pl.ds((me ^ offset) * each, each)]
        half_ref[offset] = part.astype(half_ref.dtype)
        stores.append(piece_stores(half_ref.at[offset], offset, even_refs, odd_ref, put))
        stores[-1].start()
    stores.extend(fetch(held_ref, image_ref, whole, whole.shape[0]))
    start_all(stores[peers:])
    wait_all(stores)


def adjoint(me, rows, cols, count, sens, even, odd, after, blocks, peers):
    slots = sens.shape[0]
    width = even.shape[2]
    piece = (blocks // peers, BLK, width)
    image = (RB_DEV, BLK, width)
    outs = pl.pallas_call(
        adjoint_body,
        out_shape=[jax.ShapeDtypeStruct(piece, jnp.bfloat16)]
        + [jax.ShapeDtypeStruct((2 * piece[0], *piece[1:]), jnp.bfloat16)] * (peers // 2 - 1)
        + piece_shapes(piece, peers, jnp.bfloat16)[-1:]
        + [jax.ShapeDtypeStruct(image, jnp.bfloat16)],
        in_specs=[SMEM_SPEC] * 4 + [ANY_SPEC] * 4,
        out_specs=[ANY_SPEC] * (peers // 2 + 2),
        scratch_shapes=[
            pltpu.VMEM(sens.shape, sens.dtype),
            pltpu.VMEM(image, jnp.bfloat16),
            pltpu.VMEM((blocks + 1, BLK, width), jnp.float32),
            pltpu.VMEM((peers, *piece), jnp.bfloat16),
            pltpu.SemaphoreType.DMA((slots // STEP,)),
            pltpu.SemaphoreType.DMA((peers,)),
            pltpu.SemaphoreType.DMA((peers,)),
            pltpu.SemaphoreType.DMA((4,)),
        ],
        compiler_params=pltpu.CompilerParams(vmem_limit_bytes=LARGE),
        cost_estimate=pl.CostEstimate(
            flops=2 * slots * BLK * BLK * width, bytes_accessed=2 * slots * BLK * BLK,
            transcendentals=0,
        ),
        name="adjoint",
    )(me, rows, cols, count, sens, even, odd, after)
    return outs[:-2], outs[-2], outs[-1]


def join_body(*refs):
    count = (len(refs) - 3) // 2
    other_ref, out_refs, sems = refs[count], refs[count + 2 : -1], refs[-1]
    each = out_refs[0].shape[0] // 2
    copies = [
        pltpu.make_async_copy(
            other_ref.at[pl.ds((i + 1) * each, each)], out_ref.at[pl.ds(each, each)], sems.at[i]
        )
        for i, out_ref in enumerate(out_refs)
    ]
    start_all(copies)
    wait_all(copies)


def join(own, other, after):
    count = len(own)
    return pl.pallas_call(
        join_body,
        out_shape=[jax.ShapeDtypeStruct(x.shape, x.dtype) for x in own],
        in_specs=[ANY_SPEC] * (count + 2),
        out_specs=[ANY_SPEC] * count,
        input_output_aliases={i: i for i in range(count)},
        scratch_shapes=[pltpu.SemaphoreType.DMA((count,))],
        compiler_params=pltpu.CompilerParams(vmem_limit_bytes=LARGE),
        cost_estimate=pl.CostEstimate(
            flops=0, bytes_accessed=4 * other.size, transcendentals=0
        ),
        name="join",
    )(*own, other, after)


def tile_value(near, face, window):
    span = lax.broadcasted_iota(jnp.int32, (2 * BLK, BLK), 0)
    center = lax.broadcasted_iota(jnp.int32, (2 * BLK, BLK), 1) + RIM
    mix = jnp.where(span == center, jnp.sum(face, axis=0, keepdims=True), 0.0)
    for k in range(4):
        mix = mix - jnp.where(span == near[k : k + 1], face[k : k + 1], 0.0)
    mix_high = mix.astype(jnp.bfloat16)
    mix_low = (mix - mix_high.astype(jnp.float32)).astype(jnp.bfloat16)
    near_high = window.astype(jnp.bfloat16)
    near_low = (window - near_high.astype(jnp.float32)).astype(jnp.bfloat16)
    return lax.dot_general(
        jnp.concatenate([mix_high, mix_high, mix_low], axis=0),
        jnp.concatenate([near_high, near_low, near_high], axis=0),
        (((0,), (0,)), ((), ())), preferred_element_type=jnp.float32,
    )


def smooth_body(offset_ref, model_ref, near_ref, weight_ref, after_ref,
                out_ref, ext_ref, value_ref, got, put):
    cells, width = model_ref.shape
    steps = put.shape[0]
    tiles = cells // BLK // steps
    each = cells // got.shape[0]
    loads = [
        pltpu.make_async_copy(
            model_ref.at[pl.ds(i * each, each)], ext_ref.at[pl.ds(RIM + i * each, each)], got.at[i]
        )
        for i in range(got.shape[0])
    ]
    start_all(loads)
    ext_ref[:RIM] = jnp.zeros((RIM, width), jnp.float32)
    ext_ref[RIM + cells :] = jnp.zeros((RIM, width), jnp.float32)
    wait_all(loads)

    def store(step):
        part = pl.ds(step * tiles * BLK, tiles * BLK)
        return pltpu.make_async_copy(value_ref.at[part], out_ref.at[part], put.at[step])

    @pl.loop(0, steps)
    def _(step):
        for t in range(tiles):
            start = pl.multiple_of((step * tiles + t) * BLK, BLK)
            near = near_ref[:, pl.ds(start, BLK)] - (offset_ref[0] + start)
            face = weight_ref[:, pl.ds(start, BLK)]
            window = ext_ref[pl.ds(start, 2 * BLK), :]
            value_ref[pl.ds(start, BLK), :] = tile_value(near, face, window)
        store(step).start()

    for step in range(steps):
        store(step).wait()


def smoothing(offset, model, neighbors, face_weight, after):
    cells, width = model.shape
    return pl.pallas_call(
        smooth_body,
        out_shape=jax.ShapeDtypeStruct((cells, width), jnp.float32),
        in_specs=[SMEM_SPEC, ANY_SPEC, VMEM_SPEC, VMEM_SPEC, ANY_SPEC],
        out_specs=ANY_SPEC,
        scratch_shapes=[
            pltpu.VMEM((cells + 2 * RIM, width), jnp.float32),
            pltpu.VMEM((cells, width), jnp.float32),
            pltpu.SemaphoreType.DMA((16,)),
            pltpu.SemaphoreType.DMA((8,)),
        ],
        compiler_params=pltpu.CompilerParams(vmem_limit_bytes=LARGE),
        cost_estimate=pl.CostEstimate(
            flops=24 * cells * BLK * width, bytes_accessed=16 * cells * width, transcendentals=0
        ),
        name="smoothing",
    )(offset, model, neighbors, face_weight, after)


def edges_body(me_ref, offset_ref, model_ref, near_ref, weight_ref, base_ref, after_ref, *refs):
    odd_refs, refs = refs[:-6], refs[-6:]
    out_ref, window_ref, value_ref, ends_ref, got, put = refs
    cells = model_ref.shape[0]
    each = odd_refs[-1].shape[0] - 1
    inner = 2 * BLK - RIM
    starts = (0, cells - BLK)
    me = me_ref[0]
    loads = [
        pltpu.make_async_copy(
            model_ref.at[pl.ds(0, inner)], window_ref.at[0, pl.ds(RIM, inner)], got.at[0]
        ),
        pltpu.make_async_copy(
            model_ref.at[pl.ds(cells - inner, inner)], window_ref.at[1, pl.ds(0, inner)], got.at[1]
        ),
    ]
    for i, odd_ref in enumerate(odd_refs):
        loads.append(
            pltpu.make_async_copy(odd_ref.at[each], ends_ref.at[i], got.at[2 + i])
        )
    start_all(loads)
    wait_all(loads)
    zero = jnp.zeros((RIM, model_ref.shape[1]), jnp.float32)
    low, high = zero, zero
    for i in range(len(odd_refs)):
        rows = ends_ref[i, :RIM].astype(jnp.float32) + ends_ref[i, RIM:].astype(jnp.float32)
        peer = me ^ (2 * i + 1)
        low = jnp.where(peer == me - 1, rows, low)
        high = jnp.where(peer == me + 1, rows, high)
    window_ref[0, :RIM] = low
    window_ref[1, inner:] = high
    stores = []
    for i, start in enumerate(starts):
        near = near_ref[:, start : start + BLK] - (offset_ref[0] + start)
        value_ref[i] = tile_value(near, weight_ref[:, start : start + BLK], window_ref[i])
        stores.append(
            pltpu.make_async_copy(value_ref.at[i], out_ref.at[pl.ds(start, BLK)], put.at[i])
        )
    start_all(stores)
    wait_all(stores)


def edges(me, offset, model, neighbors, face_weight, base, after, odd_pieces):
    width = model.shape[1]
    count = len(odd_pieces)
    return pl.pallas_call(
        edges_body,
        out_shape=jax.ShapeDtypeStruct(base.shape, base.dtype),
        in_specs=[SMEM_SPEC, SMEM_SPEC, ANY_SPEC, VMEM_SPEC, VMEM_SPEC]
        + [ANY_SPEC] * (2 + count),
        out_specs=ANY_SPEC,
        input_output_aliases={5: 0},
        scratch_shapes=[
            pltpu.VMEM((2, 2 * BLK, width), jnp.float32),
            pltpu.VMEM((2, BLK, width), jnp.float32),
            pltpu.VMEM((count, BLK, width), jnp.bfloat16),
            pltpu.SemaphoreType.DMA((2 + count,)),
            pltpu.SemaphoreType.DMA((2,)),
        ],
        compiler_params=pltpu.CompilerParams(vmem_limit_bytes=LARGE),
        cost_estimate=pl.CostEstimate(
            flops=24 * 2 * BLK * BLK * width, bytes_accessed=32 * BLK * width, transcendentals=0
        ),
        name="edges",
    )(me, offset, model, neighbors, face_weight, base, after, *odd_pieces)


def finish_body(me_ref, take_ref, order_ref, basis_ref, got_ref, mine_ref, base_ref, after_ref,
                out_ref, token_ref, block_ref, value_ref, got, put, *, offsets):
    cols = got_ref.shape[0]
    per_peer = cols // len(offsets)
    fetches, stores = [], []
    for i in range(cols):
        offset = offsets[i // per_peer]
        cell = order_ref[0, (me_ref[0] ^ offset) * per_peer + i % per_peer]
        fetches.append(pltpu.make_async_copy(base_ref.at[cell], block_ref.at[i], got.at[i]))
        stores.append(pltpu.make_async_copy(block_ref.at[i], out_ref.at[cell], put.at[i]))
    start_all(fetches)
    for i in range(cols):
        wave = jnp.where(take_ref[0] > 0, got_ref[i], mine_ref[i])
        both = jnp.concatenate([wave, wave], axis=0)
        value_ref[i] = jnp.dot(basis_ref[...], both, preferred_element_type=jnp.float32)
    wait_all(fetches)
    block_ref[...] += value_ref[...]
    start_all(stores)
    token_ref[...] = jnp.zeros_like(token_ref)
    wait_all(stores)


def finish(me, take, order, got, mine, base, after, offsets):
    cols, _, width = got.shape
    basis = haar_matrix(BLK).T.astype(np.float32)
    high = basis.astype(jnp.bfloat16)
    low = (basis - high.astype(np.float32)).astype(jnp.bfloat16)
    basis2 = jnp.asarray(np.concatenate([high, low], axis=1))
    return pl.pallas_call(
        lambda *refs: finish_body(*refs, offsets=offsets),
        out_shape=[
            jax.ShapeDtypeStruct(base.shape, base.dtype),
            jax.ShapeDtypeStruct((8, BLK), jnp.float32),
        ],
        in_specs=[SMEM_SPEC] * 3 + [VMEM_SPEC] * 3 + [ANY_SPEC] * 2,
        out_specs=[ANY_SPEC, VMEM_SPEC],
        input_output_aliases={6: 0},
        scratch_shapes=[
            pltpu.VMEM((cols, BLK, width), jnp.float32),
            pltpu.VMEM((cols, BLK, width), jnp.float32),
            pltpu.SemaphoreType.DMA((cols,)),
            pltpu.SemaphoreType.DMA((cols,)),
        ],
        compiler_params=pltpu.CompilerParams(vmem_limit_bytes=SMALL),
        cost_estimate=pl.CostEstimate(
            flops=4 * cols * BLK * BLK * width, bytes_accessed=10 * cols * BLK * width,
            transcendentals=0,
        ),
        name="finish",
    )(me, take, order, basis2, got, mine, base, after)


def merge_body(got_ref, mine_ref, after_ref, out_ref):
    total = got_ref[...].astype(jnp.float32) + mine_ref[...].astype(jnp.float32)
    out_ref[...] = total.astype(out_ref.dtype)


def merge(got, mine, after):
    return pl.pallas_call(
        merge_body,
        out_shape=jax.ShapeDtypeStruct(mine.shape, mine.dtype),
        in_specs=[VMEM_SPEC, VMEM_SPEC, ANY_SPEC],
        out_specs=VMEM_SPEC,
        compiler_params=pltpu.CompilerParams(vmem_limit_bytes=SMALL),
        cost_estimate=pl.CostEstimate(
            flops=mine.size, bytes_accessed=6 * mine.size, transcendentals=0
        ),
        name="merge",
    )(got, mine, after)


def line_sums(count_parts, make, axis, deliver):
    count = lax.axis_size(axis)
    half = count // 2
    me = lax.axis_index(axis)
    stages = []
    for hop in range(half - 1):
        stages.append(([(hop, hop + 1), (count - 1 - hop, count - 2 - hop)], False))
    stages.append(([(half - 1, half), (half, half - 1)], False))
    for hop in range(half - 1):
        left, right = half - 1 - hop, half + hop
        stages.append(([(left, left - 1), (right, right + 1)], True))
    state = [make(k) for k in range(count_parts)]
    got = [lax.ppermute(part, axis, stages[0][0]) for part in state]
    after = state[0]
    for time in range(count_parts + len(stages) - 1):
        for s, (pairs, outwards) in enumerate(stages):
            k = time - s
            if not 0 <= k < count_parts:
                continue
            last = s + 1 == len(stages)
            if outwards:
                take = (me == pairs[0][1]) | (me == pairs[1][1])
                take = take.astype(jnp.int32).reshape(1)
                if last:
                    after = deliver(k, take, got[k], state[k], after)
                else:
                    state[k] = jnp.where(take[0] > 0, got[k], state[k])
            else:
                state[k] = after = merge(got[k], state[k], after)
                if last:
                    after = deliver(k, jnp.zeros((1,), jnp.int32), state[k], state[k], after)
            if not last:
                got[k] = lax.ppermute(state[k], axis, stages[s + 1][0])


def swap(piece, axis, offset):
    return lax.ppermute(piece, axis, [(c, c ^ offset) for c in range(lax.axis_size(axis))])


def local(model_dir, sens_blocks, blk_row, blk_col, blk_count, send_order, neighbors, face_weight):
    cell_count, width = model_dir.shape
    blocks = cell_count // BLK
    peers = lax.axis_size("cols")
    half = peers // 2
    per_peer = blocks // peers
    col = lax.axis_index("cols").astype(jnp.int32)
    me = col.reshape(1)
    offset = (col * cell_count - RIM).reshape(1)
    sens = sens_blocks[0]
    evens = range(1, half)

    *own, odd = analyze(me, send_order, model_dir.reshape(blocks, BLK, width), peers)
    partner = swap(odd, "cols", 1)
    direct = {j: swap(own[j], "cols", 2 * j) for j in reversed(evens)}
    passed = {
        j: swap(partner[j * (per_peer + 1) : (j + 1) * (per_peer + 1)], "cols", 2 * j)
        for j in reversed(evens)
    }
    waves = [own[0], partner]
    for j in evens:
        waves += [direct[j], passed[j]]
    smooth = smoothing(offset, model_dir, neighbors, face_weight, partner)

    even_rows, odd_rows = forward(
        me, blk_row, blk_col, blk_count, sens, waves, (smooth, blocks)
    )
    pair = (even_rows + swap(odd_rows, "cols", 1)).reshape(half, -1, BLK, width)
    to_send = pair.astype(jnp.bfloat16)
    shares = [swap(to_send[j], "cols", 2 * j) for j in evens]
    total = pair[0] + sum(share.astype(jnp.float32) for share in shares)
    image_share = total.astype(jnp.bfloat16)
    even_image = jnp.concatenate(
        [image_share] + [swap(image_share, "cols", 2 * j) for j in evens], axis=0
    )
    odd_image = swap(even_image, "cols", 1)
    smooth = edges(
        me, offset, model_dir, neighbors, face_weight, smooth, to_send, waves[1::2]
    )

    own, odd, image = adjoint(
        me, blk_row, blk_col, blk_count, sens, even_image, odd_image, smooth, blocks, peers
    )
    data_image = image.reshape(RB_DEV * BLK, width).astype(jnp.float32)
    partner = swap(odd, "cols", 1)
    groups = [[0], [1]] + [[2 * j, 2 * j + 1] for j in evens]

    joined = []

    def make(chunk):
        if chunk == 0:
            return own[0]
        if chunk == 1:
            return partner[:per_peer]
        if not joined:
            joined.extend(join(own[1:], partner, own[0]))
        return swap(joined[chunk - 2], "cols", 2 * (chunk - 1))

    normal = smooth.reshape(blocks, BLK, width)

    def deliver(chunk, take, got, mine, after):
        nonlocal normal
        normal, token = finish(me, take, send_order, got, mine, normal, after, groups[chunk])
        return token

    line_sums(len(groups), make, "rows", deliver)
    return (data_image, normal.reshape(cell_count, width))


def solution(mesh):
    placed = (
        P("cols", None),
        P("rows", "cols", None, None),
        P("rows", "cols"),
        P("rows", "cols"),
        P("rows", "cols"),
        P("cols", None),
        P(None, "cols"),
        P(None, "cols"),
    )
    return jax.shard_map(
        local,
        mesh=mesh,
        in_specs=placed,
        out_specs=(P("rows", None), P("cols", None)),
        check_vma=False,
    )
```

```python
import math

import jax
import jax.numpy as jnp
import numpy as np
from jax import lax
from jax.experimental import pallas as pl
from jax.experimental.pallas import tpu as pltpu
from jax.sharding import PartitionSpec as P

BLK = 128
RB_DEV = 32
RIM = 64
STEP = 16
MIB = 1 << 20
SMALL = 16 * MIB
LARGE = 56 * MIB
ANY_SPEC = pl.BlockSpec(memory_space=pl.ANY)
VMEM_SPEC = pl.BlockSpec(memory_space=pltpu.VMEM)
SMEM_SPEC = pl.BlockSpec(memory_space=pltpu.SMEM)


def haar_matrix(order_n):
    matrix = np.ones((1, 1))
    while matrix.shape[0] < order_n:
        length = matrix.shape[0]
        upper = np.kron(matrix, np.array([[1.0, 1.0]]))
        lower = np.kron(np.eye(length), np.array([[1.0, -1.0]]))
        matrix = np.concatenate([upper, lower], axis=0) / math.sqrt(2.0)
    return matrix


def fetch(source, target, sems, pieces):
    each = source.shape[0] // pieces
    parts = [pl.ds(i * each, each) for i in range(pieces)]
    return [
        pltpu.make_async_copy(source.at[part], target.at[part], sems.at[i])
        for i, part in enumerate(parts)
    ]


def gather_pieces(sources, held_ref, me, sems):
    each = held_ref.shape[0] // len(sources)
    return [
        pltpu.make_async_copy(
            ref.at[pl.ds(first, each)],
            held_ref.at[pl.ds((me ^ offset) * each, each)],
            sems.at[offset],
        )
        for offset, (ref, first) in enumerate(sources)
    ]


def piece_stores(source, offset, even_refs, odd_ref, sems):
    each = source.shape[0]
    stride = odd_ref.shape[0] // (sems.shape[0] // 2)
    if offset % 2:
        target = odd_ref.at[pl.ds((offset // 2) * stride, each)]
    else:
        target = even_refs[offset // 2].at[pl.ds(0, each)]
    return pltpu.make_async_copy(source, target, sems.at[offset])


def start_all(copies):
    for copy in copies:
        copy.start()


def wait_all(copies):
    for copy in copies:
        copy.wait()


def analyze_body(me_ref, order_ref, model_ref, *refs):
    even_refs, (odd_ref, block_ref, coeff_ref, got, put) = refs[:-5], refs[-5:]
    width = model_ref.shape[2]
    per_peer = even_refs[0].shape[0]
    peers = put.shape[0]
    me = me_ref[0]
    loads = fetch(model_ref, block_ref, got, got.shape[0])
    start_all(loads)
    row = lax.broadcasted_iota(jnp.int32, (BLK, BLK), 0)
    col = lax.broadcasted_iota(jnp.int32, (BLK, BLK), 1)
    level = jnp.ones_like(row)
    scale = jnp.full((BLK, width), BLK**-0.5, jnp.float32)
    wide_row = lax.broadcasted_iota(jnp.int32, (BLK, width), 0)
    size = 2
    while size < BLK:
        level = jnp.where(row >= size, size, level)
        scale = jnp.where(wide_row >= size, (size / BLK) ** 0.5, scale)
        size *= 2
    span = BLK // level
    inside = col - (row - level) * span
    sign = jnp.where(inside * 2 < span, 1.0, -1.0)
    sign = jnp.where((inside >= 0) & (inside < span), sign, 0.0)
    sign = jnp.where(row == 0, 1.0, sign).astype(jnp.bfloat16)
    both_signs = jnp.concatenate([sign, sign], axis=1)
    wait_all(loads)
    stores = []
    ends = []
    for rows in (block_ref[model_ref.shape[0] - 1, BLK - RIM :], block_ref[0, :RIM]):
        high = rows.astype(jnp.bfloat16)
        low = (rows - high.astype(jnp.float32)).astype(jnp.bfloat16)
        ends.append(jnp.concatenate([high, low], axis=0))
    for offset in [*range(1, peers, 2), *range(peers - 2, -1, -2)]:
        peer = (me ^ offset) * per_peer
        for q in range(per_peer):
            x = block_ref[order_ref[0, peer + q]]
            high = x.astype(jnp.bfloat16)
            low = (x - high.astype(jnp.float32)).astype(jnp.bfloat16)
            raw = jnp.dot(
                both_signs, jnp.concatenate([high, low], axis=0),
                preferred_element_type=jnp.float32,
            )
            coeff_ref[offset, q] = (raw * scale).astype(jnp.bfloat16)
        length = per_peer
        if offset % 2:
            coeff_ref[offset, per_peer] = jnp.where(me ^ offset == me + 1, ends[0], ends[1])
            length += 1
        source = coeff_ref.at[offset, pl.ds(0, length)]
        stores.append(piece_stores(source, offset, even_refs, odd_ref, put))
        stores[-1].start()
    wait_all(stores)


def piece_shapes(piece, peers, dtype, more=0):
    half = peers // 2
    return [jax.ShapeDtypeStruct(piece, dtype)] * half + [
        jax.ShapeDtypeStruct((half * (piece[0] + more), *piece[1:]), dtype)
    ]


def analyze(me, order, model_blocks, peers):
    blocks, _, width = model_blocks.shape
    piece = (blocks // peers, BLK, width)
    return pl.pallas_call(
        analyze_body,
        out_shape=piece_shapes(piece, peers, jnp.bfloat16, 1),
        in_specs=[SMEM_SPEC, SMEM_SPEC, ANY_SPEC],
        out_specs=[ANY_SPEC] * (peers // 2 + 1),
        scratch_shapes=[
            pltpu.VMEM((blocks, BLK, width), jnp.float32),
            pltpu.VMEM((peers, piece[0] + 1, *piece[1:]), jnp.bfloat16),
            pltpu.SemaphoreType.DMA((16,)),
            pltpu.SemaphoreType.DMA((peers,)),
        ],
        compiler_params=pltpu.CompilerParams(vmem_limit_bytes=LARGE),
        cost_estimate=pl.CostEstimate(
            flops=4 * blocks * BLK * BLK * width, bytes_accessed=6 * blocks * BLK * width,
            transcendentals=0,
        ),
        name="analyze",
    )(me, order, model_blocks)


def slot_loop(count, sens_ref, block_ref, sems, others, acc_ref, work):
    steps = sems.shape[0]
    each = sens_ref.shape[0] // steps

    def block_copy(step):
        part = pl.ds(step * each, each)
        return pltpu.make_async_copy(sens_ref.at[part], block_ref.at[part], sems.at[step])

    start_all(others)
    needed = (count + each - 1) // each

    @pl.loop(0, needed)
    def _(step):
        block_copy(step).start()

    acc_ref[...] = jnp.zeros_like(acc_ref)
    wait_all(others)

    @pl.loop(0, needed)
    def _(step):
        block_copy(step).wait()
        for k in range(each):
            slot = step * each + k
            work(slot, block_ref[slot], slot < count)


def forward_body(me_ref, rows_ref, cols_ref, count_ref, sens_ref, *refs):
    peers = len(refs) - 9
    wave_refs, (even_ref, odd_ref) = refs[:peers], refs[peers + 1 : peers + 3]
    block_ref, held_ref, acc_ref, sems, got, put = refs[peers + 3 :]
    row_blocks = acc_ref.shape[0] - 1
    each = row_blocks // peers
    me = me_ref[0]
    def work(slot, block, live):
        row = jnp.where(live, rows_ref[0, slot], row_blocks)
        acc_ref[row] += jnp.dot(
            block, held_ref[cols_ref[0, slot]], preferred_element_type=jnp.float32
        )

    waves = gather_pieces([(ref, 0) for ref in wave_refs], held_ref, me, got)
    slot_loop(count_ref[0, 0], sens_ref, block_ref, sems, waves, acc_ref, work)
    stores = []
    for offset in [*range(1, peers, 2), *range(0, peers, 2)]:
        target = odd_ref if offset % 2 else even_ref
        stores.append(
            pltpu.make_async_copy(
                acc_ref.at[pl.ds((me ^ offset) * each, each)],
                target.at[pl.ds((offset // 2) * each, each)],
                put.at[offset],
            )
        )
    start_all(stores)
    wait_all(stores)


def forward(me, rows, cols, count, sens, waves, after):
    slots = sens.shape[0]
    peers = len(waves)
    blocks, width = after[1], sens.shape[2]
    half = (RB_DEV // 2, BLK, width)
    return pl.pallas_call(
        forward_body,
        out_shape=[jax.ShapeDtypeStruct(half, jnp.float32)] * 2,
        in_specs=[SMEM_SPEC] * 4 + [ANY_SPEC] * (1 + peers + 1),
        out_specs=[ANY_SPEC] * 2,
        scratch_shapes=[
            pltpu.VMEM(sens.shape, sens.dtype),
            pltpu.VMEM((blocks, BLK, width), jnp.bfloat16),
            pltpu.VMEM((RB_DEV + 1, BLK, width), jnp.float32),
            pltpu.SemaphoreType.DMA((slots // STEP,)),
            pltpu.SemaphoreType.DMA((peers,)),
            pltpu.SemaphoreType.DMA((peers,)),
        ],
        compiler_params=pltpu.CompilerParams(vmem_limit_bytes=LARGE),
        cost_estimate=pl.CostEstimate(
            flops=2 * slots * BLK * BLK * width, bytes_accessed=2 * slots * BLK * BLK,
            transcendentals=0,
        ),
        name="forward",
    )(me, rows, cols, count, sens, *waves, after[0])


def adjoint_body(me_ref, rows_ref, cols_ref, count_ref, sens_ref, even_in_ref, odd_in_ref,
                 after_ref, *refs):
    out_refs, image_ref = refs[:-9], refs[-9]
    block_ref, held_ref, acc_ref, half_ref, sems, got, put, whole = refs[-8:]
    peers = put.shape[0]
    col_blocks = acc_ref.shape[0] - 1
    each = col_blocks // peers
    me = me_ref[0]
    def work(slot, block, live):
        col = jnp.where(live, cols_ref[0, slot], col_blocks)
        acc_ref[col] += lax.dot_general(
            block, held_ref[rows_ref[0, slot]], (((0,), (0,)), ((), ())),
            preferred_element_type=jnp.float32,
        )

    each_in = held_ref.shape[0] // peers
    sources = [
        (odd_in_ref if o % 2 else even_in_ref, o // 2 * each_in) for o in range(peers)
    ]
    images = gather_pieces(sources, held_ref, me, got)
    slot_loop(count_ref[0, 0], sens_ref, block_ref, sems, images, acc_ref, work)
    stores = []
    for offset in reversed(range(peers)):
        part = acc_ref[pl.ds((me ^ offset) * each, each)]
        half_ref[offset] = part.astype(half_ref.dtype)
        target = out_refs[offset // 2].at[pl.ds(offset % 2 * each, each)]
        stores.append(pltpu.make_async_copy(half_ref.at[offset], target, put.at[offset]))
        stores[-1].start()
    stores.extend(fetch(held_ref, image_ref, whole, whole.shape[0]))
    start_all(stores[peers:])
    wait_all(stores)


def adjoint(me, rows, cols, count, sens, even, odd, after, blocks, peers):
    slots = sens.shape[0]
    width = even.shape[2]
    piece = (blocks // peers, BLK, width)
    image = (RB_DEV, BLK, width)
    outs = pl.pallas_call(
        adjoint_body,
        out_shape=[jax.ShapeDtypeStruct((2 * piece[0], *piece[1:]), jnp.bfloat16)] * (peers // 2)
        + [jax.ShapeDtypeStruct(image, jnp.bfloat16)],
        in_specs=[SMEM_SPEC] * 4 + [ANY_SPEC] * 4,
        out_specs=[ANY_SPEC] * (peers // 2 + 1),
        scratch_shapes=[
            pltpu.VMEM(sens.shape, sens.dtype),
            pltpu.VMEM(image, jnp.bfloat16),
            pltpu.VMEM((blocks + 1, BLK, width), jnp.float32),
            pltpu.VMEM((peers, *piece), jnp.bfloat16),
            pltpu.SemaphoreType.DMA((slots // STEP,)),
            pltpu.SemaphoreType.DMA((peers,)),
            pltpu.SemaphoreType.DMA((peers,)),
            pltpu.SemaphoreType.DMA((4,)),
        ],
        compiler_params=pltpu.CompilerParams(vmem_limit_bytes=LARGE),
        cost_estimate=pl.CostEstimate(
            flops=2 * slots * BLK * BLK * width, bytes_accessed=2 * slots * BLK * BLK,
            transcendentals=0,
        ),
        name="adjoint",
    )(me, rows, cols, count, sens, even, odd, after)
    return outs[:-1], outs[-1]


def tile_value(near, face, window):
    span = lax.broadcasted_iota(jnp.int32, (2 * BLK, BLK), 0)
    center = lax.broadcasted_iota(jnp.int32, (2 * BLK, BLK), 1) + RIM
    mix = jnp.where(span == center, jnp.sum(face, axis=0, keepdims=True), 0.0)
    for k in range(4):
        mix = mix - jnp.where(span == near[k : k + 1], face[k : k + 1], 0.0)
    mix_high = mix.astype(jnp.bfloat16)
    mix_low = (mix - mix_high.astype(jnp.float32)).astype(jnp.bfloat16)
    near_high = window.astype(jnp.bfloat16)
    near_low = (window - near_high.astype(jnp.float32)).astype(jnp.bfloat16)
    return lax.dot_general(
        jnp.concatenate([mix_high, mix_high, mix_low], axis=0),
        jnp.concatenate([near_high, near_low, near_high], axis=0),
        (((0,), (0,)), ((), ())), preferred_element_type=jnp.float32,
    )


def smooth_body(offset_ref, model_ref, near_ref, weight_ref, after_ref,
                out_ref, ext_ref, value_ref, got, put):
    cells, width = model_ref.shape
    steps = put.shape[0]
    tiles = cells // BLK // steps
    each = cells // got.shape[0]
    loads = [
        pltpu.make_async_copy(
            model_ref.at[pl.ds(i * each, each)], ext_ref.at[pl.ds(RIM + i * each, each)], got.at[i]
        )
        for i in range(got.shape[0])
    ]
    start_all(loads)
    ext_ref[:RIM] = jnp.zeros((RIM, width), jnp.float32)
    ext_ref[RIM + cells :] = jnp.zeros((RIM, width), jnp.float32)
    wait_all(loads)

    def store(step):
        part = pl.ds(step * tiles * BLK, tiles * BLK)
        return pltpu.make_async_copy(value_ref.at[part], out_ref.at[part], put.at[step])

    @pl.loop(0, steps)
    def _(step):
        for t in range(tiles):
            start = pl.multiple_of((step * tiles + t) * BLK, BLK)
            near = near_ref[:, pl.ds(start, BLK)] - (offset_ref[0] + start)
            face = weight_ref[:, pl.ds(start, BLK)]
            window = ext_ref[pl.ds(start, 2 * BLK), :]
            value_ref[pl.ds(start, BLK), :] = tile_value(near, face, window)
        store(step).start()

    for step in range(steps):
        store(step).wait()


def smoothing(offset, model, neighbors, face_weight, after):
    cells, width = model.shape
    return pl.pallas_call(
        smooth_body,
        out_shape=jax.ShapeDtypeStruct((cells, width), jnp.float32),
        in_specs=[SMEM_SPEC, ANY_SPEC, VMEM_SPEC, VMEM_SPEC, ANY_SPEC],
        out_specs=ANY_SPEC,
        scratch_shapes=[
            pltpu.VMEM((cells + 2 * RIM, width), jnp.float32),
            pltpu.VMEM((cells, width), jnp.float32),
            pltpu.SemaphoreType.DMA((16,)),
            pltpu.SemaphoreType.DMA((8,)),
        ],
        compiler_params=pltpu.CompilerParams(vmem_limit_bytes=LARGE),
        cost_estimate=pl.CostEstimate(
            flops=24 * cells * BLK * width, bytes_accessed=16 * cells * width, transcendentals=0
        ),
        name="smoothing",
    )(offset, model, neighbors, face_weight, after)


def edges_body(me_ref, offset_ref, model_ref, near_ref, weight_ref, base_ref, after_ref, *refs):
    odd_refs, refs = refs[:-6], refs[-6:]
    out_ref, window_ref, value_ref, ends_ref, got, put = refs
    cells = model_ref.shape[0]
    each = odd_refs[-1].shape[0] - 1
    inner = 2 * BLK - RIM
    starts = (0, cells - BLK)
    me = me_ref[0]
    loads = [
        pltpu.make_async_copy(
            model_ref.at[pl.ds(0, inner)], window_ref.at[0, pl.ds(RIM, inner)], got.at[0]
        ),
        pltpu.make_async_copy(
            model_ref.at[pl.ds(cells - inner, inner)], window_ref.at[1, pl.ds(0, inner)], got.at[1]
        ),
    ]
    for i, odd_ref in enumerate(odd_refs):
        loads.append(
            pltpu.make_async_copy(odd_ref.at[each], ends_ref.at[i], got.at[2 + i])
        )
    start_all(loads)
    wait_all(loads)
    zero = jnp.zeros((RIM, model_ref.shape[1]), jnp.float32)
    low, high = zero, zero
    for i in range(len(odd_refs)):
        rows = ends_ref[i, :RIM].astype(jnp.float32) + ends_ref[i, RIM:].astype(jnp.float32)
        peer = me ^ (2 * i + 1)
        low = jnp.where(peer == me - 1, rows, low)
        high = jnp.where(peer == me + 1, rows, high)
    window_ref[0, :RIM] = low
    window_ref[1, inner:] = high
    stores = []
    for i, start in enumerate(starts):
        near = near_ref[:, start : start + BLK] - (offset_ref[0] + start)
        value_ref[i] = tile_value(near, weight_ref[:, start : start + BLK], window_ref[i])
        stores.append(
            pltpu.make_async_copy(value_ref.at[i], out_ref.at[pl.ds(start, BLK)], put.at[i])
        )
    start_all(stores)
    wait_all(stores)


def edges(me, offset, model, neighbors, face_weight, base, after, odd_pieces):
    width = model.shape[1]
    count = len(odd_pieces)
    return pl.pallas_call(
        edges_body,
        out_shape=jax.ShapeDtypeStruct(base.shape, base.dtype),
        in_specs=[SMEM_SPEC, SMEM_SPEC, ANY_SPEC, VMEM_SPEC, VMEM_SPEC]
        + [ANY_SPEC] * (2 + count),
        out_specs=ANY_SPEC,
        input_output_aliases={5: 0},
        scratch_shapes=[
            pltpu.VMEM((2, 2 * BLK, width), jnp.float32),
            pltpu.VMEM((2, BLK, width), jnp.float32),
            pltpu.VMEM((count, BLK, width), jnp.bfloat16),
            pltpu.SemaphoreType.DMA((2 + count,)),
            pltpu.SemaphoreType.DMA((2,)),
        ],
        compiler_params=pltpu.CompilerParams(vmem_limit_bytes=LARGE),
        cost_estimate=pl.CostEstimate(
            flops=24 * 2 * BLK * BLK * width, bytes_accessed=32 * BLK * width, transcendentals=0
        ),
        name="edges",
    )(me, offset, model, neighbors, face_weight, base, after, *odd_pieces)


def finish_body(me_ref, order_ref, basis_ref, even_ref, odd_ref, base_ref,
                out_ref, token_ref, block_ref, value_ref, got, put, *, offset):
    per_peer = odd_ref.shape[0]
    cols = 2 * per_peer
    fetches, stores = [], []
    for i in range(cols):
        peer = me_ref[0] ^ (offset + i // per_peer)
        cell = order_ref[0, peer * per_peer + i % per_peer]
        fetches.append(pltpu.make_async_copy(base_ref.at[cell], block_ref.at[i], got.at[i]))
        stores.append(pltpu.make_async_copy(block_ref.at[i], out_ref.at[cell], put.at[i]))
    start_all(fetches)
    for i in range(cols):
        wave = even_ref[i] if i < per_peer else odd_ref[i - per_peer]
        both = jnp.concatenate([wave, wave], axis=0)
        value_ref[i] = jnp.dot(basis_ref[...], both, preferred_element_type=jnp.float32)
    wait_all(fetches)
    block_ref[...] += value_ref[...]
    start_all(stores)
    token_ref[...] = jnp.zeros_like(token_ref)
    wait_all(stores)


def finish(me, order, even, odd, base, offset):
    width = odd.shape[2]
    cols = 2 * odd.shape[0]
    basis = haar_matrix(BLK).T.astype(np.float32)
    high = basis.astype(jnp.bfloat16)
    low = (basis - high.astype(np.float32)).astype(jnp.bfloat16)
    basis2 = jnp.asarray(np.concatenate([high, low], axis=1))
    return pl.pallas_call(
        lambda *refs: finish_body(*refs, offset=offset),
        out_shape=[
            jax.ShapeDtypeStruct(base.shape, base.dtype),
            jax.ShapeDtypeStruct((8, BLK), jnp.float32),
        ],
        in_specs=[SMEM_SPEC] * 2 + [VMEM_SPEC] * 3 + [ANY_SPEC],
        out_specs=[ANY_SPEC, VMEM_SPEC],
        input_output_aliases={5: 0},
        scratch_shapes=[
            pltpu.VMEM((cols, BLK, width), jnp.float32),
            pltpu.VMEM((cols, BLK, width), jnp.float32),
            pltpu.SemaphoreType.DMA((cols,)),
            pltpu.SemaphoreType.DMA((cols,)),
        ],
        compiler_params=pltpu.CompilerParams(vmem_limit_bytes=SMALL),
        cost_estimate=pl.CostEstimate(
            flops=4 * cols * BLK * BLK * width, bytes_accessed=10 * cols * BLK * width,
            transcendentals=0,
        ),
        name="finish",
    )(me, order, basis2, even, odd, base)


def merge_body(got_ref, mine_ref, after_ref, out_ref):
    total = got_ref[...].astype(jnp.float32) + mine_ref[...].astype(jnp.float32)
    out_ref[...] = total.astype(out_ref.dtype)


def merge(got, mine, after):
    return pl.pallas_call(
        merge_body,
        out_shape=jax.ShapeDtypeStruct(mine.shape, mine.dtype),
        in_specs=[VMEM_SPEC, VMEM_SPEC, ANY_SPEC],
        out_specs=VMEM_SPEC,
        compiler_params=pltpu.CompilerParams(vmem_limit_bytes=SMALL),
        cost_estimate=pl.CostEstimate(
            flops=mine.size, bytes_accessed=6 * mine.size, transcendentals=0
        ),
        name="merge",
    )(got, mine, after)


def pick_body(take_ref, got_ref, mine_ref, after_ref, token_ref, *out_refs):
    each = out_refs[0].shape[0]
    for i, out_ref in enumerate(out_refs):
        part = pl.ds(i * each, each)
        out_ref[...] = jnp.where(take_ref[0] > 0, got_ref[part], mine_ref[part])


def pick(take, got, mine, after, token, parts):
    shape = (mine.shape[0] // parts, *mine.shape[1:])
    return pl.pallas_call(
        pick_body,
        out_shape=[jax.ShapeDtypeStruct(shape, mine.dtype)] * parts,
        in_specs=[SMEM_SPEC, VMEM_SPEC, VMEM_SPEC, ANY_SPEC, ANY_SPEC],
        out_specs=[VMEM_SPEC] * parts,
        compiler_params=pltpu.CompilerParams(vmem_limit_bytes=SMALL),
        cost_estimate=pl.CostEstimate(
            flops=mine.size, bytes_accessed=6 * mine.size, transcendentals=0
        ),
        name="pick",
    )(take, got, mine, after, token)


def line_sums(parts, axis, deliver):
    count = lax.axis_size(axis)
    half = count // 2
    me = lax.axis_index(axis)
    stages = []
    for hop in range(half - 1):
        stages.append(([(hop, hop + 1), (count - 1 - hop, count - 2 - hop)], False))
    stages.append(([(half - 1, half), (half, half - 1)], False))
    for hop in range(half - 1):
        left, right = half - 1 - hop, half + hop
        stages.append(([(left, left - 1), (right, right + 1)], True))
    state = list(parts)
    got = [lax.ppermute(part, axis, stages[0][0]) for part in parts]
    after = parts[0]
    for time in range(len(parts) + len(stages) - 1):
        for s, (pairs, outwards) in enumerate(stages):
            k = time - s
            if not 0 <= k < len(parts):
                continue
            last = s + 1 == len(stages)
            if outwards:
                take = (me == pairs[0][1]) | (me == pairs[1][1])
                take = take.astype(jnp.int32).reshape(1)
                if last:
                    after = deliver(k, take, got[k], state[k], after)
                else:
                    state[k] = jnp.where(take[0] > 0, got[k], state[k])
            else:
                state[k] = after = merge(got[k], state[k], after)
                if last:
                    take = jnp.zeros((1,), jnp.int32)
                    after = deliver(k, take, state[k], state[k], after)
            if not last:
                got[k] = lax.ppermute(state[k], axis, stages[s + 1][0])


def swap(piece, axis, offset):
    return lax.ppermute(piece, axis, [(c, c ^ offset) for c in range(lax.axis_size(axis))])


def local(model_dir, sens_blocks, blk_row, blk_col, blk_count, send_order, neighbors, face_weight):
    cell_count, width = model_dir.shape
    blocks = cell_count // BLK
    peers = lax.axis_size("cols")
    half = peers // 2
    per_peer = blocks // peers
    col = lax.axis_index("cols").astype(jnp.int32)
    me = col.reshape(1)
    offset = (col * cell_count - RIM).reshape(1)
    sens = sens_blocks[0]
    evens = range(1, half)

    *own, odd = analyze(me, send_order, model_dir.reshape(blocks, BLK, width), peers)
    partner = swap(odd, "cols", 1)
    direct = {j: swap(own[j], "cols", 2 * j) for j in reversed(evens)}
    passed = {
        j: swap(partner[j * (per_peer + 1) : (j + 1) * (per_peer + 1)], "cols", 2 * j)
        for j in reversed(evens)
    }
    waves = [own[0], partner]
    for j in evens:
        waves += [direct[j], passed[j]]
    smooth = smoothing(offset, model_dir, neighbors, face_weight, partner)

    even_rows, odd_rows = forward(
        me, blk_row, blk_col, blk_count, sens, waves, (smooth, blocks)
    )
    pair = (even_rows + swap(odd_rows, "cols", 1)).reshape(half, -1, BLK, width)
    to_send = pair.astype(jnp.bfloat16)
    shares = [swap(to_send[j], "cols", 2 * j) for j in evens]
    total = pair[0] + sum(share.astype(jnp.float32) for share in shares)
    image_share = total.astype(jnp.bfloat16)
    even_image = jnp.concatenate(
        [image_share] + [swap(image_share, "cols", 2 * j) for j in evens], axis=0
    )
    odd_image = swap(even_image, "cols", 1)
    smooth = edges(
        me, offset, model_dir, neighbors, face_weight, smooth, to_send, waves[1::2]
    )

    partial_cols, image = adjoint(
        me, blk_row, blk_col, blk_count, sens, even_image, odd_image, smooth, blocks, peers
    )
    data_image = image.reshape(RB_DEV * BLK, width).astype(jnp.float32)
    normal = smooth.reshape(blocks, BLK, width)
    order = sorted(range(half), key=lambda j: (-bin(j).count("1"), j))
    waiting, tokens = [], []

    def end_one():
        nonlocal normal
        even, odd_piece, j = waiting.pop(0)
        normal, token = finish(me, send_order, even, odd_piece, normal, 2 * j)
        tokens.append(token)

    def deliver(k, take, got, mine, after):
        if k >= 2:
            end_one()
        token = tokens[-1] if tokens else after
        j = order[k]
        if j:
            [total] = pick(take, got, mine, after, token, 1)
            even = swap(total, "cols", 2 * j)
            other = even[per_peer:]
        else:
            even, other = pick(take, got, mine, after, token, 2)
            total = even
        waiting.append((even, swap(other, "cols", 1), j))
        return total

    line_sums([partial_cols[j] for j in order], "rows", deliver)
    while waiting:
        end_one()
    return (data_image, normal.reshape(cell_count, width))


def solution(mesh):
    placed = (
        P("cols", None),
        P("rows", "cols", None, None),
        P("rows", "cols"),
        P("rows", "cols"),
        P("rows", "cols"),
        P("cols", None),
        P(None, "cols"),
        P(None, "cols"),
    )
    return jax.shard_map(
        local,
        mesh=mesh,
        in_specs=placed,
        out_specs=(P("rows", None), P("cols", None)),
        check_vma=False,
    )
```

```python
import math

import jax
import jax.numpy as jnp
import numpy as np
from jax import lax
from jax.experimental import pallas as pl
from jax.experimental.pallas import tpu as pltpu
from jax.sharding import PartitionSpec as P

BLK = 128
RB_DEV = 32
RIM = 64
STEP = 16
MIB = 1 << 20
SMALL = 16 * MIB
LARGE = 56 * MIB
ANY_SPEC = pl.BlockSpec(memory_space=pl.ANY)
VMEM_SPEC = pl.BlockSpec(memory_space=pltpu.VMEM)
SMEM_SPEC = pl.BlockSpec(memory_space=pltpu.SMEM)


def haar_matrix(order_n):
    matrix = np.ones((1, 1))
    while matrix.shape[0] < order_n:
        length = matrix.shape[0]
        upper = np.kron(matrix, np.array([[1.0, 1.0]]))
        lower = np.kron(np.eye(length), np.array([[1.0, -1.0]]))
        matrix = np.concatenate([upper, lower], axis=0) / math.sqrt(2.0)
    return matrix


def fetch(source, target, sems, pieces):
    each = source.shape[0] // pieces
    parts = [pl.ds(i * each, each) for i in range(pieces)]
    return [
        pltpu.make_async_copy(source.at[part], target.at[part], sems.at[i])
        for i, part in enumerate(parts)
    ]


def gather_pieces(sources, held_ref, me, sems):
    each = held_ref.shape[0] // len(sources)
    return [
        pltpu.make_async_copy(
            ref.at[pl.ds(first, each)],
            held_ref.at[pl.ds((me ^ offset) * each, each)],
            sems.at[offset],
        )
        for ref, first, offset in sources
    ]


def far_first(peers):
    return sorted(range(1, peers // 2), key=lambda j: (-bin(j).count("1"), j))


def wave_offsets(peers):
    far = far_first(peers)
    return [0, 1, *[2 * j for j in far], *[2 * j + 1 for j in far]]


def piece_stores(source, offset, even_refs, odd_ref, sems):
    each = source.shape[0]
    stride = odd_ref.shape[0] // (sems.shape[0] // 2)
    if offset % 2:
        target = odd_ref.at[pl.ds((offset // 2) * stride, each)]
    else:
        target = even_refs[offset // 2].at[pl.ds(0, each)]
    return pltpu.make_async_copy(source, target, sems.at[offset])


def start_all(copies):
    for copy in copies:
        copy.start()


def wait_all(copies):
    for copy in copies:
        copy.wait()


def analyze_body(me_ref, order_ref, model_ref, *refs):
    even_refs, (odd_ref, block_ref, coeff_ref, got, put) = refs[:-5], refs[-5:]
    width = model_ref.shape[2]
    per_peer = even_refs[0].shape[0]
    peers = put.shape[0]
    me = me_ref[0]
    loads = fetch(model_ref, block_ref, got, got.shape[0])
    start_all(loads)
    row = lax.broadcasted_iota(jnp.int32, (BLK, BLK), 0)
    col = lax.broadcasted_iota(jnp.int32, (BLK, BLK), 1)
    level = jnp.ones_like(row)
    scale = jnp.full((BLK, width), BLK**-0.5, jnp.float32)
    wide_row = lax.broadcasted_iota(jnp.int32, (BLK, width), 0)
    size = 2
    while size < BLK:
        level = jnp.where(row >= size, size, level)
        scale = jnp.where(wide_row >= size, (size / BLK) ** 0.5, scale)
        size *= 2
    span = BLK // level
    inside = col - (row - level) * span
    sign = jnp.where(inside * 2 < span, 1.0, -1.0)
    sign = jnp.where((inside >= 0) & (inside < span), sign, 0.0)
    sign = jnp.where(row == 0, 1.0, sign).astype(jnp.bfloat16)
    both_signs = jnp.concatenate([sign, sign], axis=1)
    wait_all(loads)
    stores = []
    ends = []
    for rows in (block_ref[model_ref.shape[0] - 1, BLK - RIM :], block_ref[0, :RIM]):
        high = rows.astype(jnp.bfloat16)
        low = (rows - high.astype(jnp.float32)).astype(jnp.bfloat16)
        ends.append(jnp.concatenate([high, low], axis=0))
    for offset in [*range(1, peers, 2), *range(peers - 2, -1, -2)]:
        peer = (me ^ offset) * per_peer
        for q in range(per_peer):
            x = block_ref[order_ref[0, peer + q]]
            high = x.astype(jnp.bfloat16)
            low = (x - high.astype(jnp.float32)).astype(jnp.bfloat16)
            raw = jnp.dot(
                both_signs, jnp.concatenate([high, low], axis=0),
                preferred_element_type=jnp.float32,
            )
            coeff_ref[offset, q] = (raw * scale).astype(jnp.bfloat16)
        length = per_peer
        if offset % 2:
            coeff_ref[offset, per_peer] = jnp.where(me ^ offset == me + 1, ends[0], ends[1])
            length += 1
        source = coeff_ref.at[offset, pl.ds(0, length)]
        stores.append(piece_stores(source, offset, even_refs, odd_ref, put))
        stores[-1].start()
    wait_all(stores)


def piece_shapes(piece, peers, dtype, more=0):
    half = peers // 2
    return [jax.ShapeDtypeStruct(piece, dtype)] * half + [
        jax.ShapeDtypeStruct((half * (piece[0] + more), *piece[1:]), dtype)
    ]


def analyze(me, order, model_blocks, peers):
    blocks, _, width = model_blocks.shape
    piece = (blocks // peers, BLK, width)
    return pl.pallas_call(
        analyze_body,
        out_shape=piece_shapes(piece, peers, jnp.bfloat16, 1),
        in_specs=[SMEM_SPEC, SMEM_SPEC, ANY_SPEC],
        out_specs=[ANY_SPEC] * (peers // 2 + 1),
        scratch_shapes=[
            pltpu.VMEM((blocks, BLK, width), jnp.float32),
            pltpu.VMEM((peers, piece[0] + 1, *piece[1:]), jnp.bfloat16),
            pltpu.SemaphoreType.DMA((16,)),
            pltpu.SemaphoreType.DMA((peers,)),
        ],
        compiler_params=pltpu.CompilerParams(vmem_limit_bytes=LARGE),
        cost_estimate=pl.CostEstimate(
            flops=4 * blocks * BLK * BLK * width, bytes_accessed=6 * blocks * BLK * width,
            transcendentals=0,
        ),
        name="analyze",
    )(me, order, model_blocks)


def slot_loop(count, sens_ref, block_ref, sems, others, acc_ref, work, then=()):
    steps = sems.shape[0]
    each = sens_ref.shape[0] // steps

    def block_copy(step):
        part = pl.ds(step * each, each)
        return pltpu.make_async_copy(sens_ref.at[part], block_ref.at[part], sems.at[step])

    start_all(others)
    needed = (count + each - 1) // each

    @pl.loop(0, needed)
    def _(step):
        block_copy(step).start()

    acc_ref[...] = jnp.zeros_like(acc_ref)
    wait_all(others)
    start_all(then)

    @pl.loop(0, needed)
    def _(step):
        block_copy(step).wait()
        for k in range(each):
            slot = step * each + k
            work(slot, block_ref[slot], slot < count)


def forward_body(me_ref, rows_ref, cols_ref, count_ref, sens_ref, *refs):
    peers = len(refs) - 9
    wave_refs, (even_ref, odd_ref) = refs[:peers], refs[peers + 1 : peers + 3]
    block_ref, held_ref, acc_ref, sems, got, put = refs[peers + 3 :]
    row_blocks = acc_ref.shape[0] - 1
    each = row_blocks // peers
    me = me_ref[0]
    def work(slot, block, live):
        row = jnp.where(live, rows_ref[0, slot], row_blocks)
        acc_ref[row] += jnp.dot(
            block, held_ref[cols_ref[0, slot]], preferred_element_type=jnp.float32
        )

    sources = [(ref, 0, offset) for ref, offset in zip(wave_refs, wave_offsets(peers))]
    waves = gather_pieces(sources, held_ref, me, got)
    slot_loop(count_ref[0, 0], sens_ref, block_ref, sems, waves, acc_ref, work)
    stores = []
    for offset in [*range(1, peers, 2), *range(0, peers, 2)]:
        target = odd_ref if offset % 2 else even_ref
        stores.append(
            pltpu.make_async_copy(
                acc_ref.at[pl.ds((me ^ offset) * each, each)],
                target.at[pl.ds((offset // 2) * each, each)],
                put.at[offset],
            )
        )
    start_all(stores)
    wait_all(stores)


def forward(me, rows, cols, count, sens, waves, after):
    slots = sens.shape[0]
    peers = len(waves)
    blocks, width = after[1], sens.shape[2]
    half = (RB_DEV // 2, BLK, width)
    return pl.pallas_call(
        forward_body,
        out_shape=[jax.ShapeDtypeStruct(half, jnp.float32)] * 2,
        in_specs=[SMEM_SPEC] * 4 + [ANY_SPEC] * (1 + peers + 1),
        out_specs=[ANY_SPEC] * 2,
        scratch_shapes=[
            pltpu.VMEM(sens.shape, sens.dtype),
            pltpu.VMEM((blocks, BLK, width), jnp.bfloat16),
            pltpu.VMEM((RB_DEV + 1, BLK, width), jnp.float32),
            pltpu.SemaphoreType.DMA((slots // STEP,)),
            pltpu.SemaphoreType.DMA((peers,)),
            pltpu.SemaphoreType.DMA((peers,)),
        ],
        compiler_params=pltpu.CompilerParams(vmem_limit_bytes=LARGE),
        cost_estimate=pl.CostEstimate(
            flops=2 * slots * BLK * BLK * width, bytes_accessed=2 * slots * BLK * BLK,
            transcendentals=0,
        ),
        name="forward",
    )(me, rows, cols, count, sens, *waves, after[0])


def adjoint_body(me_ref, rows_ref, cols_ref, count_ref, sens_ref, even_in_ref, odd_in_ref,
                 after_ref, *refs):
    out_refs, image_ref = refs[:-9], refs[-9]
    block_ref, held_ref, acc_ref, half_ref, sems, got, put, whole = refs[-8:]
    peers = put.shape[0]
    col_blocks = acc_ref.shape[0] - 1
    each = col_blocks // peers
    me = me_ref[0]
    def work(slot, block, live):
        col = jnp.where(live, cols_ref[0, slot], col_blocks)
        acc_ref[col] += lax.dot_general(
            block, held_ref[rows_ref[0, slot]], (((0,), (0,)), ((), ())),
            preferred_element_type=jnp.float32,
        )

    each_in = held_ref.shape[0] // peers
    sources = [
        (ref, i * each_in, 2 * j + odd)
        for i, j in enumerate([0, *far_first(peers)])
        for odd, ref in enumerate((even_in_ref, odd_in_ref))
    ]
    images = gather_pieces(sources, held_ref, me, got)
    stores = fetch(held_ref, image_ref, whole, whole.shape[0])
    slot_loop(count_ref[0, 0], sens_ref, block_ref, sems, images, acc_ref, work, stores)
    for offset in reversed(range(peers)):
        part = acc_ref[pl.ds((me ^ offset) * each, each)]
        half_ref[offset] = part.astype(half_ref.dtype)
        target = out_refs[offset // 2].at[pl.ds(offset % 2 * each, each)]
        stores.append(pltpu.make_async_copy(half_ref.at[offset], target, put.at[offset]))
        stores[-1].start()
    wait_all(stores)


def adjoint(me, rows, cols, count, sens, even, odd, after, blocks, peers):
    slots = sens.shape[0]
    width = even.shape[2]
    piece = (blocks // peers, BLK, width)
    image = (RB_DEV, BLK, width)
    outs = pl.pallas_call(
        adjoint_body,
        out_shape=[jax.ShapeDtypeStruct((2 * piece[0], *piece[1:]), jnp.bfloat16)] * (peers // 2)
        + [jax.ShapeDtypeStruct(image, jnp.bfloat16)],
        in_specs=[SMEM_SPEC] * 4 + [ANY_SPEC] * 4,
        out_specs=[ANY_SPEC] * (peers // 2 + 1),
        scratch_shapes=[
            pltpu.VMEM(sens.shape, sens.dtype),
            pltpu.VMEM(image, jnp.bfloat16),
            pltpu.VMEM((blocks + 1, BLK, width), jnp.float32),
            pltpu.VMEM((peers, *piece), jnp.bfloat16),
            pltpu.SemaphoreType.DMA((slots // STEP,)),
            pltpu.SemaphoreType.DMA((peers,)),
            pltpu.SemaphoreType.DMA((peers,)),
            pltpu.SemaphoreType.DMA((4,)),
        ],
        compiler_params=pltpu.CompilerParams(vmem_limit_bytes=LARGE),
        cost_estimate=pl.CostEstimate(
            flops=2 * slots * BLK * BLK * width, bytes_accessed=2 * slots * BLK * BLK,
            transcendentals=0,
        ),
        name="adjoint",
    )(me, rows, cols, count, sens, even, odd, after)
    return outs[:-1], outs[-1]


def tile_value(near, face, window):
    span = lax.broadcasted_iota(jnp.int32, (2 * BLK, BLK), 0)
    center = lax.broadcasted_iota(jnp.int32, (2 * BLK, BLK), 1) + RIM
    mix = jnp.where(span == center, jnp.sum(face, axis=0, keepdims=True), 0.0)
    for k in range(4):
        mix = mix - jnp.where(span == near[k : k + 1], face[k : k + 1], 0.0)
    mix_high = mix.astype(jnp.bfloat16)
    mix_low = (mix - mix_high.astype(jnp.float32)).astype(jnp.bfloat16)
    near_high = window.astype(jnp.bfloat16)
    near_low = (window - near_high.astype(jnp.float32)).astype(jnp.bfloat16)
    return lax.dot_general(
        jnp.concatenate([mix_high, mix_high, mix_low], axis=0),
        jnp.concatenate([near_high, near_low, near_high], axis=0),
        (((0,), (0,)), ((), ())), preferred_element_type=jnp.float32,
    )


def smooth_body(offset_ref, model_ref, near_ref, weight_ref, after_ref,
                out_ref, ext_ref, value_ref, got, put):
    cells, width = model_ref.shape
    steps = put.shape[0]
    tiles = cells // BLK // steps
    each = cells // got.shape[0]
    loads = [
        pltpu.make_async_copy(
            model_ref.at[pl.ds(i * each, each)], ext_ref.at[pl.ds(RIM + i * each, each)], got.at[i]
        )
        for i in range(got.shape[0])
    ]
    start_all(loads)
    ext_ref[:RIM] = jnp.zeros((RIM, width), jnp.float32)
    ext_ref[RIM + cells :] = jnp.zeros((RIM, width), jnp.float32)
    wait_all(loads)

    def store(step):
        part = pl.ds(step * tiles * BLK, tiles * BLK)
        return pltpu.make_async_copy(value_ref.at[part], out_ref.at[part], put.at[step])

    @pl.loop(0, steps)
    def _(step):
        for t in range(tiles):
            start = pl.multiple_of((step * tiles + t) * BLK, BLK)
            near = near_ref[:, pl.ds(start, BLK)] - (offset_ref[0] + start)
            face = weight_ref[:, pl.ds(start, BLK)]
            window = ext_ref[pl.ds(start, 2 * BLK), :]
            value_ref[pl.ds(start, BLK), :] = tile_value(near, face, window)
        store(step).start()

    for step in range(steps):
        store(step).wait()


def smoothing(offset, model, neighbors, face_weight, after):
    cells, width = model.shape
    return pl.pallas_call(
        smooth_body,
        out_shape=jax.ShapeDtypeStruct((cells, width), jnp.float32),
        in_specs=[SMEM_SPEC, ANY_SPEC, VMEM_SPEC, VMEM_SPEC, ANY_SPEC],
        out_specs=ANY_SPEC,
        scratch_shapes=[
            pltpu.VMEM((cells + 2 * RIM, width), jnp.float32),
            pltpu.VMEM((cells, width), jnp.float32),
            pltpu.SemaphoreType.DMA((16,)),
            pltpu.SemaphoreType.DMA((8,)),
        ],
        compiler_params=pltpu.CompilerParams(vmem_limit_bytes=LARGE),
        cost_estimate=pl.CostEstimate(
            flops=24 * cells * BLK * width, bytes_accessed=16 * cells * width, transcendentals=0
        ),
        name="smoothing",
    )(offset, model, neighbors, face_weight, after)


def edges_body(me_ref, offset_ref, model_ref, near_ref, weight_ref, base_ref, after_ref, *refs):
    odd_refs, refs = refs[:-6], refs[-6:]
    out_ref, window_ref, value_ref, ends_ref, got, put = refs
    cells = model_ref.shape[0]
    each = odd_refs[-1].shape[0] - 1
    inner = 2 * BLK - RIM
    starts = (0, cells - BLK)
    me = me_ref[0]
    loads = [
        pltpu.make_async_copy(
            model_ref.at[pl.ds(0, inner)], window_ref.at[0, pl.ds(RIM, inner)], got.at[0]
        ),
        pltpu.make_async_copy(
            model_ref.at[pl.ds(cells - inner, inner)], window_ref.at[1, pl.ds(0, inner)], got.at[1]
        ),
    ]
    for i, odd_ref in enumerate(odd_refs):
        loads.append(
            pltpu.make_async_copy(odd_ref.at[each], ends_ref.at[i], got.at[2 + i])
        )
    start_all(loads)
    wait_all(loads)
    zero = jnp.zeros((RIM, model_ref.shape[1]), jnp.float32)
    low, high = zero, zero
    for i in range(len(odd_refs)):
        rows = ends_ref[i, :RIM].astype(jnp.float32) + ends_ref[i, RIM:].astype(jnp.float32)
        peer = me ^ (2 * i + 1)
        low = jnp.where(peer == me - 1, rows, low)
        high = jnp.where(peer == me + 1, rows, high)
    window_ref[0, :RIM] = low
    window_ref[1, inner:] = high
    stores = []
    for i, start in enumerate(starts):
        near = near_ref[:, start : start + BLK] - (offset_ref[0] + start)
        value_ref[i] = tile_value(near, weight_ref[:, start : start + BLK], window_ref[i])
        stores.append(
            pltpu.make_async_copy(value_ref.at[i], out_ref.at[pl.ds(start, BLK)], put.at[i])
        )
    start_all(stores)
    wait_all(stores)


def edges(me, offset, model, neighbors, face_weight, base, after, odd_pieces):
    width = model.shape[1]
    count = len(odd_pieces)
    return pl.pallas_call(
        edges_body,
        out_shape=jax.ShapeDtypeStruct(base.shape, base.dtype),
        in_specs=[SMEM_SPEC, SMEM_SPEC, ANY_SPEC, VMEM_SPEC, VMEM_SPEC]
        + [ANY_SPEC] * (2 + count),
        out_specs=ANY_SPEC,
        input_output_aliases={5: 0},
        scratch_shapes=[
            pltpu.VMEM((2, 2 * BLK, width), jnp.float32),
            pltpu.VMEM((2, BLK, width), jnp.float32),
            pltpu.VMEM((count, BLK, width), jnp.bfloat16),
            pltpu.SemaphoreType.DMA((2 + count,)),
            pltpu.SemaphoreType.DMA((2,)),
        ],
        compiler_params=pltpu.CompilerParams(vmem_limit_bytes=LARGE),
        cost_estimate=pl.CostEstimate(
            flops=24 * 2 * BLK * BLK * width, bytes_accessed=32 * BLK * width, transcendentals=0
        ),
        name="edges",
    )(me, offset, model, neighbors, face_weight, base, after, *odd_pieces)


def finish_body(me_ref, order_ref, basis_ref, even_ref, odd_ref, base_ref,
                out_ref, token_ref, block_ref, value_ref, got, put, *, offset):
    per_peer = odd_ref.shape[0]
    cols = 2 * per_peer
    fetches, stores = [], []
    for i in range(cols):
        peer = me_ref[0] ^ (offset + i // per_peer)
        cell = order_ref[0, peer * per_peer + i % per_peer]
        fetches.append(pltpu.make_async_copy(base_ref.at[cell], block_ref.at[i], got.at[i]))
        stores.append(pltpu.make_async_copy(block_ref.at[i], out_ref.at[cell], put.at[i]))
    start_all(fetches)
    for i in range(cols):
        wave = even_ref[i] if i < per_peer else odd_ref[i - per_peer]
        both = jnp.concatenate([wave, wave], axis=0)
        value_ref[i] = jnp.dot(basis_ref[...], both, preferred_element_type=jnp.float32)
    wait_all(fetches)
    block_ref[...] += value_ref[...]
    start_all(stores)
    token_ref[...] = jnp.zeros_like(token_ref)
    wait_all(stores)


def finish(me, order, even, odd, base, offset):
    width = odd.shape[2]
    cols = 2 * odd.shape[0]
    basis = haar_matrix(BLK).T.astype(np.float32)
    high = basis.astype(jnp.bfloat16)
    low = (basis - high.astype(np.float32)).astype(jnp.bfloat16)
    basis2 = jnp.asarray(np.concatenate([high, low], axis=1))
    return pl.pallas_call(
        lambda *refs: finish_body(*refs, offset=offset),
        out_shape=[
            jax.ShapeDtypeStruct(base.shape, base.dtype),
            jax.ShapeDtypeStruct((8, BLK), jnp.float32),
        ],
        in_specs=[SMEM_SPEC] * 2 + [VMEM_SPEC] * 3 + [ANY_SPEC],
        out_specs=[ANY_SPEC, VMEM_SPEC],
        input_output_aliases={5: 0},
        scratch_shapes=[
            pltpu.VMEM((cols, BLK, width), jnp.float32),
            pltpu.VMEM((cols, BLK, width), jnp.float32),
            pltpu.SemaphoreType.DMA((cols,)),
            pltpu.SemaphoreType.DMA((cols,)),
        ],
        compiler_params=pltpu.CompilerParams(vmem_limit_bytes=SMALL),
        cost_estimate=pl.CostEstimate(
            flops=4 * cols * BLK * BLK * width, bytes_accessed=10 * cols * BLK * width,
            transcendentals=0,
        ),
        name="finish",
    )(me, order, basis2, even, odd, base)


def merge_body(got_ref, mine_ref, after_ref, out_ref):
    total = got_ref[...].astype(jnp.float32) + mine_ref[...].astype(jnp.float32)
    out_ref[...] = total.astype(out_ref.dtype)


def merge(got, mine, after):
    return pl.pallas_call(
        merge_body,
        out_shape=jax.ShapeDtypeStruct(mine.shape, mine.dtype),
        in_specs=[VMEM_SPEC, VMEM_SPEC, ANY_SPEC],
        out_specs=VMEM_SPEC,
        compiler_params=pltpu.CompilerParams(vmem_limit_bytes=SMALL),
        cost_estimate=pl.CostEstimate(
            flops=mine.size, bytes_accessed=6 * mine.size, transcendentals=0
        ),
        name="merge",
    )(got, mine, after)


def pick_body(take_ref, got_ref, mine_ref, after_ref, token_ref, *out_refs):
    each = out_refs[0].shape[0]
    for i, out_ref in enumerate(out_refs):
        part = pl.ds(i * each, each)
        out_ref[...] = jnp.where(take_ref[0] > 0, got_ref[part], mine_ref[part])


def pick(take, got, mine, after, token, parts):
    shape = (mine.shape[0] // parts, *mine.shape[1:])
    return pl.pallas_call(
        pick_body,
        out_shape=[jax.ShapeDtypeStruct(shape, mine.dtype)] * parts,
        in_specs=[SMEM_SPEC, VMEM_SPEC, VMEM_SPEC, ANY_SPEC, ANY_SPEC],
        out_specs=[VMEM_SPEC] * parts,
        compiler_params=pltpu.CompilerParams(vmem_limit_bytes=SMALL),
        cost_estimate=pl.CostEstimate(
            flops=mine.size, bytes_accessed=6 * mine.size, transcendentals=0
        ),
        name="pick",
    )(take, got, mine, after, token)


def line_sums(parts, axis, deliver):
    count = lax.axis_size(axis)
    half = count // 2
    me = lax.axis_index(axis)
    stages = []
    for hop in range(half - 1):
        stages.append(([(hop, hop + 1), (count - 1 - hop, count - 2 - hop)], False))
    stages.append(([(half - 1, half), (half, half - 1)], False))
    for hop in range(half - 1):
        left, right = half - 1 - hop, half + hop
        stages.append(([(left, left - 1), (right, right + 1)], True))
    state = list(parts)
    got = [lax.ppermute(part, axis, stages[0][0]) for part in parts]
    after = parts[0]
    for time in range(len(parts) + len(stages) - 1):
        for s, (pairs, outwards) in enumerate(stages):
            k = time - s
            if not 0 <= k < len(parts):
                continue
            last = s + 1 == len(stages)
            if outwards:
                take = (me == pairs[0][1]) | (me == pairs[1][1])
                take = take.astype(jnp.int32).reshape(1)
                if last:
                    after = deliver(k, take, got[k], state[k], after)
                else:
                    state[k] = jnp.where(take[0] > 0, got[k], state[k])
            else:
                state[k] = after = merge(got[k], state[k], after)
                if last:
                    take = jnp.zeros((1,), jnp.int32)
                    after = deliver(k, take, state[k], state[k], after)
            if not last:
                got[k] = lax.ppermute(state[k], axis, stages[s + 1][0])


def swap(piece, axis, offset):
    return lax.ppermute(piece, axis, [(c, c ^ offset) for c in range(lax.axis_size(axis))])


def local(model_dir, sens_blocks, blk_row, blk_col, blk_count, send_order, neighbors, face_weight):
    cell_count, width = model_dir.shape
    blocks = cell_count // BLK
    peers = lax.axis_size("cols")
    half = peers // 2
    per_peer = blocks // peers
    col = lax.axis_index("cols").astype(jnp.int32)
    me = col.reshape(1)
    offset = (col * cell_count - RIM).reshape(1)
    sens = sens_blocks[0]
    far = far_first(peers)

    *own, odd = analyze(me, send_order, model_dir.reshape(blocks, BLK, width), peers)
    partner = swap(odd, "cols", 1)
    direct = {j: swap(own[j], "cols", 2 * j) for j in far}
    passed = {
        j: swap(partner[j * (per_peer + 1) : (j + 1) * (per_peer + 1)], "cols", 2 * j)
        for j in far
    }
    waves = [own[0], partner, *[direct[j] for j in far], *[passed[j] for j in far]]
    smooth = smoothing(offset, model_dir, neighbors, face_weight, partner)

    even_rows, odd_rows = forward(
        me, blk_row, blk_col, blk_count, sens, waves, (smooth, blocks)
    )
    pair = (even_rows + swap(odd_rows, "cols", 1)).reshape(half, -1, BLK, width)
    to_send = pair.astype(jnp.bfloat16)
    shares = [swap(to_send[j], "cols", 2 * j) for j in far]
    total = pair[0] + sum(share.astype(jnp.float32) for share in shares)
    image_share = total.astype(jnp.bfloat16)
    even_image = jnp.concatenate(
        [image_share] + [swap(image_share, "cols", 2 * j) for j in far], axis=0
    )
    odd_image = swap(even_image, "cols", 1)
    smooth = edges(
        me, offset, model_dir, neighbors, face_weight, smooth, to_send, [partner, *[passed[j] for j in range(1, half)]]
    )

    partial_cols, image = adjoint(
        me, blk_row, blk_col, blk_count, sens, even_image, odd_image, smooth, blocks, peers
    )
    data_image = image.reshape(RB_DEV * BLK, width).astype(jnp.float32)
    normal = smooth.reshape(blocks, BLK, width)
    order = [*far, 0]
    waiting, tokens = [], []

    def end_one(place):
        nonlocal normal
        even, odd_piece, j = waiting.pop(place)
        normal, token = finish(me, send_order, even, odd_piece, normal, 2 * j)
        tokens.append(token)

    def deliver(k, take, got, mine, after):
        if k >= 2:
            end_one(0)
        token = tokens[-1] if tokens else after
        j = order[k]
        if j:
            [total] = pick(take, got, mine, after, token, 1)
            even = swap(total, "cols", 2 * j)
            other = even[per_peer:]
        else:
            even, other = pick(take, got, mine, after, token, 2)
            total = even
        waiting.append((even, swap(other, "cols", 1), j))
        return total

    line_sums([partial_cols[j] for j in order], "rows", deliver)
    while waiting:
        end_one(-1)
    return (data_image, normal.reshape(cell_count, width))


def solution(mesh):
    placed = (
        P("cols", None),
        P("rows", "cols", None, None),
        P("rows", "cols"),
        P("rows", "cols"),
        P("rows", "cols"),
        P("cols", None),
        P(None, "cols"),
        P(None, "cols"),
    )
    return jax.shard_map(
        local,
        mesh=mesh,
        in_specs=placed,
        out_specs=(P("rows", None), P("cols", None)),
        check_vma=False,
    )
```

```python
import math

import jax
import jax.numpy as jnp
import numpy as np
from jax import lax
from jax.experimental import pallas as pl
from jax.experimental.pallas import tpu as pltpu
from jax.sharding import PartitionSpec as P

BLK = 128
RB_DEV = 32
RIM = 64
STEP = 16
MIB = 1 << 20
SMALL = 16 * MIB
LARGE = 56 * MIB
ANY_SPEC = pl.BlockSpec(memory_space=pl.ANY)
VMEM_SPEC = pl.BlockSpec(memory_space=pltpu.VMEM)
SMEM_SPEC = pl.BlockSpec(memory_space=pltpu.SMEM)


def haar_matrix(order_n):
    matrix = np.ones((1, 1))
    while matrix.shape[0] < order_n:
        length = matrix.shape[0]
        upper = np.kron(matrix, np.array([[1.0, 1.0]]))
        lower = np.kron(np.eye(length), np.array([[1.0, -1.0]]))
        matrix = np.concatenate([upper, lower], axis=0) / math.sqrt(2.0)
    return matrix


def fetch(source, target, sems, pieces):
    each = source.shape[0] // pieces
    parts = [pl.ds(i * each, each) for i in range(pieces)]
    return [
        pltpu.make_async_copy(source.at[part], target.at[part], sems.at[i])
        for i, part in enumerate(parts)
    ]


def gather_pieces(sources, held_ref, me, sems):
    each = held_ref.shape[0] // len(sources)
    return [
        pltpu.make_async_copy(
            ref.at[pl.ds(first, each)],
            held_ref.at[pl.ds((me ^ offset) * each, each)],
            sems.at[offset],
        )
        for ref, first, offset in sources
    ]


def far_first(peers):
    return sorted(range(1, peers // 2), key=lambda j: (-bin(j).count("1"), j))


def wave_offsets(peers):
    far = far_first(peers)
    return [0, 1, *[2 * j for j in far], *[2 * j + 1 for j in far]]


def piece_stores(source, offset, even_refs, odd_ref, sems):
    each = source.shape[0]
    stride = odd_ref.shape[0] // (sems.shape[0] // 2)
    if offset % 2:
        target = odd_ref.at[pl.ds((offset // 2) * stride, each)]
    else:
        target = even_refs[offset // 2].at[pl.ds(0, each)]
    return pltpu.make_async_copy(source, target, sems.at[offset])


def start_all(copies):
    for copy in copies:
        copy.start()


def wait_all(copies):
    for copy in copies:
        copy.wait()


def analyze_body(me_ref, order_ref, model_ref, *refs):
    even_refs, (odd_ref, block_ref, coeff_ref, got, put) = refs[:-5], refs[-5:]
    width = model_ref.shape[2]
    per_peer = even_refs[0].shape[0]
    peers = put.shape[0]
    me = me_ref[0]
    loads = fetch(model_ref, block_ref, got, got.shape[0])
    start_all(loads)
    row = lax.broadcasted_iota(jnp.int32, (BLK, BLK), 0)
    col = lax.broadcasted_iota(jnp.int32, (BLK, BLK), 1)
    level = jnp.ones_like(row)
    scale = jnp.full((BLK, width), BLK**-0.5, jnp.float32)
    wide_row = lax.broadcasted_iota(jnp.int32, (BLK, width), 0)
    size = 2
    while size < BLK:
        level = jnp.where(row >= size, size, level)
        scale = jnp.where(wide_row >= size, (size / BLK) ** 0.5, scale)
        size *= 2
    span = BLK // level
    inside = col - (row - level) * span
    sign = jnp.where(inside * 2 < span, 1.0, -1.0)
    sign = jnp.where((inside >= 0) & (inside < span), sign, 0.0)
    sign = jnp.where(row == 0, 1.0, sign).astype(jnp.bfloat16)
    both_signs = jnp.concatenate([sign, sign], axis=1)
    wait_all(loads)
    stores = []
    ends = []
    for rows in (block_ref[model_ref.shape[0] - 1, BLK - RIM :], block_ref[0, :RIM]):
        high = rows.astype(jnp.bfloat16)
        low = (rows - high.astype(jnp.float32)).astype(jnp.bfloat16)
        ends.append(jnp.concatenate([high, low], axis=0))
    for offset in [*range(1, peers, 2), *range(peers - 2, -1, -2)]:
        peer = (me ^ offset) * per_peer
        for q in range(per_peer):
            x = block_ref[order_ref[0, peer + q]]
            high = x.astype(jnp.bfloat16)
            low = (x - high.astype(jnp.float32)).astype(jnp.bfloat16)
            raw = jnp.dot(
                both_signs, jnp.concatenate([high, low], axis=0),
                preferred_element_type=jnp.float32,
            )
            coeff_ref[offset, q] = (raw * scale).astype(jnp.bfloat16)
        length = per_peer
        if offset % 2:
            coeff_ref[offset, per_peer] = jnp.where(me ^ offset == me + 1, ends[0], ends[1])
            length += 1
        source = coeff_ref.at[offset, pl.ds(0, length)]
        stores.append(piece_stores(source, offset, even_refs, odd_ref, put))
        stores[-1].start()
    wait_all(stores)


def piece_shapes(piece, peers, dtype, more=0):
    half = peers // 2
    return [jax.ShapeDtypeStruct(piece, dtype)] * half + [
        jax.ShapeDtypeStruct((half * (piece[0] + more), *piece[1:]), dtype)
    ]


def analyze(me, order, model_blocks, peers):
    blocks, _, width = model_blocks.shape
    piece = (blocks // peers, BLK, width)
    return pl.pallas_call(
        analyze_body,
        out_shape=piece_shapes(piece, peers, jnp.bfloat16, 1),
        in_specs=[SMEM_SPEC, SMEM_SPEC, ANY_SPEC],
        out_specs=[ANY_SPEC] * (peers // 2 + 1),
        scratch_shapes=[
            pltpu.VMEM((blocks, BLK, width), jnp.float32),
            pltpu.VMEM((peers, piece[0] + 1, *piece[1:]), jnp.bfloat16),
            pltpu.SemaphoreType.DMA((16,)),
            pltpu.SemaphoreType.DMA((peers,)),
        ],
        compiler_params=pltpu.CompilerParams(vmem_limit_bytes=LARGE),
        cost_estimate=pl.CostEstimate(
            flops=4 * blocks * BLK * BLK * width, bytes_accessed=6 * blocks * BLK * width,
            transcendentals=0,
        ),
        name="analyze",
    )(me, order, model_blocks)


def slot_loop(count, sens_ref, block_ref, sems, others, acc_ref, work, then=()):
    steps = sems.shape[0]
    each = sens_ref.shape[0] // steps

    def block_copy(step):
        part = pl.ds(step * each, each)
        return pltpu.make_async_copy(sens_ref.at[part], block_ref.at[part], sems.at[step])

    start_all(others)
    needed = (count + each - 1) // each

    @pl.loop(0, needed)
    def _(step):
        block_copy(step).start()

    acc_ref[...] = jnp.zeros_like(acc_ref)
    wait_all(others)
    start_all(then)

    @pl.loop(0, needed)
    def _(step):
        block_copy(step).wait()
        for k in range(each):
            slot = step * each + k
            work(slot, block_ref[slot], slot < count)


def forward_body(me_ref, rows_ref, cols_ref, count_ref, sens_ref, *refs):
    peers = len(refs) - 9
    wave_refs, (even_ref, odd_ref) = refs[:peers], refs[peers + 1 : peers + 3]
    block_ref, held_ref, acc_ref, sems, got, put = refs[peers + 3 :]
    row_blocks = acc_ref.shape[0] - 1
    each = row_blocks // peers
    me = me_ref[0]
    def work(slot, block, live):
        row = jnp.where(live, rows_ref[0, slot], row_blocks)
        acc_ref[row] += jnp.dot(
            block, held_ref[cols_ref[0, slot]], preferred_element_type=jnp.float32
        )

    sources = [(ref, 0, offset) for ref, offset in zip(wave_refs, wave_offsets(peers))]
    waves = gather_pieces(sources, held_ref, me, got)
    slot_loop(count_ref[0, 0], sens_ref, block_ref, sems, waves, acc_ref, work)
    stores = []
    for offset in [*range(1, peers, 2), *range(0, peers, 2)]:
        target = odd_ref if offset % 2 else even_ref
        stores.append(
            pltpu.make_async_copy(
                acc_ref.at[pl.ds((me ^ offset) * each, each)],
                target.at[pl.ds((offset // 2) * each, each)],
                put.at[offset],
            )
        )
    start_all(stores)
    wait_all(stores)


def forward(me, rows, cols, count, sens, waves, after):
    slots = sens.shape[0]
    peers = len(waves)
    blocks, width = after[1], sens.shape[2]
    half = (RB_DEV // 2, BLK, width)
    return pl.pallas_call(
        forward_body,
        out_shape=[jax.ShapeDtypeStruct(half, jnp.float32)] * 2,
        in_specs=[SMEM_SPEC] * 4 + [ANY_SPEC] * (1 + peers + 1),
        out_specs=[ANY_SPEC] * 2,
        scratch_shapes=[
            pltpu.VMEM(sens.shape, sens.dtype),
            pltpu.VMEM((blocks, BLK, width), jnp.bfloat16),
            pltpu.VMEM((RB_DEV + 1, BLK, width), jnp.float32),
            pltpu.SemaphoreType.DMA((slots // STEP,)),
            pltpu.SemaphoreType.DMA((peers,)),
            pltpu.SemaphoreType.DMA((peers,)),
        ],
        compiler_params=pltpu.CompilerParams(vmem_limit_bytes=LARGE),
        cost_estimate=pl.CostEstimate(
            flops=2 * slots * BLK * BLK * width, bytes_accessed=2 * slots * BLK * BLK,
            transcendentals=0,
        ),
        name="forward",
    )(me, rows, cols, count, sens, *waves, after[0])


def adjoint_body(me_ref, rows_ref, cols_ref, count_ref, sens_ref, even_in_ref, odd_in_ref,
                 *refs):
    out_refs, image_ref = refs[:-9], refs[-9]
    block_ref, held_ref, acc_ref, half_ref, sems, got, put, whole = refs[-8:]
    peers = put.shape[0]
    col_blocks = acc_ref.shape[0] - 1
    each = col_blocks // peers
    me = me_ref[0]
    def work(slot, block, live):
        col = jnp.where(live, cols_ref[0, slot], col_blocks)
        acc_ref[col] += lax.dot_general(
            block, held_ref[rows_ref[0, slot]], (((0,), (0,)), ((), ())),
            preferred_element_type=jnp.float32,
        )

    each_in = held_ref.shape[0] // peers
    sources = [
        (ref, i * each_in, 2 * j + odd)
        for i, j in enumerate([0, *far_first(peers)])
        for odd, ref in enumerate((even_in_ref, odd_in_ref))
    ]
    images = gather_pieces(sources, held_ref, me, got)
    stores = fetch(held_ref, image_ref, whole, whole.shape[0])
    slot_loop(count_ref[0, 0], sens_ref, block_ref, sems, images, acc_ref, work, stores)
    for offset in reversed(range(peers)):
        part = acc_ref[pl.ds((me ^ offset) * each, each)]
        half_ref[offset] = part.astype(half_ref.dtype)
        stores.append(
            pltpu.make_async_copy(half_ref.at[offset], out_refs[offset], put.at[offset])
        )
        stores[-1].start()
    wait_all(stores)


def adjoint(me, rows, cols, count, sens, even, odd, blocks, peers):
    slots = sens.shape[0]
    width = even.shape[2]
    piece = (blocks // peers, BLK, width)
    image = (RB_DEV, BLK, width)
    outs = pl.pallas_call(
        adjoint_body,
        out_shape=[jax.ShapeDtypeStruct(piece, jnp.bfloat16)] * peers
        + [jax.ShapeDtypeStruct(image, jnp.bfloat16)],
        in_specs=[SMEM_SPEC] * 4 + [ANY_SPEC] * 3,
        out_specs=[ANY_SPEC] * (peers + 1),
        scratch_shapes=[
            pltpu.VMEM(sens.shape, sens.dtype),
            pltpu.VMEM(image, jnp.bfloat16),
            pltpu.VMEM((blocks + 1, BLK, width), jnp.float32),
            pltpu.VMEM((peers, *piece), jnp.bfloat16),
            pltpu.SemaphoreType.DMA((slots // STEP,)),
            pltpu.SemaphoreType.DMA((peers,)),
            pltpu.SemaphoreType.DMA((peers,)),
            pltpu.SemaphoreType.DMA((4,)),
        ],
        compiler_params=pltpu.CompilerParams(vmem_limit_bytes=LARGE),
        cost_estimate=pl.CostEstimate(
            flops=2 * slots * BLK * BLK * width, bytes_accessed=2 * slots * BLK * BLK,
            transcendentals=0,
        ),
        name="adjoint",
    )(me, rows, cols, count, sens, even, odd)
    return outs[:-1], outs[-1]


def tile_value(near, face, window):
    span = lax.broadcasted_iota(jnp.int32, (2 * BLK, BLK), 0)
    center = lax.broadcasted_iota(jnp.int32, (2 * BLK, BLK), 1) + RIM
    mix = jnp.where(span == center, jnp.sum(face, axis=0, keepdims=True), 0.0)
    for k in range(4):
        mix = mix - jnp.where(span == near[k : k + 1], face[k : k + 1], 0.0)
    mix_high = mix.astype(jnp.bfloat16)
    mix_low = (mix - mix_high.astype(jnp.float32)).astype(jnp.bfloat16)
    near_high = window.astype(jnp.bfloat16)
    near_low = (window - near_high.astype(jnp.float32)).astype(jnp.bfloat16)
    return lax.dot_general(
        jnp.concatenate([mix_high, mix_high, mix_low], axis=0),
        jnp.concatenate([near_high, near_low, near_high], axis=0),
        (((0,), (0,)), ((), ())), preferred_element_type=jnp.float32,
    )


def smooth_body(offset_ref, model_ref, near_ref, weight_ref, after_ref,
                out_ref, ext_ref, value_ref, got, put):
    cells, width = model_ref.shape
    steps = put.shape[0]
    tiles = cells // BLK // steps
    each = cells // got.shape[0]
    loads = [
        pltpu.make_async_copy(
            model_ref.at[pl.ds(i * each, each)], ext_ref.at[pl.ds(RIM + i * each, each)], got.at[i]
        )
        for i in range(got.shape[0])
    ]
    start_all(loads)
    ext_ref[:RIM] = jnp.zeros((RIM, width), jnp.float32)
    ext_ref[RIM + cells :] = jnp.zeros((RIM, width), jnp.float32)
    wait_all(loads)

    def store(step):
        part = pl.ds(step * tiles * BLK, tiles * BLK)
        return pltpu.make_async_copy(value_ref.at[part], out_ref.at[part], put.at[step])

    @pl.loop(0, steps)
    def _(step):
        for t in range(tiles):
            start = pl.multiple_of((step * tiles + t) * BLK, BLK)
            near = near_ref[:, pl.ds(start, BLK)] - (offset_ref[0] + start)
            face = weight_ref[:, pl.ds(start, BLK)]
            window = ext_ref[pl.ds(start, 2 * BLK), :]
            value_ref[pl.ds(start, BLK), :] = tile_value(near, face, window)
        store(step).start()

    for step in range(steps):
        store(step).wait()


def smoothing(offset, model, neighbors, face_weight, after):
    cells, width = model.shape
    return pl.pallas_call(
        smooth_body,
        out_shape=jax.ShapeDtypeStruct((cells, width), jnp.float32),
        in_specs=[SMEM_SPEC, ANY_SPEC, VMEM_SPEC, VMEM_SPEC, ANY_SPEC],
        out_specs=ANY_SPEC,
        scratch_shapes=[
            pltpu.VMEM((cells + 2 * RIM, width), jnp.float32),
            pltpu.VMEM((cells, width), jnp.float32),
            pltpu.SemaphoreType.DMA((16,)),
            pltpu.SemaphoreType.DMA((8,)),
        ],
        compiler_params=pltpu.CompilerParams(vmem_limit_bytes=LARGE),
        cost_estimate=pl.CostEstimate(
            flops=24 * cells * BLK * width, bytes_accessed=16 * cells * width, transcendentals=0
        ),
        name="smoothing",
    )(offset, model, neighbors, face_weight, after)


def edges_body(me_ref, offset_ref, model_ref, near_ref, weight_ref, base_ref, after_ref, *refs):
    odd_refs, refs = refs[:-7], refs[-7:]
    out_ref, token_ref, window_ref, value_ref, ends_ref, got, put = refs
    token_ref[...] = jnp.zeros_like(token_ref)
    cells = model_ref.shape[0]
    each = odd_refs[-1].shape[0] - 1
    inner = 2 * BLK - RIM
    starts = (0, cells - BLK)
    me = me_ref[0]
    loads = [
        pltpu.make_async_copy(
            model_ref.at[pl.ds(0, inner)], window_ref.at[0, pl.ds(RIM, inner)], got.at[0]
        ),
        pltpu.make_async_copy(
            model_ref.at[pl.ds(cells - inner, inner)], window_ref.at[1, pl.ds(0, inner)], got.at[1]
        ),
    ]
    for i, odd_ref in enumerate(odd_refs):
        loads.append(
            pltpu.make_async_copy(odd_ref.at[each], ends_ref.at[i], got.at[2 + i])
        )
    start_all(loads)
    wait_all(loads)
    zero = jnp.zeros((RIM, model_ref.shape[1]), jnp.float32)
    low, high = zero, zero
    for i in range(len(odd_refs)):
        rows = ends_ref[i, :RIM].astype(jnp.float32) + ends_ref[i, RIM:].astype(jnp.float32)
        peer = me ^ (2 * i + 1)
        low = jnp.where(peer == me - 1, rows, low)
        high = jnp.where(peer == me + 1, rows, high)
    window_ref[0, :RIM] = low
    window_ref[1, inner:] = high
    stores = []
    for i, start in enumerate(starts):
        near = near_ref[:, start : start + BLK] - (offset_ref[0] + start)
        value_ref[i] = tile_value(near, weight_ref[:, start : start + BLK], window_ref[i])
        stores.append(
            pltpu.make_async_copy(value_ref.at[i], out_ref.at[pl.ds(start, BLK)], put.at[i])
        )
    start_all(stores)
    wait_all(stores)


def edges(me, offset, model, neighbors, face_weight, base, after, odd_pieces):
    width = model.shape[1]
    count = len(odd_pieces)
    return pl.pallas_call(
        edges_body,
        out_shape=[
            jax.ShapeDtypeStruct(base.shape, base.dtype),
            jax.ShapeDtypeStruct((8, BLK), jnp.float32),
        ],
        in_specs=[SMEM_SPEC, SMEM_SPEC, ANY_SPEC, VMEM_SPEC, VMEM_SPEC]
        + [ANY_SPEC] * (2 + count),
        out_specs=[ANY_SPEC, VMEM_SPEC],
        input_output_aliases={5: 0},
        scratch_shapes=[
            pltpu.VMEM((2, 2 * BLK, width), jnp.float32),
            pltpu.VMEM((2, BLK, width), jnp.float32),
            pltpu.VMEM((count, BLK, width), jnp.bfloat16),
            pltpu.SemaphoreType.DMA((2 + count,)),
            pltpu.SemaphoreType.DMA((2,)),
        ],
        compiler_params=pltpu.CompilerParams(vmem_limit_bytes=LARGE),
        cost_estimate=pl.CostEstimate(
            flops=24 * 2 * BLK * BLK * width, bytes_accessed=32 * BLK * width, transcendentals=0
        ),
        name="edges",
    )(me, offset, model, neighbors, face_weight, base, after, *odd_pieces)


def finish_body(me_ref, order_ref, basis_ref, even_ref, odd_ref, base_ref,
                out_ref, token_ref, block_ref, value_ref, got, put, *, offset):
    per_peer = odd_ref.shape[0]
    cols = 2 * per_peer
    fetches, stores = [], []
    for i in range(cols):
        peer = me_ref[0] ^ (offset + i // per_peer)
        cell = order_ref[0, peer * per_peer + i % per_peer]
        fetches.append(pltpu.make_async_copy(base_ref.at[cell], block_ref.at[i], got.at[i]))
        stores.append(pltpu.make_async_copy(block_ref.at[i], out_ref.at[cell], put.at[i]))
    start_all(fetches)
    for i in range(cols):
        wave = even_ref[i] if i < per_peer else odd_ref[i - per_peer]
        both = jnp.concatenate([wave, wave], axis=0)
        value_ref[i] = jnp.dot(basis_ref[...], both, preferred_element_type=jnp.float32)
    wait_all(fetches)
    block_ref[...] += value_ref[...]
    start_all(stores)
    token_ref[...] = jnp.zeros_like(token_ref)
    wait_all(stores)


def finish(me, order, even, odd, base, offset):
    width = odd.shape[2]
    cols = 2 * odd.shape[0]
    basis = haar_matrix(BLK).T.astype(np.float32)
    high = basis.astype(jnp.bfloat16)
    low = (basis - high.astype(np.float32)).astype(jnp.bfloat16)
    basis2 = jnp.asarray(np.concatenate([high, low], axis=1))
    return pl.pallas_call(
        lambda *refs: finish_body(*refs, offset=offset),
        out_shape=[
            jax.ShapeDtypeStruct(base.shape, base.dtype),
            jax.ShapeDtypeStruct((8, BLK), jnp.float32),
        ],
        in_specs=[SMEM_SPEC] * 2 + [VMEM_SPEC] * 3 + [ANY_SPEC],
        out_specs=[ANY_SPEC, VMEM_SPEC],
        input_output_aliases={5: 0},
        scratch_shapes=[
            pltpu.VMEM((cols, BLK, width), jnp.float32),
            pltpu.VMEM((cols, BLK, width), jnp.float32),
            pltpu.SemaphoreType.DMA((cols,)),
            pltpu.SemaphoreType.DMA((cols,)),
        ],
        compiler_params=pltpu.CompilerParams(vmem_limit_bytes=SMALL),
        cost_estimate=pl.CostEstimate(
            flops=4 * cols * BLK * BLK * width, bytes_accessed=10 * cols * BLK * width,
            transcendentals=0,
        ),
        name="finish",
    )(me, order, basis2, even, odd, base)


def merge_body(got_ref, mine_ref, after_ref, out_ref):
    total = got_ref[...].astype(jnp.float32) + mine_ref[...].astype(jnp.float32)
    out_ref[...] = total.astype(out_ref.dtype)


def merge(got, mine, after):
    return pl.pallas_call(
        merge_body,
        out_shape=jax.ShapeDtypeStruct(mine.shape, mine.dtype),
        in_specs=[VMEM_SPEC, VMEM_SPEC, ANY_SPEC],
        out_specs=VMEM_SPEC,
        compiler_params=pltpu.CompilerParams(vmem_limit_bytes=SMALL),
        cost_estimate=pl.CostEstimate(
            flops=mine.size, bytes_accessed=6 * mine.size, transcendentals=0
        ),
        name="merge",
    )(got, mine, after)


def pick_body(take_ref, got_ref, mine_ref, after_ref, token_ref, *out_refs):
    each = out_refs[0].shape[0]
    for i, out_ref in enumerate(out_refs):
        part = pl.ds(i * each, each)
        out_ref[...] = jnp.where(take_ref[0] > 0, got_ref[part], mine_ref[part])


def pick(take, got, mine, after, token, parts):
    shape = (mine.shape[0] // parts, *mine.shape[1:])
    return pl.pallas_call(
        pick_body,
        out_shape=[jax.ShapeDtypeStruct(shape, mine.dtype)] * parts,
        in_specs=[SMEM_SPEC, VMEM_SPEC, VMEM_SPEC, ANY_SPEC, ANY_SPEC],
        out_specs=[VMEM_SPEC] * parts,
        compiler_params=pltpu.CompilerParams(vmem_limit_bytes=SMALL),
        cost_estimate=pl.CostEstimate(
            flops=mine.size, bytes_accessed=6 * mine.size, transcendentals=0
        ),
        name="pick",
    )(take, got, mine, after, token)


def line_sums(parts, axis, after, deliver):
    count = lax.axis_size(axis)
    half = count // 2
    me = lax.axis_index(axis)
    stages = []
    for hop in range(half - 1):
        stages.append(([(hop, hop + 1), (count - 1 - hop, count - 2 - hop)], False))
    stages.append(([(half - 1, half), (half, half - 1)], False))
    for hop in range(half - 1):
        left, right = half - 1 - hop, half + hop
        stages.append(([(left, left - 1), (right, right + 1)], True))
    state = list(parts)
    got = [lax.ppermute(part, axis, stages[0][0]) for part in parts]
    for time in range(len(parts) + len(stages) - 1):
        for s, (pairs, outwards) in enumerate(stages):
            k = time - s
            if not 0 <= k < len(parts):
                continue
            last = s + 1 == len(stages)
            if outwards:
                take = (me == pairs[0][1]) | (me == pairs[1][1])
                take = take.astype(jnp.int32).reshape(1)
                if last:
                    after = deliver(k, take, got[k], state[k], after)
                else:
                    state[k] = jnp.where(take[0] > 0, got[k], state[k])
            else:
                state[k] = after = merge(got[k], state[k], after)
                if last:
                    take = jnp.zeros((1,), jnp.int32)
                    after = deliver(k, take, state[k], state[k], after)
            if not last:
                got[k] = lax.ppermute(state[k], axis, stages[s + 1][0])


def swap(piece, axis, offset):
    return lax.ppermute(piece, axis, [(c, c ^ offset) for c in range(lax.axis_size(axis))])


def local(model_dir, sens_blocks, blk_row, blk_col, blk_count, send_order, neighbors, face_weight):
    cell_count, width = model_dir.shape
    blocks = cell_count // BLK
    peers = lax.axis_size("cols")
    half = peers // 2
    per_peer = blocks // peers
    col = lax.axis_index("cols").astype(jnp.int32)
    me = col.reshape(1)
    offset = (col * cell_count - RIM).reshape(1)
    sens = sens_blocks[0]
    far = far_first(peers)

    *own, odd = analyze(me, send_order, model_dir.reshape(blocks, BLK, width), peers)
    partner = swap(odd, "cols", 1)
    direct = {j: swap(own[j], "cols", 2 * j) for j in far}
    passed = {
        j: swap(partner[j * (per_peer + 1) : (j + 1) * (per_peer + 1)], "cols", 2 * j)
        for j in far
    }
    waves = [own[0], partner, *[direct[j] for j in far], *[passed[j] for j in far]]
    smooth = smoothing(offset, model_dir, neighbors, face_weight, partner)

    even_rows, odd_rows = forward(
        me, blk_row, blk_col, blk_count, sens, waves, (smooth, blocks)
    )
    pair = (even_rows + swap(odd_rows, "cols", 1)).reshape(half, -1, BLK, width)
    to_send = pair.astype(jnp.bfloat16)
    shares = [swap(to_send[j], "cols", 2 * j) for j in far]
    total = pair[0] + sum(share.astype(jnp.float32) for share in shares)
    image_share = total.astype(jnp.bfloat16)
    even_image = jnp.concatenate(
        [image_share] + [swap(image_share, "cols", 2 * j) for j in far], axis=0
    )
    odd_image = swap(even_image, "cols", 1)
    partial_cols, image = adjoint(
        me, blk_row, blk_col, blk_count, sens, even_image, odd_image, blocks, peers
    )
    data_image = image.reshape(RB_DEV * BLK, width).astype(jnp.float32)
    smooth, first = edges(
        me, offset, model_dir, neighbors, face_weight, smooth, partial_cols[0],
        [partner, *[passed[j] for j in range(1, half)]],
    )
    normal = smooth.reshape(blocks, BLK, width)
    order = [2 * j + odd for j in far for odd in (1, 0)] + [1, 0]
    returned, waiting, tokens = {}, [], []

    def end_one():
        nonlocal normal
        j = waiting.pop(0)
        even, odd = returned[2 * j], returned[2 * j + 1]
        normal, token = finish(me, send_order, even, odd, normal, 2 * j)
        tokens.append(token)

    def deliver(k, take, got, mine, after):
        if k % 2 == 0 and k >= 4:
            end_one()
        token = tokens[-1] if tokens else after
        o = order[k]
        [total] = pick(take, got, mine, after, token, 1)
        returned[o] = swap(total, "cols", o) if o else total
        if k % 2:
            waiting.append(o // 2)
        return total

    line_sums([partial_cols[o] for o in order], "rows", first, deliver)
    while waiting:
        end_one()
    return (data_image, normal.reshape(cell_count, width))


def solution(mesh):
    placed = (
        P("cols", None),
        P("rows", "cols", None, None),
        P("rows", "cols"),
        P("rows", "cols"),
        P("rows", "cols"),
        P("cols", None),
        P(None, "cols"),
        P(None, "cols"),
    )
    return jax.shard_map(
        local,
        mesh=mesh,
        in_specs=placed,
        out_specs=(P("rows", None), P("cols", None)),
        check_vma=False,
    )
```

```python
import math

import jax
import jax.numpy as jnp
import numpy as np
from jax import lax
from jax.experimental import pallas as pl
from jax.experimental.pallas import tpu as pltpu
from jax.sharding import PartitionSpec as P

BLK = 128
RB_DEV = 32
RIM = 64
STEP = 16
MIB = 1 << 20
SMALL = 16 * MIB
LARGE = 56 * MIB
ANY_SPEC = pl.BlockSpec(memory_space=pl.ANY)
VMEM_SPEC = pl.BlockSpec(memory_space=pltpu.VMEM)
SMEM_SPEC = pl.BlockSpec(memory_space=pltpu.SMEM)


def haar_matrix(order_n):
    matrix = np.ones((1, 1))
    while matrix.shape[0] < order_n:
        length = matrix.shape[0]
        upper = np.kron(matrix, np.array([[1.0, 1.0]]))
        lower = np.kron(np.eye(length), np.array([[1.0, -1.0]]))
        matrix = np.concatenate([upper, lower], axis=0) / math.sqrt(2.0)
    return matrix


def fetch(source, target, sems, pieces):
    each = source.shape[0] // pieces
    parts = [pl.ds(i * each, each) for i in range(pieces)]
    return [
        pltpu.make_async_copy(source.at[part], target.at[part], sems.at[i])
        for i, part in enumerate(parts)
    ]


def gather_pieces(sources, held_ref, me, sems):
    each = held_ref.shape[0] // len(sources)
    return [
        pltpu.make_async_copy(
            ref.at[pl.ds(first, each)],
            held_ref.at[pl.ds((me ^ offset) * each, each)],
            sems.at[offset],
        )
        for ref, first, offset in sources
    ]


def far_first(peers):
    return sorted(range(1, peers // 2), key=lambda j: (-bin(j).count("1"), j))


def wave_offsets(peers):
    far = far_first(peers)
    return [0, 1, *[2 * j for j in far], *[2 * j + 1 for j in far]]


def piece_stores(source, offset, even_refs, odd_ref, sems):
    each = source.shape[0]
    stride = odd_ref.shape[0] // (sems.shape[0] // 2)
    if offset % 2:
        target = odd_ref.at[pl.ds((offset // 2) * stride, each)]
    else:
        target = even_refs[offset // 2].at[pl.ds(0, each)]
    return pltpu.make_async_copy(source, target, sems.at[offset])


def start_all(copies):
    for copy in copies:
        copy.start()


def wait_all(copies):
    for copy in copies:
        copy.wait()


def analyze_body(me_ref, order_ref, model_ref, *refs):
    even_refs, (odd_ref, block_ref, coeff_ref, got, put) = refs[:-5], refs[-5:]
    width = model_ref.shape[2]
    per_peer = even_refs[0].shape[0]
    peers = put.shape[0]
    me = me_ref[0]
    loads = fetch(model_ref, block_ref, got, got.shape[0])
    start_all(loads)
    row = lax.broadcasted_iota(jnp.int32, (BLK, BLK), 0)
    col = lax.broadcasted_iota(jnp.int32, (BLK, BLK), 1)
    level = jnp.ones_like(row)
    scale = jnp.full((BLK, width), BLK**-0.5, jnp.float32)
    wide_row = lax.broadcasted_iota(jnp.int32, (BLK, width), 0)
    size = 2
    while size < BLK:
        level = jnp.where(row >= size, size, level)
        scale = jnp.where(wide_row >= size, (size / BLK) ** 0.5, scale)
        size *= 2
    span = BLK // level
    inside = col - (row - level) * span
    sign = jnp.where(inside * 2 < span, 1.0, -1.0)
    sign = jnp.where((inside >= 0) & (inside < span), sign, 0.0)
    sign = jnp.where(row == 0, 1.0, sign).astype(jnp.bfloat16)
    both_signs = jnp.concatenate([sign, sign], axis=1)
    wait_all(loads)
    stores = []
    ends = []
    for rows in (block_ref[model_ref.shape[0] - 1, BLK - RIM :], block_ref[0, :RIM]):
        high = rows.astype(jnp.bfloat16)
        low = (rows - high.astype(jnp.float32)).astype(jnp.bfloat16)
        ends.append(jnp.concatenate([high, low], axis=0))
    for offset in [*range(1, peers, 2), *range(peers - 2, -1, -2)]:
        peer = (me ^ offset) * per_peer
        for q in range(per_peer):
            x = block_ref[order_ref[0, peer + q]]
            high = x.astype(jnp.bfloat16)
            low = (x - high.astype(jnp.float32)).astype(jnp.bfloat16)
            raw = jnp.dot(
                both_signs, jnp.concatenate([high, low], axis=0),
                preferred_element_type=jnp.float32,
            )
            coeff_ref[offset, q] = (raw * scale).astype(jnp.bfloat16)
        length = per_peer
        if offset % 2:
            coeff_ref[offset, per_peer] = jnp.where(me ^ offset == me + 1, ends[0], ends[1])
            length += 1
        source = coeff_ref.at[offset, pl.ds(0, length)]
        stores.append(piece_stores(source, offset, even_refs, odd_ref, put))
        stores[-1].start()
    wait_all(stores)


def piece_shapes(piece, peers, dtype, more=0):
    half = peers // 2
    return [jax.ShapeDtypeStruct(piece, dtype)] * half + [
        jax.ShapeDtypeStruct((half * (piece[0] + more), *piece[1:]), dtype)
    ]


def analyze(me, order, model_blocks, peers):
    blocks, _, width = model_blocks.shape
    piece = (blocks // peers, BLK, width)
    return pl.pallas_call(
        analyze_body,
        out_shape=piece_shapes(piece, peers, jnp.bfloat16, 1),
        in_specs=[SMEM_SPEC, SMEM_SPEC, ANY_SPEC],
        out_specs=[ANY_SPEC] * (peers // 2 + 1),
        scratch_shapes=[
            pltpu.VMEM((blocks, BLK, width), jnp.float32),
            pltpu.VMEM((peers, piece[0] + 1, *piece[1:]), jnp.bfloat16),
            pltpu.SemaphoreType.DMA((16,)),
            pltpu.SemaphoreType.DMA((peers,)),
        ],
        compiler_params=pltpu.CompilerParams(vmem_limit_bytes=LARGE),
        cost_estimate=pl.CostEstimate(
            flops=4 * blocks * BLK * BLK * width, bytes_accessed=6 * blocks * BLK * width,
            transcendentals=0,
        ),
        name="analyze",
    )(me, order, model_blocks)


def slot_loop(count, sens_ref, block_ref, sems, others, acc_ref, work, then=()):
    steps = sems.shape[0]
    each = sens_ref.shape[0] // steps

    def block_copy(step):
        part = pl.ds(step * each, each)
        return pltpu.make_async_copy(sens_ref.at[part], block_ref.at[part], sems.at[step])

    start_all(others)
    needed = (count + each - 1) // each

    @pl.loop(0, needed)
    def _(step):
        block_copy(step).start()

    acc_ref[...] = jnp.zeros_like(acc_ref)
    wait_all(others)
    start_all(then)

    @pl.loop(0, needed)
    def _(step):
        block_copy(step).wait()
        for k in range(each):
            slot = step * each + k
            work(slot, block_ref[slot], slot < count)


def forward_body(me_ref, rows_ref, cols_ref, count_ref, sens_ref, *refs):
    peers = len(refs) - 9
    wave_refs, (even_ref, odd_ref) = refs[:peers], refs[peers + 1 : peers + 3]
    block_ref, held_ref, acc_ref, sems, got, put = refs[peers + 3 :]
    row_blocks = acc_ref.shape[0] - 1
    each = row_blocks // peers
    me = me_ref[0]
    def work(slot, block, live):
        row = jnp.where(live, rows_ref[0, slot], row_blocks)
        acc_ref[row] += jnp.dot(
            block, held_ref[cols_ref[0, slot]], preferred_element_type=jnp.float32
        )

    sources = [(ref, 0, offset) for ref, offset in zip(wave_refs, wave_offsets(peers))]
    waves = gather_pieces(sources, held_ref, me, got)
    slot_loop(count_ref[0, 0], sens_ref, block_ref, sems, waves, acc_ref, work)
    stores = []
    for offset in [*range(1, peers, 2), *range(0, peers, 2)]:
        target = odd_ref if offset % 2 else even_ref
        stores.append(
            pltpu.make_async_copy(
                acc_ref.at[pl.ds((me ^ offset) * each, each)],
                target.at[pl.ds((offset // 2) * each, each)],
                put.at[offset],
            )
        )
    start_all(stores)
    wait_all(stores)


def forward(me, rows, cols, count, sens, waves, after):
    slots = sens.shape[0]
    peers = len(waves)
    blocks, width = after[1], sens.shape[2]
    half = (RB_DEV // 2, BLK, width)
    return pl.pallas_call(
        forward_body,
        out_shape=[jax.ShapeDtypeStruct(half, jnp.float32)] * 2,
        in_specs=[SMEM_SPEC] * 4 + [ANY_SPEC] * (1 + peers + 1),
        out_specs=[ANY_SPEC] * 2,
        scratch_shapes=[
            pltpu.VMEM(sens.shape, sens.dtype),
            pltpu.VMEM((blocks, BLK, width), jnp.bfloat16),
            pltpu.VMEM((RB_DEV + 1, BLK, width), jnp.float32),
            pltpu.SemaphoreType.DMA((slots // STEP,)),
            pltpu.SemaphoreType.DMA((peers,)),
            pltpu.SemaphoreType.DMA((peers,)),
        ],
        compiler_params=pltpu.CompilerParams(vmem_limit_bytes=LARGE),
        cost_estimate=pl.CostEstimate(
            flops=2 * slots * BLK * BLK * width, bytes_accessed=2 * slots * BLK * BLK,
            transcendentals=0,
        ),
        name="forward",
    )(me, rows, cols, count, sens, *waves, after[0])


def adjoint_body(me_ref, rows_ref, cols_ref, count_ref, sens_ref, even_in_ref, odd_in_ref,
                 *refs):
    out_refs, image_ref = refs[:-9], refs[-9]
    block_ref, held_ref, acc_ref, half_ref, sems, got, put, whole = refs[-8:]
    peers = put.shape[0]
    col_blocks = acc_ref.shape[0] - 1
    each = col_blocks // peers
    me = me_ref[0]
    def work(slot, block, live):
        col = jnp.where(live, cols_ref[0, slot], col_blocks)
        acc_ref[col] += lax.dot_general(
            block, held_ref[rows_ref[0, slot]], (((0,), (0,)), ((), ())),
            preferred_element_type=jnp.float32,
        )

    each_in = held_ref.shape[0] // peers
    sources = [
        (ref, i * each_in, 2 * j + odd)
        for i, j in enumerate([0, *far_first(peers)])
        for odd, ref in enumerate((even_in_ref, odd_in_ref))
    ]
    images = gather_pieces(sources, held_ref, me, got)
    stores = fetch(held_ref, image_ref, whole, whole.shape[0])
    slot_loop(count_ref[0, 0], sens_ref, block_ref, sems, images, acc_ref, work, stores)
    for offset in reversed(range(peers)):
        part = acc_ref[pl.ds((me ^ offset) * each, each)]
        half_ref[offset] = part.astype(half_ref.dtype)
        target = out_refs[offset // 2].at[pl.ds(offset % 2 * each, each)]
        stores.append(pltpu.make_async_copy(half_ref.at[offset], target, put.at[offset]))
        stores[-1].start()
    wait_all(stores)


def adjoint(me, rows, cols, count, sens, even, odd, blocks, peers):
    slots = sens.shape[0]
    width = even.shape[2]
    piece = (blocks // peers, BLK, width)
    image = (RB_DEV, BLK, width)
    outs = pl.pallas_call(
        adjoint_body,
        out_shape=[jax.ShapeDtypeStruct((2 * piece[0], *piece[1:]), jnp.bfloat16)] * (peers // 2)
        + [jax.ShapeDtypeStruct(image, jnp.bfloat16)],
        in_specs=[SMEM_SPEC] * 4 + [ANY_SPEC] * 3,
        out_specs=[ANY_SPEC] * (peers // 2 + 1),
        scratch_shapes=[
            pltpu.VMEM(sens.shape, sens.dtype),
            pltpu.VMEM(image, jnp.bfloat16),
            pltpu.VMEM((blocks + 1, BLK, width), jnp.float32),
            pltpu.VMEM((peers, *piece), jnp.bfloat16),
            pltpu.SemaphoreType.DMA((slots // STEP,)),
            pltpu.SemaphoreType.DMA((peers,)),
            pltpu.SemaphoreType.DMA((peers,)),
            pltpu.SemaphoreType.DMA((4,)),
        ],
        compiler_params=pltpu.CompilerParams(vmem_limit_bytes=LARGE),
        cost_estimate=pl.CostEstimate(
            flops=2 * slots * BLK * BLK * width, bytes_accessed=2 * slots * BLK * BLK,
            transcendentals=0,
        ),
        name="adjoint",
    )(me, rows, cols, count, sens, even, odd)
    return outs[:-1], outs[-1]


def tile_value(near, face, window):
    span = lax.broadcasted_iota(jnp.int32, (2 * BLK, BLK), 0)
    center = lax.broadcasted_iota(jnp.int32, (2 * BLK, BLK), 1) + RIM
    mix = jnp.where(span == center, jnp.sum(face, axis=0, keepdims=True), 0.0)
    for k in range(4):
        mix = mix - jnp.where(span == near[k : k + 1], face[k : k + 1], 0.0)
    mix_high = mix.astype(jnp.bfloat16)
    mix_low = (mix - mix_high.astype(jnp.float32)).astype(jnp.bfloat16)
    near_high = window.astype(jnp.bfloat16)
    near_low = (window - near_high.astype(jnp.float32)).astype(jnp.bfloat16)
    return lax.dot_general(
        jnp.concatenate([mix_high, mix_high, mix_low], axis=0),
        jnp.concatenate([near_high, near_low, near_high], axis=0),
        (((0,), (0,)), ((), ())), preferred_element_type=jnp.float32,
    )


def smooth_body(offset_ref, model_ref, near_ref, weight_ref, after_ref,
                out_ref, ext_ref, value_ref, got, put):
    cells, width = model_ref.shape
    steps = put.shape[0]
    tiles = cells // BLK // steps
    each = cells // got.shape[0]
    loads = [
        pltpu.make_async_copy(
            model_ref.at[pl.ds(i * each, each)], ext_ref.at[pl.ds(RIM + i * each, each)], got.at[i]
        )
        for i in range(got.shape[0])
    ]
    start_all(loads)
    ext_ref[:RIM] = jnp.zeros((RIM, width), jnp.float32)
    ext_ref[RIM + cells :] = jnp.zeros((RIM, width), jnp.float32)
    wait_all(loads)

    def store(step):
        part = pl.ds(step * tiles * BLK, tiles * BLK)
        return pltpu.make_async_copy(value_ref.at[part], out_ref.at[part], put.at[step])

    @pl.loop(0, steps)
    def _(step):
        for t in range(tiles):
            start = pl.multiple_of((step * tiles + t) * BLK, BLK)
            near = near_ref[:, pl.ds(start, BLK)] - (offset_ref[0] + start)
            face = weight_ref[:, pl.ds(start, BLK)]
            window = ext_ref[pl.ds(start, 2 * BLK), :]
            value_ref[pl.ds(start, BLK), :] = tile_value(near, face, window)
        store(step).start()

    for step in range(steps):
        store(step).wait()


def smoothing(offset, model, neighbors, face_weight, after):
    cells, width = model.shape
    return pl.pallas_call(
        smooth_body,
        out_shape=jax.ShapeDtypeStruct((cells, width), jnp.float32),
        in_specs=[SMEM_SPEC, ANY_SPEC, VMEM_SPEC, VMEM_SPEC, ANY_SPEC],
        out_specs=ANY_SPEC,
        scratch_shapes=[
            pltpu.VMEM((cells + 2 * RIM, width), jnp.float32),
            pltpu.VMEM((cells, width), jnp.float32),
            pltpu.SemaphoreType.DMA((16,)),
            pltpu.SemaphoreType.DMA((8,)),
        ],
        compiler_params=pltpu.CompilerParams(vmem_limit_bytes=LARGE),
        cost_estimate=pl.CostEstimate(
            flops=24 * cells * BLK * width, bytes_accessed=16 * cells * width, transcendentals=0
        ),
        name="smoothing",
    )(offset, model, neighbors, face_weight, after)


def edges_body(me_ref, offset_ref, model_ref, near_ref, weight_ref, base_ref, after_ref, *refs):
    odd_refs, refs = refs[:-7], refs[-7:]
    out_ref, token_ref, window_ref, value_ref, ends_ref, got, put = refs
    token_ref[...] = jnp.zeros_like(token_ref)
    cells = model_ref.shape[0]
    each = odd_refs[-1].shape[0] - 1
    inner = 2 * BLK - RIM
    starts = (0, cells - BLK)
    me = me_ref[0]
    loads = [
        pltpu.make_async_copy(
            model_ref.at[pl.ds(0, inner)], window_ref.at[0, pl.ds(RIM, inner)], got.at[0]
        ),
        pltpu.make_async_copy(
            model_ref.at[pl.ds(cells - inner, inner)], window_ref.at[1, pl.ds(0, inner)], got.at[1]
        ),
    ]
    for i, odd_ref in enumerate(odd_refs):
        loads.append(
            pltpu.make_async_copy(odd_ref.at[each], ends_ref.at[i], got.at[2 + i])
        )
    start_all(loads)
    wait_all(loads)
    zero = jnp.zeros((RIM, model_ref.shape[1]), jnp.float32)
    low, high = zero, zero
    for i in range(len(odd_refs)):
        rows = ends_ref[i, :RIM].astype(jnp.float32) + ends_ref[i, RIM:].astype(jnp.float32)
        peer = me ^ (2 * i + 1)
        low = jnp.where(peer == me - 1, rows, low)
        high = jnp.where(peer == me + 1, rows, high)
    window_ref[0, :RIM] = low
    window_ref[1, inner:] = high
    stores = []
    for i, start in enumerate(starts):
        near = near_ref[:, start : start + BLK] - (offset_ref[0] + start)
        value_ref[i] = tile_value(near, weight_ref[:, start : start + BLK], window_ref[i])
        stores.append(
            pltpu.make_async_copy(value_ref.at[i], out_ref.at[pl.ds(start, BLK)], put.at[i])
        )
    start_all(stores)
    wait_all(stores)


def edges(me, offset, model, neighbors, face_weight, base, after, odd_pieces):
    width = model.shape[1]
    count = len(odd_pieces)
    return pl.pallas_call(
        edges_body,
        out_shape=[
            jax.ShapeDtypeStruct(base.shape, base.dtype),
            jax.ShapeDtypeStruct((8, BLK), jnp.float32),
        ],
        in_specs=[SMEM_SPEC, SMEM_SPEC, ANY_SPEC, VMEM_SPEC, VMEM_SPEC]
        + [ANY_SPEC] * (2 + count),
        out_specs=[ANY_SPEC, VMEM_SPEC],
        input_output_aliases={5: 0},
        scratch_shapes=[
            pltpu.VMEM((2, 2 * BLK, width), jnp.float32),
            pltpu.VMEM((2, BLK, width), jnp.float32),
            pltpu.VMEM((count, BLK, width), jnp.bfloat16),
            pltpu.SemaphoreType.DMA((2 + count,)),
            pltpu.SemaphoreType.DMA((2,)),
        ],
        compiler_params=pltpu.CompilerParams(vmem_limit_bytes=LARGE),
        cost_estimate=pl.CostEstimate(
            flops=24 * 2 * BLK * BLK * width, bytes_accessed=32 * BLK * width, transcendentals=0
        ),
        name="edges",
    )(me, offset, model, neighbors, face_weight, base, after, *odd_pieces)


def finish_body(me_ref, order_ref, basis_ref, even_ref, odd_ref, base_ref,
                out_ref, token_ref, block_ref, value_ref, got, put, *, offset):
    per_peer = odd_ref.shape[0]
    cols = 2 * per_peer
    fetches, stores = [], []
    for i in range(cols):
        peer = me_ref[0] ^ (offset + i // per_peer)
        cell = order_ref[0, peer * per_peer + i % per_peer]
        fetches.append(pltpu.make_async_copy(base_ref.at[cell], block_ref.at[i], got.at[i]))
        stores.append(pltpu.make_async_copy(block_ref.at[i], out_ref.at[cell], put.at[i]))
    start_all(fetches)
    for i in range(cols):
        wave = even_ref[i] if i < per_peer else odd_ref[i - per_peer]
        both = jnp.concatenate([wave, wave], axis=0)
        value_ref[i] = jnp.dot(basis_ref[...], both, preferred_element_type=jnp.float32)
    wait_all(fetches)
    block_ref[...] += value_ref[...]
    start_all(stores)
    token_ref[...] = jnp.zeros_like(token_ref)
    wait_all(stores)


def finish(me, order, even, odd, base, offset):
    width = odd.shape[2]
    cols = 2 * odd.shape[0]
    basis = haar_matrix(BLK).T.astype(np.float32)
    high = basis.astype(jnp.bfloat16)
    low = (basis - high.astype(np.float32)).astype(jnp.bfloat16)
    basis2 = jnp.asarray(np.concatenate([high, low], axis=1))
    return pl.pallas_call(
        lambda *refs: finish_body(*refs, offset=offset),
        out_shape=[
            jax.ShapeDtypeStruct(base.shape, base.dtype),
            jax.ShapeDtypeStruct((8, BLK), jnp.float32),
        ],
        in_specs=[SMEM_SPEC] * 2 + [VMEM_SPEC] * 3 + [ANY_SPEC],
        out_specs=[ANY_SPEC, VMEM_SPEC],
        input_output_aliases={5: 0},
        scratch_shapes=[
            pltpu.VMEM((cols, BLK, width), jnp.float32),
            pltpu.VMEM((cols, BLK, width), jnp.float32),
            pltpu.SemaphoreType.DMA((cols,)),
            pltpu.SemaphoreType.DMA((cols,)),
        ],
        compiler_params=pltpu.CompilerParams(vmem_limit_bytes=SMALL),
        cost_estimate=pl.CostEstimate(
            flops=4 * cols * BLK * BLK * width, bytes_accessed=10 * cols * BLK * width,
            transcendentals=0,
        ),
        name="finish",
    )(me, order, basis2, even, odd, base)


def merge_body(got_ref, mine_ref, after_ref, out_ref):
    total = got_ref[...].astype(jnp.float32) + mine_ref[...].astype(jnp.float32)
    out_ref[...] = total.astype(out_ref.dtype)


def merge(got, mine, after):
    return pl.pallas_call(
        merge_body,
        out_shape=jax.ShapeDtypeStruct(mine.shape, mine.dtype),
        in_specs=[VMEM_SPEC, VMEM_SPEC, ANY_SPEC],
        out_specs=VMEM_SPEC,
        compiler_params=pltpu.CompilerParams(vmem_limit_bytes=SMALL),
        cost_estimate=pl.CostEstimate(
            flops=mine.size, bytes_accessed=6 * mine.size, transcendentals=0
        ),
        name="merge",
    )(got, mine, after)


def pick_body(take_ref, got_ref, mine_ref, after_ref, token_ref, *out_refs):
    each = out_refs[0].shape[0]
    for i, out_ref in enumerate(out_refs):
        part = pl.ds(i * each, each)
        out_ref[...] = jnp.where(take_ref[0] > 0, got_ref[part], mine_ref[part])


def pick(take, got, mine, after, token, parts):
    shape = (mine.shape[0] // parts, *mine.shape[1:])
    return pl.pallas_call(
        pick_body,
        out_shape=[jax.ShapeDtypeStruct(shape, mine.dtype)] * parts,
        in_specs=[SMEM_SPEC, VMEM_SPEC, VMEM_SPEC, ANY_SPEC, ANY_SPEC],
        out_specs=[VMEM_SPEC] * parts,
        compiler_params=pltpu.CompilerParams(vmem_limit_bytes=SMALL),
        cost_estimate=pl.CostEstimate(
            flops=mine.size, bytes_accessed=6 * mine.size, transcendentals=0
        ),
        name="pick",
    )(take, got, mine, after, token)


def second_half_body(whole_ref, after_ref, out_ref):
    out_ref[...] = whole_ref[out_ref.shape[0] :]


def second_half(whole, after):
    shape = (whole.shape[0] // 2, *whole.shape[1:])
    return pl.pallas_call(
        second_half_body,
        out_shape=jax.ShapeDtypeStruct(shape, whole.dtype),
        in_specs=[VMEM_SPEC, ANY_SPEC],
        out_specs=VMEM_SPEC,
        compiler_params=pltpu.CompilerParams(vmem_limit_bytes=SMALL),
        cost_estimate=pl.CostEstimate(
            flops=0, bytes_accessed=2 * whole.size, transcendentals=0
        ),
        name="second_half",
    )(whole, after)


def line_sums(parts, axis, after, deliver):
    count = lax.axis_size(axis)
    half = count // 2
    me = lax.axis_index(axis)
    stages = []
    for hop in range(half - 1):
        stages.append(([(hop, hop + 1), (count - 1 - hop, count - 2 - hop)], False))
    stages.append(([(half - 1, half), (half, half - 1)], False))
    for hop in range(half - 1):
        left, right = half - 1 - hop, half + hop
        stages.append(([(left, left - 1), (right, right + 1)], True))
    state = list(parts)
    got = [lax.ppermute(part, axis, stages[0][0]) for part in parts]
    for time in range(len(parts) + len(stages) - 1):
        for s, (pairs, outwards) in enumerate(stages):
            k = time - s
            if not 0 <= k < len(parts):
                continue
            last = s + 1 == len(stages)
            if outwards:
                take = (me == pairs[0][1]) | (me == pairs[1][1])
                take = take.astype(jnp.int32).reshape(1)
                if last:
                    after = deliver(k, take, got[k], state[k], after)
                else:
                    state[k] = jnp.where(take[0] > 0, got[k], state[k])
            else:
                state[k] = after = merge(got[k], state[k], after)
                if last:
                    take = jnp.zeros((1,), jnp.int32)
                    after = deliver(k, take, state[k], state[k], after)
            if not last:
                got[k] = lax.ppermute(state[k], axis, stages[s + 1][0])


def swap(piece, axis, offset):
    return lax.ppermute(piece, axis, [(c, c ^ offset) for c in range(lax.axis_size(axis))])


def local(model_dir, sens_blocks, blk_row, blk_col, blk_count, send_order, neighbors, face_weight):
    cell_count, width = model_dir.shape
    blocks = cell_count // BLK
    peers = lax.axis_size("cols")
    half = peers // 2
    per_peer = blocks // peers
    col = lax.axis_index("cols").astype(jnp.int32)
    me = col.reshape(1)
    offset = (col * cell_count - RIM).reshape(1)
    sens = sens_blocks[0]
    far = far_first(peers)

    *own, odd = analyze(me, send_order, model_dir.reshape(blocks, BLK, width), peers)
    partner = swap(odd, "cols", 1)
    direct = {j: swap(own[j], "cols", 2 * j) for j in far}
    passed = {
        j: swap(partner[j * (per_peer + 1) : (j + 1) * (per_peer + 1)], "cols", 2 * j)
        for j in far
    }
    waves = [own[0], partner, *[direct[j] for j in far], *[passed[j] for j in far]]
    smooth = smoothing(offset, model_dir, neighbors, face_weight, partner)

    even_rows, odd_rows = forward(
        me, blk_row, blk_col, blk_count, sens, waves, (smooth, blocks)
    )
    pair = (even_rows + swap(odd_rows, "cols", 1)).reshape(half, -1, BLK, width)
    to_send = pair.astype(jnp.bfloat16)
    shares = [swap(to_send[j], "cols", 2 * j) for j in far]
    total = pair[0] + sum(share.astype(jnp.float32) for share in shares)
    image_share = total.astype(jnp.bfloat16)
    even_image = jnp.concatenate(
        [image_share] + [swap(image_share, "cols", 2 * j) for j in far], axis=0
    )
    odd_image = swap(even_image, "cols", 1)
    partial_cols, image = adjoint(
        me, blk_row, blk_col, blk_count, sens, even_image, odd_image, blocks, peers
    )
    data_image = image.reshape(RB_DEV * BLK, width).astype(jnp.float32)
    smooth, first = edges(
        me, offset, model_dir, neighbors, face_weight, smooth, partial_cols[0],
        [partner, *[passed[j] for j in range(1, half)]],
    )
    normal = smooth.reshape(blocks, BLK, width)
    order = [*far, 0]
    waiting, tokens = [], []

    def end_one(place):
        nonlocal normal
        even, other, j = waiting.pop(place)
        if other is None:
            other = swap(second_half(even, tokens[-1]), "cols", 1)
        normal, token = finish(me, send_order, even, other, normal, 2 * j)
        tokens.append(token)

    def deliver(k, take, got, mine, after):
        if k >= 2:
            end_one(0)
        token = tokens[-1] if tokens else after
        j = order[k]
        if j == 0:
            even, other = pick(take, got, mine, after, token, 2)
            waiting.append((even, swap(other, "cols", 1), j))
            return even
        [total] = pick(take, got, mine, after, token, 1)
        even = swap(total, "cols", 2 * j)
        other = None if k == half - 2 else swap(even[per_peer:], "cols", 1)
        waiting.append((even, other, j))
        return total

    line_sums([partial_cols[j] for j in order], "rows", first, deliver)
    while waiting:
        end_one(-1)
    return (data_image, normal.reshape(cell_count, width))


def solution(mesh):
    placed = (
        P("cols", None),
        P("rows", "cols", None, None),
        P("rows", "cols"),
        P("rows", "cols"),
        P("rows", "cols"),
        P("cols", None),
        P(None, "cols"),
        P(None, "cols"),
    )
    return jax.shard_map(
        local,
        mesh=mesh,
        in_specs=placed,
        out_specs=(P("rows", None), P("cols", None)),
        check_vma=False,
    )
```

```python
import math

import jax
import jax.numpy as jnp
import numpy as np
from jax import lax
from jax.experimental import pallas as pl
from jax.experimental.pallas import tpu as pltpu
from jax.sharding import PartitionSpec as P

BLK = 128
RB_DEV = 32
RIM = 64
STEP = 16
MIB = 1 << 20
SMALL = 16 * MIB
LARGE = 56 * MIB
ANY_SPEC = pl.BlockSpec(memory_space=pl.ANY)
VMEM_SPEC = pl.BlockSpec(memory_space=pltpu.VMEM)
SMEM_SPEC = pl.BlockSpec(memory_space=pltpu.SMEM)


def haar_matrix(order_n):
    matrix = np.ones((1, 1))
    while matrix.shape[0] < order_n:
        length = matrix.shape[0]
        upper = np.kron(matrix, np.array([[1.0, 1.0]]))
        lower = np.kron(np.eye(length), np.array([[1.0, -1.0]]))
        matrix = np.concatenate([upper, lower], axis=0) / math.sqrt(2.0)
    return matrix


def fetch(source, target, sems, pieces):
    each = source.shape[0] // pieces
    parts = [pl.ds(i * each, each) for i in range(pieces)]
    return [
        pltpu.make_async_copy(source.at[part], target.at[part], sems.at[i])
        for i, part in enumerate(parts)
    ]


def gather_pieces(sources, held_ref, me, sems):
    each = held_ref.shape[0] // len(sources)
    return [
        pltpu.make_async_copy(
            ref.at[pl.ds(first, each)],
            held_ref.at[pl.ds((me ^ offset) * each, each)],
            sems.at[offset],
        )
        for ref, first, offset in sources
    ]


def far_first(peers):
    return sorted(range(1, peers // 2), key=lambda j: (-bin(j).count("1"), j))


def wave_offsets(peers):
    far = far_first(peers)
    return [0, 1, *[2 * j for j in far], *[2 * j + 1 for j in far]]


def piece_stores(source, offset, even_refs, odd_ref, sems):
    each = source.shape[0]
    stride = odd_ref.shape[0] // (sems.shape[0] // 2)
    if offset % 2:
        target = odd_ref.at[pl.ds((offset // 2) * stride, each)]
    else:
        target = even_refs[offset // 2].at[pl.ds(0, each)]
    return pltpu.make_async_copy(source, target, sems.at[offset])


def start_all(copies):
    for copy in copies:
        copy.start()


def wait_all(copies):
    for copy in copies:
        copy.wait()


def analyze_body(me_ref, order_ref, model_ref, *refs):
    even_refs, (odd_ref, block_ref, coeff_ref, got, put) = refs[:-5], refs[-5:]
    width = model_ref.shape[2]
    per_peer = even_refs[0].shape[0]
    peers = put.shape[0]
    me = me_ref[0]
    loads = fetch(model_ref, block_ref, got, got.shape[0])
    start_all(loads)
    row = lax.broadcasted_iota(jnp.int32, (BLK, BLK), 0)
    col = lax.broadcasted_iota(jnp.int32, (BLK, BLK), 1)
    level = jnp.ones_like(row)
    scale = jnp.full((BLK, width), BLK**-0.5, jnp.float32)
    wide_row = lax.broadcasted_iota(jnp.int32, (BLK, width), 0)
    size = 2
    while size < BLK:
        level = jnp.where(row >= size, size, level)
        scale = jnp.where(wide_row >= size, (size / BLK) ** 0.5, scale)
        size *= 2
    span = BLK // level
    inside = col - (row - level) * span
    sign = jnp.where(inside * 2 < span, 1.0, -1.0)
    sign = jnp.where((inside >= 0) & (inside < span), sign, 0.0)
    sign = jnp.where(row == 0, 1.0, sign).astype(jnp.bfloat16)
    both_signs = jnp.concatenate([sign, sign], axis=1)
    wait_all(loads)
    stores = []
    ends = []
    for rows in (block_ref[model_ref.shape[0] - 1, BLK - RIM :], block_ref[0, :RIM]):
        high = rows.astype(jnp.bfloat16)
        low = (rows - high.astype(jnp.float32)).astype(jnp.bfloat16)
        ends.append(jnp.concatenate([high, low], axis=0))
    for offset in [*range(1, peers, 2), *range(peers - 2, -1, -2)]:
        peer = (me ^ offset) * per_peer
        for q in range(per_peer):
            x = block_ref[order_ref[0, peer + q]]
            high = x.astype(jnp.bfloat16)
            low = (x - high.astype(jnp.float32)).astype(jnp.bfloat16)
            raw = jnp.dot(
                both_signs, jnp.concatenate([high, low], axis=0),
                preferred_element_type=jnp.float32,
            )
            coeff_ref[offset, q] = (raw * scale).astype(jnp.bfloat16)
        length = per_peer
        if offset % 2:
            coeff_ref[offset, per_peer] = jnp.where(me ^ offset == me + 1, ends[0], ends[1])
            length += 1
        source = coeff_ref.at[offset, pl.ds(0, length)]
        stores.append(piece_stores(source, offset, even_refs, odd_ref, put))
        stores[-1].start()
    wait_all(stores)


def piece_shapes(piece, peers, dtype, more=0):
    half = peers // 2
    return [jax.ShapeDtypeStruct(piece, dtype)] * half + [
        jax.ShapeDtypeStruct((half * (piece[0] + more), *piece[1:]), dtype)
    ]


def analyze(me, order, model_blocks, peers):
    blocks, _, width = model_blocks.shape
    piece = (blocks // peers, BLK, width)
    return pl.pallas_call(
        analyze_body,
        out_shape=piece_shapes(piece, peers, jnp.bfloat16, 1),
        in_specs=[SMEM_SPEC, SMEM_SPEC, ANY_SPEC],
        out_specs=[ANY_SPEC] * (peers // 2 + 1),
        scratch_shapes=[
            pltpu.VMEM((blocks, BLK, width), jnp.float32),
            pltpu.VMEM((peers, piece[0] + 1, *piece[1:]), jnp.bfloat16),
            pltpu.SemaphoreType.DMA((16,)),
            pltpu.SemaphoreType.DMA((peers,)),
        ],
        compiler_params=pltpu.CompilerParams(vmem_limit_bytes=LARGE),
        cost_estimate=pl.CostEstimate(
            flops=4 * blocks * BLK * BLK * width, bytes_accessed=6 * blocks * BLK * width,
            transcendentals=0,
        ),
        name="analyze",
    )(me, order, model_blocks)


def slot_loop(count, sens_ref, block_ref, sems, others, acc_ref, work, then=()):
    steps = sems.shape[0]
    each = sens_ref.shape[0] // steps

    def block_copy(step):
        part = pl.ds(step * each, each)
        return pltpu.make_async_copy(sens_ref.at[part], block_ref.at[part], sems.at[step])

    start_all(others)
    needed = (count + each - 1) // each

    @pl.loop(0, needed)
    def _(step):
        block_copy(step).start()

    acc_ref[...] = jnp.zeros_like(acc_ref)
    wait_all(others)
    start_all(then)

    @pl.loop(0, needed)
    def _(step):
        block_copy(step).wait()
        for k in range(each):
            slot = step * each + k
            work(slot, block_ref[slot], slot < count)


def forward_body(me_ref, rows_ref, cols_ref, count_ref, sens_ref, *refs):
    peers = len(refs) - 9
    wave_refs, (even_ref, odd_ref) = refs[:peers], refs[peers + 1 : peers + 3]
    block_ref, held_ref, acc_ref, sems, got, put = refs[peers + 3 :]
    row_blocks = acc_ref.shape[0] - 1
    each = row_blocks // peers
    me = me_ref[0]
    def work(slot, block, live):
        row = jnp.where(live, rows_ref[0, slot], row_blocks)
        acc_ref[row] += jnp.dot(
            block, held_ref[cols_ref[0, slot]], preferred_element_type=jnp.float32
        )

    sources = [(ref, 0, offset) for ref, offset in zip(wave_refs, wave_offsets(peers))]
    waves = gather_pieces(sources, held_ref, me, got)
    slot_loop(count_ref[0, 0], sens_ref, block_ref, sems, waves, acc_ref, work)
    stores = []
    for offset in [*range(1, peers, 2), *range(0, peers, 2)]:
        target = odd_ref if offset % 2 else even_ref
        stores.append(
            pltpu.make_async_copy(
                acc_ref.at[pl.ds((me ^ offset) * each, each)],
                target.at[pl.ds((offset // 2) * each, each)],
                put.at[offset],
            )
        )
    start_all(stores)
    wait_all(stores)


def forward(me, rows, cols, count, sens, waves, after):
    slots = sens.shape[0]
    peers = len(waves)
    blocks, width = after[1], sens.shape[2]
    half = (RB_DEV // 2, BLK, width)
    return pl.pallas_call(
        forward_body,
        out_shape=[jax.ShapeDtypeStruct(half, jnp.float32)] * 2,
        in_specs=[SMEM_SPEC] * 4 + [ANY_SPEC] * (1 + peers + 1),
        out_specs=[ANY_SPEC] * 2,
        scratch_shapes=[
            pltpu.VMEM(sens.shape, sens.dtype),
            pltpu.VMEM((blocks, BLK, width), jnp.bfloat16),
            pltpu.VMEM((RB_DEV + 1, BLK, width), jnp.float32),
            pltpu.SemaphoreType.DMA((slots // STEP,)),
            pltpu.SemaphoreType.DMA((peers,)),
            pltpu.SemaphoreType.DMA((peers,)),
        ],
        compiler_params=pltpu.CompilerParams(vmem_limit_bytes=LARGE),
        cost_estimate=pl.CostEstimate(
            flops=2 * slots * BLK * BLK * width, bytes_accessed=2 * slots * BLK * BLK,
            transcendentals=0,
        ),
        name="forward",
    )(me, rows, cols, count, sens, *waves, after[0])


def adjoint_body(me_ref, rows_ref, cols_ref, count_ref, sens_ref, even_in_ref, odd_in_ref,
                 after_ref, *refs):
    out_refs, image_ref = refs[:-9], refs[-9]
    block_ref, held_ref, acc_ref, half_ref, sems, got, put, whole = refs[-8:]
    peers = put.shape[0]
    col_blocks = acc_ref.shape[0] - 1
    each = col_blocks // peers
    me = me_ref[0]
    def work(slot, block, live):
        col = jnp.where(live, cols_ref[0, slot], col_blocks)
        acc_ref[col] += lax.dot_general(
            block, held_ref[rows_ref[0, slot]], (((0,), (0,)), ((), ())),
            preferred_element_type=jnp.float32,
        )

    each_in = held_ref.shape[0] // peers
    sources = [
        (ref, i * each_in, 2 * j + odd)
        for i, j in enumerate([0, *far_first(peers)])
        for odd, ref in enumerate((even_in_ref, odd_in_ref))
    ]
    images = gather_pieces(sources, held_ref, me, got)
    stores = fetch(held_ref, image_ref, whole, whole.shape[0])
    slot_loop(count_ref[0, 0], sens_ref, block_ref, sems, images, acc_ref, work, stores)
    for offset in reversed(range(peers)):
        part = acc_ref[pl.ds((me ^ offset) * each, each)]
        half_ref[offset] = part.astype(half_ref.dtype)
        target = out_refs[offset // 2].at[pl.ds(offset % 2 * each, each)]
        stores.append(pltpu.make_async_copy(half_ref.at[offset], target, put.at[offset]))
        stores[-1].start()
    wait_all(stores)


def adjoint(me, rows, cols, count, sens, even, odd, after, blocks, peers):
    slots = sens.shape[0]
    width = even.shape[2]
    piece = (blocks // peers, BLK, width)
    image = (RB_DEV, BLK, width)
    outs = pl.pallas_call(
        adjoint_body,
        out_shape=[jax.ShapeDtypeStruct((2 * piece[0], *piece[1:]), jnp.bfloat16)] * (peers // 2)
        + [jax.ShapeDtypeStruct(image, jnp.bfloat16)],
        in_specs=[SMEM_SPEC] * 4 + [ANY_SPEC] * 4,
        out_specs=[ANY_SPEC] * (peers // 2 + 1),
        scratch_shapes=[
            pltpu.VMEM(sens.shape, sens.dtype),
            pltpu.VMEM(image, jnp.bfloat16),
            pltpu.VMEM((blocks + 1, BLK, width), jnp.float32),
            pltpu.VMEM((peers, *piece), jnp.bfloat16),
            pltpu.SemaphoreType.DMA((slots // STEP,)),
            pltpu.SemaphoreType.DMA((peers,)),
            pltpu.SemaphoreType.DMA((peers,)),
            pltpu.SemaphoreType.DMA((4,)),
        ],
        compiler_params=pltpu.CompilerParams(vmem_limit_bytes=LARGE),
        cost_estimate=pl.CostEstimate(
            flops=2 * slots * BLK * BLK * width, bytes_accessed=2 * slots * BLK * BLK,
            transcendentals=0,
        ),
        name="adjoint",
    )(me, rows, cols, count, sens, even, odd, after)
    return outs[:-1], outs[-1]


def tile_value(near, face, window):
    span = lax.broadcasted_iota(jnp.int32, (2 * BLK, BLK), 0)
    center = lax.broadcasted_iota(jnp.int32, (2 * BLK, BLK), 1) + RIM
    mix = jnp.where(span == center, jnp.sum(face, axis=0, keepdims=True), 0.0)
    for k in range(4):
        mix = mix - jnp.where(span == near[k : k + 1], face[k : k + 1], 0.0)
    mix_high = mix.astype(jnp.bfloat16)
    mix_low = (mix - mix_high.astype(jnp.float32)).astype(jnp.bfloat16)
    near_high = window.astype(jnp.bfloat16)
    near_low = (window - near_high.astype(jnp.float32)).astype(jnp.bfloat16)
    return lax.dot_general(
        jnp.concatenate([mix_high, mix_high, mix_low], axis=0),
        jnp.concatenate([near_high, near_low, near_high], axis=0),
        (((0,), (0,)), ((), ())), preferred_element_type=jnp.float32,
    )


def smooth_body(offset_ref, model_ref, near_ref, weight_ref, after_ref,
                out_ref, ext_ref, value_ref, got, put):
    cells, width = model_ref.shape
    steps = put.shape[0]
    tiles = cells // BLK // steps
    each = cells // got.shape[0]
    loads = [
        pltpu.make_async_copy(
            model_ref.at[pl.ds(i * each, each)], ext_ref.at[pl.ds(RIM + i * each, each)], got.at[i]
        )
        for i in range(got.shape[0])
    ]
    start_all(loads)
    ext_ref[:RIM] = jnp.zeros((RIM, width), jnp.float32)
    ext_ref[RIM + cells :] = jnp.zeros((RIM, width), jnp.float32)
    wait_all(loads)

    def store(step):
        part = pl.ds(step * tiles * BLK, tiles * BLK)
        return pltpu.make_async_copy(value_ref.at[part], out_ref.at[part], put.at[step])

    @pl.loop(0, steps)
    def _(step):
        for t in range(tiles):
            start = pl.multiple_of((step * tiles + t) * BLK, BLK)
            near = near_ref[:, pl.ds(start, BLK)] - (offset_ref[0] + start)
            face = weight_ref[:, pl.ds(start, BLK)]
            window = ext_ref[pl.ds(start, 2 * BLK), :]
            value_ref[pl.ds(start, BLK), :] = tile_value(near, face, window)
        store(step).start()

    for step in range(steps):
        store(step).wait()


def smoothing(offset, model, neighbors, face_weight, after):
    cells, width = model.shape
    return pl.pallas_call(
        smooth_body,
        out_shape=jax.ShapeDtypeStruct((cells, width), jnp.float32),
        in_specs=[SMEM_SPEC, ANY_SPEC, VMEM_SPEC, VMEM_SPEC, ANY_SPEC],
        out_specs=ANY_SPEC,
        scratch_shapes=[
            pltpu.VMEM((cells + 2 * RIM, width), jnp.float32),
            pltpu.VMEM((cells, width), jnp.float32),
            pltpu.SemaphoreType.DMA((16,)),
            pltpu.SemaphoreType.DMA((8,)),
        ],
        compiler_params=pltpu.CompilerParams(vmem_limit_bytes=LARGE),
        cost_estimate=pl.CostEstimate(
            flops=24 * cells * BLK * width, bytes_accessed=16 * cells * width, transcendentals=0
        ),
        name="smoothing",
    )(offset, model, neighbors, face_weight, after)


def edges_body(me_ref, offset_ref, model_ref, near_ref, weight_ref, base_ref, after_ref, *refs):
    odd_refs, refs = refs[:-6], refs[-6:]
    out_ref, window_ref, value_ref, ends_ref, got, put = refs
    cells = model_ref.shape[0]
    each = odd_refs[-1].shape[0] - 1
    inner = 2 * BLK - RIM
    starts = (0, cells - BLK)
    me = me_ref[0]
    loads = [
        pltpu.make_async_copy(
            model_ref.at[pl.ds(0, inner)], window_ref.at[0, pl.ds(RIM, inner)], got.at[0]
        ),
        pltpu.make_async_copy(
            model_ref.at[pl.ds(cells - inner, inner)], window_ref.at[1, pl.ds(0, inner)], got.at[1]
        ),
    ]
    for i, odd_ref in enumerate(odd_refs):
        loads.append(
            pltpu.make_async_copy(odd_ref.at[each], ends_ref.at[i], got.at[2 + i])
        )
    start_all(loads)
    wait_all(loads)
    zero = jnp.zeros((RIM, model_ref.shape[1]), jnp.float32)
    low, high = zero, zero
    for i in range(len(odd_refs)):
        rows = ends_ref[i, :RIM].astype(jnp.float32) + ends_ref[i, RIM:].astype(jnp.float32)
        peer = me ^ (2 * i + 1)
        low = jnp.where(peer == me - 1, rows, low)
        high = jnp.where(peer == me + 1, rows, high)
    window_ref[0, :RIM] = low
    window_ref[1, inner:] = high
    stores = []
    for i, start in enumerate(starts):
        near = near_ref[:, start : start + BLK] - (offset_ref[0] + start)
        value_ref[i] = tile_value(near, weight_ref[:, start : start + BLK], window_ref[i])
        stores.append(
            pltpu.make_async_copy(value_ref.at[i], out_ref.at[pl.ds(start, BLK)], put.at[i])
        )
    start_all(stores)
    wait_all(stores)


def edges(me, offset, model, neighbors, face_weight, base, after, odd_pieces):
    width = model.shape[1]
    count = len(odd_pieces)
    return pl.pallas_call(
        edges_body,
        out_shape=jax.ShapeDtypeStruct(base.shape, base.dtype),
        in_specs=[SMEM_SPEC, SMEM_SPEC, ANY_SPEC, VMEM_SPEC, VMEM_SPEC]
        + [ANY_SPEC] * (2 + count),
        out_specs=ANY_SPEC,
        input_output_aliases={5: 0},
        scratch_shapes=[
            pltpu.VMEM((2, 2 * BLK, width), jnp.float32),
            pltpu.VMEM((2, BLK, width), jnp.float32),
            pltpu.VMEM((count, BLK, width), jnp.bfloat16),
            pltpu.SemaphoreType.DMA((2 + count,)),
            pltpu.SemaphoreType.DMA((2,)),
        ],
        compiler_params=pltpu.CompilerParams(vmem_limit_bytes=LARGE),
        cost_estimate=pl.CostEstimate(
            flops=24 * 2 * BLK * BLK * width, bytes_accessed=32 * BLK * width, transcendentals=0
        ),
        name="edges",
    )(me, offset, model, neighbors, face_weight, base, after, *odd_pieces)


def finish_body(me_ref, order_ref, basis_ref, even_ref, odd_ref, base_ref,
                out_ref, token_ref, block_ref, value_ref, got, put, *, offset):
    per_peer = odd_ref.shape[0]
    cols = 2 * per_peer
    fetches, stores = [], []
    for i in range(cols):
        peer = me_ref[0] ^ (offset + i // per_peer)
        cell = order_ref[0, peer * per_peer + i % per_peer]
        fetches.append(pltpu.make_async_copy(base_ref.at[cell], block_ref.at[i], got.at[i]))
        stores.append(pltpu.make_async_copy(block_ref.at[i], out_ref.at[cell], put.at[i]))
    start_all(fetches)
    for i in range(cols):
        wave = even_ref[i] if i < per_peer else odd_ref[i - per_peer]
        both = jnp.concatenate([wave, wave], axis=0)
        value_ref[i] = jnp.dot(basis_ref[...], both, preferred_element_type=jnp.float32)
    wait_all(fetches)
    block_ref[...] += value_ref[...]
    start_all(stores)
    token_ref[...] = jnp.zeros_like(token_ref)
    wait_all(stores)


def finish(me, order, even, odd, base, offset):
    width = odd.shape[2]
    cols = 2 * odd.shape[0]
    basis = haar_matrix(BLK).T.astype(np.float32)
    high = basis.astype(jnp.bfloat16)
    low = (basis - high.astype(np.float32)).astype(jnp.bfloat16)
    basis2 = jnp.asarray(np.concatenate([high, low], axis=1))
    return pl.pallas_call(
        lambda *refs: finish_body(*refs, offset=offset),
        out_shape=[
            jax.ShapeDtypeStruct(base.shape, base.dtype),
            jax.ShapeDtypeStruct((8, BLK), jnp.float32),
        ],
        in_specs=[SMEM_SPEC] * 2 + [VMEM_SPEC] * 3 + [ANY_SPEC],
        out_specs=[ANY_SPEC, VMEM_SPEC],
        input_output_aliases={5: 0},
        scratch_shapes=[
            pltpu.VMEM((cols, BLK, width), jnp.float32),
            pltpu.VMEM((cols, BLK, width), jnp.float32),
            pltpu.SemaphoreType.DMA((cols,)),
            pltpu.SemaphoreType.DMA((cols,)),
        ],
        compiler_params=pltpu.CompilerParams(vmem_limit_bytes=SMALL),
        cost_estimate=pl.CostEstimate(
            flops=4 * cols * BLK * BLK * width, bytes_accessed=10 * cols * BLK * width,
            transcendentals=0,
        ),
        name="finish",
    )(me, order, basis2, even, odd, base)


def merge_body(got_ref, mine_ref, after_ref, out_ref):
    total = got_ref[...].astype(jnp.float32) + mine_ref[...].astype(jnp.float32)
    out_ref[...] = total.astype(out_ref.dtype)


def merge(got, mine, after):
    return pl.pallas_call(
        merge_body,
        out_shape=jax.ShapeDtypeStruct(mine.shape, mine.dtype),
        in_specs=[VMEM_SPEC, VMEM_SPEC, ANY_SPEC],
        out_specs=VMEM_SPEC,
        compiler_params=pltpu.CompilerParams(vmem_limit_bytes=SMALL),
        cost_estimate=pl.CostEstimate(
            flops=mine.size, bytes_accessed=6 * mine.size, transcendentals=0
        ),
        name="merge",
    )(got, mine, after)


def pick_body(take_ref, got_ref, mine_ref, after_ref, token_ref, *out_refs):
    each = out_refs[0].shape[0]
    for i, out_ref in enumerate(out_refs):
        part = pl.ds(i * each, each)
        out_ref[...] = jnp.where(take_ref[0] > 0, got_ref[part], mine_ref[part])


def pick(take, got, mine, after, token, parts):
    shape = (mine.shape[0] // parts, *mine.shape[1:])
    return pl.pallas_call(
        pick_body,
        out_shape=[jax.ShapeDtypeStruct(shape, mine.dtype)] * parts,
        in_specs=[SMEM_SPEC, VMEM_SPEC, VMEM_SPEC, ANY_SPEC, ANY_SPEC],
        out_specs=[VMEM_SPEC] * parts,
        compiler_params=pltpu.CompilerParams(vmem_limit_bytes=SMALL),
        cost_estimate=pl.CostEstimate(
            flops=mine.size, bytes_accessed=6 * mine.size, transcendentals=0
        ),
        name="pick",
    )(take, got, mine, after, token)


def second_half_body(whole_ref, after_ref, out_ref):
    out_ref[...] = whole_ref[out_ref.shape[0] :]


def second_half(whole, after):
    shape = (whole.shape[0] // 2, *whole.shape[1:])
    return pl.pallas_call(
        second_half_body,
        out_shape=jax.ShapeDtypeStruct(shape, whole.dtype),
        in_specs=[VMEM_SPEC, ANY_SPEC],
        out_specs=VMEM_SPEC,
        compiler_params=pltpu.CompilerParams(vmem_limit_bytes=SMALL),
        cost_estimate=pl.CostEstimate(
            flops=0, bytes_accessed=2 * whole.size, transcendentals=0
        ),
        name="second_half",
    )(whole, after)


def line_sums(parts, axis, deliver):
    count = lax.axis_size(axis)
    half = count // 2
    me = lax.axis_index(axis)
    stages = []
    for hop in range(half - 1):
        stages.append(([(hop, hop + 1), (count - 1 - hop, count - 2 - hop)], False))
    stages.append(([(half - 1, half), (half, half - 1)], False))
    for hop in range(half - 1):
        left, right = half - 1 - hop, half + hop
        stages.append(([(left, left - 1), (right, right + 1)], True))
    state = list(parts)
    got = [lax.ppermute(part, axis, stages[0][0]) for part in parts]
    after = parts[0]
    for time in range(len(parts) + len(stages) - 1):
        for s, (pairs, outwards) in enumerate(stages):
            k = time - s
            if not 0 <= k < len(parts):
                continue
            last = s + 1 == len(stages)
            if outwards:
                take = (me == pairs[0][1]) | (me == pairs[1][1])
                take = take.astype(jnp.int32).reshape(1)
                if last:
                    after = deliver(k, take, got[k], state[k], after)
                else:
                    state[k] = jnp.where(take[0] > 0, got[k], state[k])
            else:
                state[k] = after = merge(got[k], state[k], after)
                if last:
                    take = jnp.zeros((1,), jnp.int32)
                    after = deliver(k, take, state[k], state[k], after)
            if not last:
                got[k] = lax.ppermute(state[k], axis, stages[s + 1][0])


def swap(piece, axis, offset):
    return lax.ppermute(piece, axis, [(c, c ^ offset) for c in range(lax.axis_size(axis))])


def local(model_dir, sens_blocks, blk_row, blk_col, blk_count, send_order, neighbors, face_weight):
    cell_count, width = model_dir.shape
    blocks = cell_count // BLK
    peers = lax.axis_size("cols")
    half = peers // 2
    per_peer = blocks // peers
    col = lax.axis_index("cols").astype(jnp.int32)
    me = col.reshape(1)
    offset = (col * cell_count - RIM).reshape(1)
    sens = sens_blocks[0]
    far = far_first(peers)

    *own, odd = analyze(me, send_order, model_dir.reshape(blocks, BLK, width), peers)
    partner = swap(odd, "cols", 1)
    direct = {j: swap(own[j], "cols", 2 * j) for j in far}
    passed = {
        j: swap(partner[j * (per_peer + 1) : (j + 1) * (per_peer + 1)], "cols", 2 * j)
        for j in far
    }
    waves = [own[0], partner, *[direct[j] for j in far], *[passed[j] for j in far]]
    smooth = smoothing(offset, model_dir, neighbors, face_weight, partner)

    even_rows, odd_rows = forward(
        me, blk_row, blk_col, blk_count, sens, waves, (smooth, blocks)
    )
    pair = (even_rows + swap(odd_rows, "cols", 1)).reshape(half, -1, BLK, width)
    to_send = pair.astype(jnp.bfloat16)
    shares = [swap(to_send[j], "cols", 2 * j) for j in far]
    total = pair[0] + sum(share.astype(jnp.float32) for share in shares)
    image_share = total.astype(jnp.bfloat16)
    even_image = jnp.concatenate(
        [image_share] + [swap(image_share, "cols", 2 * j) for j in far], axis=0
    )
    odd_image = swap(even_image, "cols", 1)
    smooth = edges(
        me, offset, model_dir, neighbors, face_weight, smooth, to_send, [partner, *[passed[j] for j in range(1, half)]]
    )

    partial_cols, image = adjoint(
        me, blk_row, blk_col, blk_count, sens, even_image, odd_image, smooth, blocks, peers
    )
    data_image = image.reshape(RB_DEV * BLK, width).astype(jnp.float32)
    normal = smooth.reshape(blocks, BLK, width)
    order = [*far, 0]
    waiting, tokens = [], []

    def end_one(place):
        nonlocal normal
        even, other, j = waiting.pop(place)
        if other is None:
            other = swap(second_half(even, tokens[-1]), "cols", 1)
        normal, token = finish(me, send_order, even, other, normal, 2 * j)
        tokens.append(token)

    def deliver(k, take, got, mine, after):
        if k >= 2:
            end_one(0)
        token = tokens[-1] if tokens else after
        j = order[k]
        if j == 0:
            even, other = pick(take, got, mine, after, token, 2)
            waiting.append((even, swap(other, "cols", 1), j))
            return even
        [total] = pick(take, got, mine, after, token, 1)
        even = swap(total, "cols", 2 * j)
        other = None if k == half - 2 else swap(even[per_peer:], "cols", 1)
        waiting.append((even, other, j))
        return total

    line_sums([partial_cols[j] for j in order], "rows", deliver)
    while waiting:
        end_one(-1)
    return (data_image, normal.reshape(cell_count, width))


def solution(mesh):
    placed = (
        P("cols", None),
        P("rows", "cols", None, None),
        P("rows", "cols"),
        P("rows", "cols"),
        P("rows", "cols"),
        P("cols", None),
        P(None, "cols"),
        P(None, "cols"),
    )
    return jax.shard_map(
        local,
        mesh=mesh,
        in_specs=placed,
        out_specs=(P("rows", None), P("cols", None)),
        check_vma=False,
    )
```

```python
import math

import jax
import jax.numpy as jnp
import numpy as np
from jax import lax
from jax.experimental import pallas as pl
from jax.experimental.pallas import tpu as pltpu
from jax.sharding import PartitionSpec as P

BLK = 128
RB_DEV = 32
RIM = 64
STEP = 16
MIB = 1 << 20
SMALL = 16 * MIB
LARGE = 56 * MIB
ANY_SPEC = pl.BlockSpec(memory_space=pl.ANY)
VMEM_SPEC = pl.BlockSpec(memory_space=pltpu.VMEM)
SMEM_SPEC = pl.BlockSpec(memory_space=pltpu.SMEM)


def haar_matrix(order_n):
    matrix = np.ones((1, 1))
    while matrix.shape[0] < order_n:
        length = matrix.shape[0]
        upper = np.kron(matrix, np.array([[1.0, 1.0]]))
        lower = np.kron(np.eye(length), np.array([[1.0, -1.0]]))
        matrix = np.concatenate([upper, lower], axis=0) / math.sqrt(2.0)
    return matrix


def fetch(source, target, sems, pieces):
    each = source.shape[0] // pieces
    parts = [pl.ds(i * each, each) for i in range(pieces)]
    return [
        pltpu.make_async_copy(source.at[part], target.at[part], sems.at[i])
        for i, part in enumerate(parts)
    ]


def gather_pieces(sources, held_ref, me, sems):
    each = held_ref.shape[0] // len(sources)
    return [
        pltpu.make_async_copy(
            ref.at[pl.ds(first, each)],
            held_ref.at[pl.ds((me ^ offset) * each, each)],
            sems.at[offset],
        )
        for ref, first, offset in sources
    ]


def far_first(peers):
    return sorted(range(1, peers // 2), key=lambda j: (-bin(j).count("1"), j))


def wave_offsets(peers):
    far = far_first(peers)
    return [0, 1, *[2 * j for j in far], *[2 * j + 1 for j in far]]


def piece_stores(source, offset, even_refs, odd_ref, sems):
    each = source.shape[0]
    stride = odd_ref.shape[0] // (sems.shape[0] // 2)
    if offset % 2:
        target = odd_ref.at[pl.ds((offset // 2) * stride, each)]
    else:
        target = even_refs[offset // 2].at[pl.ds(0, each)]
    return pltpu.make_async_copy(source, target, sems.at[offset])


def start_all(copies):
    for copy in copies:
        copy.start()


def wait_all(copies):
    for copy in copies:
        copy.wait()


def analyze_body(me_ref, order_ref, model_ref, *refs):
    even_refs, (odd_ref, block_ref, coeff_ref, got, put) = refs[:-5], refs[-5:]
    width = model_ref.shape[2]
    per_peer = even_refs[0].shape[0]
    peers = put.shape[0]
    me = me_ref[0]
    loads = fetch(model_ref, block_ref, got, got.shape[0])
    start_all(loads)
    row = lax.broadcasted_iota(jnp.int32, (BLK, BLK), 0)
    col = lax.broadcasted_iota(jnp.int32, (BLK, BLK), 1)
    level = jnp.ones_like(row)
    scale = jnp.full((BLK, width), BLK**-0.5, jnp.float32)
    wide_row = lax.broadcasted_iota(jnp.int32, (BLK, width), 0)
    size = 2
    while size < BLK:
        level = jnp.where(row >= size, size, level)
        scale = jnp.where(wide_row >= size, (size / BLK) ** 0.5, scale)
        size *= 2
    span = BLK // level
    inside = col - (row - level) * span
    sign = jnp.where(inside * 2 < span, 1.0, -1.0)
    sign = jnp.where((inside >= 0) & (inside < span), sign, 0.0)
    sign = jnp.where(row == 0, 1.0, sign).astype(jnp.bfloat16)
    both_signs = jnp.concatenate([sign, sign], axis=1)
    wait_all(loads)
    stores = []
    ends = []
    for rows in (block_ref[model_ref.shape[0] - 1, BLK - RIM :], block_ref[0, :RIM]):
        high = rows.astype(jnp.bfloat16)
        low = (rows - high.astype(jnp.float32)).astype(jnp.bfloat16)
        ends.append(jnp.concatenate([high, low], axis=0))
    for offset in [*range(1, peers, 2), *range(peers - 2, -1, -2)]:
        peer = (me ^ offset) * per_peer
        for q in range(per_peer):
            x = block_ref[order_ref[0, peer + q]]
            high = x.astype(jnp.bfloat16)
            low = (x - high.astype(jnp.float32)).astype(jnp.bfloat16)
            raw = jnp.dot(
                both_signs, jnp.concatenate([high, low], axis=0),
                preferred_element_type=jnp.float32,
            )
            coeff_ref[offset, q] = (raw * scale).astype(jnp.bfloat16)
        length = per_peer
        if offset % 2:
            coeff_ref[offset, per_peer] = jnp.where(me ^ offset == me + 1, ends[0], ends[1])
            length += 1
        source = coeff_ref.at[offset, pl.ds(0, length)]
        stores.append(piece_stores(source, offset, even_refs, odd_ref, put))
        stores[-1].start()
    wait_all(stores)


def piece_shapes(piece, peers, dtype, more=0):
    half = peers // 2
    return [jax.ShapeDtypeStruct(piece, dtype)] * half + [
        jax.ShapeDtypeStruct((half * (piece[0] + more), *piece[1:]), dtype)
    ]


def analyze(me, order, model_blocks, peers):
    blocks, _, width = model_blocks.shape
    piece = (blocks // peers, BLK, width)
    return pl.pallas_call(
        analyze_body,
        out_shape=piece_shapes(piece, peers, jnp.bfloat16, 1),
        in_specs=[SMEM_SPEC, SMEM_SPEC, ANY_SPEC],
        out_specs=[ANY_SPEC] * (peers // 2 + 1),
        scratch_shapes=[
            pltpu.VMEM((blocks, BLK, width), jnp.float32),
            pltpu.VMEM((peers, piece[0] + 1, *piece[1:]), jnp.bfloat16),
            pltpu.SemaphoreType.DMA((16,)),
            pltpu.SemaphoreType.DMA((peers,)),
        ],
        compiler_params=pltpu.CompilerParams(vmem_limit_bytes=LARGE),
        cost_estimate=pl.CostEstimate(
            flops=4 * blocks * BLK * BLK * width, bytes_accessed=6 * blocks * BLK * width,
            transcendentals=0,
        ),
        name="analyze",
    )(me, order, model_blocks)


def slot_loop(count, sens_ref, block_ref, sems, others, acc_ref, work, then=()):
    steps = sems.shape[0]
    each = sens_ref.shape[0] // steps

    def block_copy(step):
        part = pl.ds(step * each, each)
        return pltpu.make_async_copy(sens_ref.at[part], block_ref.at[part], sems.at[step])

    start_all(others)
    needed = (count + each - 1) // each

    @pl.loop(0, needed)
    def _(step):
        block_copy(step).start()

    acc_ref[...] = jnp.zeros_like(acc_ref)
    wait_all(others)
    start_all(then)

    @pl.loop(0, needed)
    def _(step):
        block_copy(step).wait()
        for k in range(each):
            slot = step * each + k
            work(slot, block_ref[slot], slot < count)


def forward_body(me_ref, rows_ref, cols_ref, count_ref, sens_ref, *refs):
    peers = len(refs) - 9
    wave_refs, (even_ref, odd_ref) = refs[:peers], refs[peers + 1 : peers + 3]
    block_ref, held_ref, acc_ref, sems, got, put = refs[peers + 3 :]
    row_blocks = acc_ref.shape[0] - 1
    each = row_blocks // peers
    me = me_ref[0]
    def work(slot, block, live):
        row = jnp.where(live, rows_ref[0, slot], row_blocks)
        acc_ref[row] += jnp.dot(
            block, held_ref[cols_ref[0, slot]], preferred_element_type=jnp.float32
        )

    sources = [(ref, 0, offset) for ref, offset in zip(wave_refs, wave_offsets(peers))]
    waves = gather_pieces(sources, held_ref, me, got)
    slot_loop(count_ref[0, 0], sens_ref, block_ref, sems, waves, acc_ref, work)
    stores = []
    for offset in [*range(1, peers, 2), *range(0, peers, 2)]:
        target = odd_ref if offset % 2 else even_ref
        stores.append(
            pltpu.make_async_copy(
                acc_ref.at[pl.ds((me ^ offset) * each, each)],
                target.at[pl.ds((offset // 2) * each, each)],
                put.at[offset],
            )
        )
    start_all(stores)
    wait_all(stores)


def forward(me, rows, cols, count, sens, waves, after):
    slots = sens.shape[0]
    peers = len(waves)
    blocks, width = after[1], sens.shape[2]
    half = (RB_DEV // 2, BLK, width)
    return pl.pallas_call(
        forward_body,
        out_shape=[jax.ShapeDtypeStruct(half, jnp.float32)] * 2,
        in_specs=[SMEM_SPEC] * 4 + [ANY_SPEC] * (1 + peers + 1),
        out_specs=[ANY_SPEC] * 2,
        scratch_shapes=[
            pltpu.VMEM(sens.shape, sens.dtype),
            pltpu.VMEM((blocks, BLK, width), jnp.bfloat16),
            pltpu.VMEM((RB_DEV + 1, BLK, width), jnp.float32),
            pltpu.SemaphoreType.DMA((slots // STEP,)),
            pltpu.SemaphoreType.DMA((peers,)),
            pltpu.SemaphoreType.DMA((peers,)),
        ],
        compiler_params=pltpu.CompilerParams(vmem_limit_bytes=LARGE),
        cost_estimate=pl.CostEstimate(
            flops=2 * slots * BLK * BLK * width, bytes_accessed=2 * slots * BLK * BLK,
            transcendentals=0,
        ),
        name="forward",
    )(me, rows, cols, count, sens, *waves, after[0])


def adjoint_body(me_ref, rows_ref, cols_ref, count_ref, sens_ref, even_in_ref, odd_in_ref,
                 after_ref, *refs):
    out_refs, image_ref = refs[:-9], refs[-9]
    block_ref, held_ref, acc_ref, half_ref, sems, got, put, whole = refs[-8:]
    peers = put.shape[0]
    col_blocks = acc_ref.shape[0] - 1
    each = col_blocks // peers
    me = me_ref[0]
    def work(slot, block, live):
        col = jnp.where(live, cols_ref[0, slot], col_blocks)
        acc_ref[col] += lax.dot_general(
            block, held_ref[rows_ref[0, slot]], (((0,), (0,)), ((), ())),
            preferred_element_type=jnp.float32,
        )

    each_in = held_ref.shape[0] // peers
    sources = [
        (ref, i * each_in, 2 * j + odd)
        for i, j in enumerate([0, *far_first(peers)])
        for odd, ref in enumerate((even_in_ref, odd_in_ref))
    ]
    images = gather_pieces(sources, held_ref, me, got)
    stores = fetch(held_ref, image_ref, whole, whole.shape[0])
    slot_loop(count_ref[0, 0], sens_ref, block_ref, sems, images, acc_ref, work, stores)
    for offset in reversed(range(peers)):
        part = acc_ref[pl.ds((me ^ offset) * each, each)]
        half_ref[offset] = part.astype(half_ref.dtype)
        target = out_refs[offset // 2].at[pl.ds(offset % 2 * each, each)]
        stores.append(pltpu.make_async_copy(half_ref.at[offset], target, put.at[offset]))
        stores[-1].start()
    wait_all(stores)


def adjoint(me, rows, cols, count, sens, even, odd, after, blocks, peers):
    slots = sens.shape[0]
    width = even.shape[2]
    piece = (blocks // peers, BLK, width)
    image = (RB_DEV, BLK, width)
    outs = pl.pallas_call(
        adjoint_body,
        out_shape=[jax.ShapeDtypeStruct((2 * piece[0], *piece[1:]), jnp.bfloat16)] * (peers // 2)
        + [jax.ShapeDtypeStruct(image, jnp.bfloat16)],
        in_specs=[SMEM_SPEC] * 4 + [ANY_SPEC] * 4,
        out_specs=[ANY_SPEC] * (peers // 2 + 1),
        scratch_shapes=[
            pltpu.VMEM(sens.shape, sens.dtype),
            pltpu.VMEM(image, jnp.bfloat16),
            pltpu.VMEM((blocks + 1, BLK, width), jnp.float32),
            pltpu.VMEM((peers, *piece), jnp.bfloat16),
            pltpu.SemaphoreType.DMA((slots // STEP,)),
            pltpu.SemaphoreType.DMA((peers,)),
            pltpu.SemaphoreType.DMA((peers,)),
            pltpu.SemaphoreType.DMA((4,)),
        ],
        compiler_params=pltpu.CompilerParams(vmem_limit_bytes=LARGE),
        cost_estimate=pl.CostEstimate(
            flops=2 * slots * BLK * BLK * width, bytes_accessed=2 * slots * BLK * BLK,
            transcendentals=0,
        ),
        name="adjoint",
    )(me, rows, cols, count, sens, even, odd, after)
    return outs[:-1], outs[-1]


def tile_value(near, face, window):
    span = lax.broadcasted_iota(jnp.int32, (2 * BLK, BLK), 0)
    center = lax.broadcasted_iota(jnp.int32, (2 * BLK, BLK), 1) + RIM
    mix = jnp.where(span == center, jnp.sum(face, axis=0, keepdims=True), 0.0)
    for k in range(4):
        mix = mix - jnp.where(span == near[k : k + 1], face[k : k + 1], 0.0)
    mix_high = mix.astype(jnp.bfloat16)
    mix_low = (mix - mix_high.astype(jnp.float32)).astype(jnp.bfloat16)
    near_high = window.astype(jnp.bfloat16)
    near_low = (window - near_high.astype(jnp.float32)).astype(jnp.bfloat16)
    return lax.dot_general(
        jnp.concatenate([mix_high, mix_high, mix_low], axis=0),
        jnp.concatenate([near_high, near_low, near_high], axis=0),
        (((0,), (0,)), ((), ())), preferred_element_type=jnp.float32,
    )


def smooth_body(offset_ref, model_ref, near_ref, weight_ref, after_ref,
                out_ref, ext_ref, value_ref, got, put):
    cells, width = model_ref.shape
    steps = put.shape[0]
    tiles = cells // BLK // steps
    each = cells // got.shape[0]
    loads = [
        pltpu.make_async_copy(
            model_ref.at[pl.ds(i * each, each)], ext_ref.at[pl.ds(RIM + i * each, each)], got.at[i]
        )
        for i in range(got.shape[0])
    ]
    start_all(loads)
    ext_ref[:RIM] = jnp.zeros((RIM, width), jnp.float32)
    ext_ref[RIM + cells :] = jnp.zeros((RIM, width), jnp.float32)
    wait_all(loads)

    def store(step):
        part = pl.ds(step * tiles * BLK, tiles * BLK)
        return pltpu.make_async_copy(value_ref.at[part], out_ref.at[part], put.at[step])

    @pl.loop(0, steps)
    def _(step):
        for t in range(tiles):
            start = pl.multiple_of((step * tiles + t) * BLK, BLK)
            near = near_ref[:, pl.ds(start, BLK)] - (offset_ref[0] + start)
            face = weight_ref[:, pl.ds(start, BLK)]
            window = ext_ref[pl.ds(start, 2 * BLK), :]
            value_ref[pl.ds(start, BLK), :] = tile_value(near, face, window)
        store(step).start()

    for step in range(steps):
        store(step).wait()


def smoothing(offset, model, neighbors, face_weight, after):
    cells, width = model.shape
    return pl.pallas_call(
        smooth_body,
        out_shape=jax.ShapeDtypeStruct((cells, width), jnp.float32),
        in_specs=[SMEM_SPEC, ANY_SPEC, VMEM_SPEC, VMEM_SPEC, ANY_SPEC],
        out_specs=ANY_SPEC,
        scratch_shapes=[
            pltpu.VMEM((cells + 2 * RIM, width), jnp.float32),
            pltpu.VMEM((cells, width), jnp.float32),
            pltpu.SemaphoreType.DMA((16,)),
            pltpu.SemaphoreType.DMA((8,)),
        ],
        compiler_params=pltpu.CompilerParams(vmem_limit_bytes=LARGE),
        cost_estimate=pl.CostEstimate(
            flops=24 * cells * BLK * width, bytes_accessed=16 * cells * width, transcendentals=0
        ),
        name="smoothing",
    )(offset, model, neighbors, face_weight, after)


def edges_body(me_ref, offset_ref, model_ref, near_ref, weight_ref, base_ref, after_ref, *refs):
    odd_refs, refs = refs[:-6], refs[-6:]
    out_ref, window_ref, value_ref, ends_ref, got, put = refs
    cells = model_ref.shape[0]
    each = odd_refs[-1].shape[0] - 1
    inner = 2 * BLK - RIM
    starts = (0, cells - BLK)
    me = me_ref[0]
    loads = [
        pltpu.make_async_copy(
            model_ref.at[pl.ds(0, inner)], window_ref.at[0, pl.ds(RIM, inner)], got.at[0]
        ),
        pltpu.make_async_copy(
            model_ref.at[pl.ds(cells - inner, inner)], window_ref.at[1, pl.ds(0, inner)], got.at[1]
        ),
    ]
    for i, odd_ref in enumerate(odd_refs):
        loads.append(
            pltpu.make_async_copy(odd_ref.at[each], ends_ref.at[i], got.at[2 + i])
        )
    start_all(loads)
    wait_all(loads)
    zero = jnp.zeros((RIM, model_ref.shape[1]), jnp.float32)
    low, high = zero, zero
    for i in range(len(odd_refs)):
        rows = ends_ref[i, :RIM].astype(jnp.float32) + ends_ref[i, RIM:].astype(jnp.float32)
        peer = me ^ (2 * i + 1)
        low = jnp.where(peer == me - 1, rows, low)
        high = jnp.where(peer == me + 1, rows, high)
    window_ref[0, :RIM] = low
    window_ref[1, inner:] = high
    stores = []
    for i, start in enumerate(starts):
        near = near_ref[:, start : start + BLK] - (offset_ref[0] + start)
        value_ref[i] = tile_value(near, weight_ref[:, start : start + BLK], window_ref[i])
        stores.append(
            pltpu.make_async_copy(value_ref.at[i], out_ref.at[pl.ds(start, BLK)], put.at[i])
        )
    start_all(stores)
    wait_all(stores)


def edges(me, offset, model, neighbors, face_weight, base, after, odd_pieces):
    width = model.shape[1]
    count = len(odd_pieces)
    return pl.pallas_call(
        edges_body,
        out_shape=jax.ShapeDtypeStruct(base.shape, base.dtype),
        in_specs=[SMEM_SPEC, SMEM_SPEC, ANY_SPEC, VMEM_SPEC, VMEM_SPEC]
        + [ANY_SPEC] * (2 + count),
        out_specs=ANY_SPEC,
        input_output_aliases={5: 0},
        scratch_shapes=[
            pltpu.VMEM((2, 2 * BLK, width), jnp.float32),
            pltpu.VMEM((2, BLK, width), jnp.float32),
            pltpu.VMEM((count, BLK, width), jnp.bfloat16),
            pltpu.SemaphoreType.DMA((2 + count,)),
            pltpu.SemaphoreType.DMA((2,)),
        ],
        compiler_params=pltpu.CompilerParams(vmem_limit_bytes=LARGE),
        cost_estimate=pl.CostEstimate(
            flops=24 * 2 * BLK * BLK * width, bytes_accessed=32 * BLK * width, transcendentals=0
        ),
        name="edges",
    )(me, offset, model, neighbors, face_weight, base, after, *odd_pieces)


def finish_body(me_ref, order_ref, basis_ref, even_ref, odd_ref, base_ref,
                out_ref, token_ref, block_ref, value_ref, got, put, *, offset):
    per_peer = odd_ref.shape[0]
    cols = 2 * per_peer
    fetches, stores = [], []
    for i in range(cols):
        peer = me_ref[0] ^ (offset + i // per_peer)
        cell = order_ref[0, peer * per_peer + i % per_peer]
        fetches.append(pltpu.make_async_copy(base_ref.at[cell], block_ref.at[i], got.at[i]))
        stores.append(pltpu.make_async_copy(block_ref.at[i], out_ref.at[cell], put.at[i]))
    start_all(fetches)
    for i in range(cols):
        wave = even_ref[i] if i < per_peer else odd_ref[i - per_peer]
        both = jnp.concatenate([wave, wave], axis=0)
        value_ref[i] = jnp.dot(basis_ref[...], both, preferred_element_type=jnp.float32)
    wait_all(fetches)
    block_ref[...] += value_ref[...]
    start_all(stores)
    token_ref[...] = jnp.zeros_like(token_ref)
    wait_all(stores)


def finish(me, order, even, odd, base, offset):
    width = odd.shape[2]
    cols = 2 * odd.shape[0]
    basis = haar_matrix(BLK).T.astype(np.float32)
    high = basis.astype(jnp.bfloat16)
    low = (basis - high.astype(np.float32)).astype(jnp.bfloat16)
    basis2 = jnp.asarray(np.concatenate([high, low], axis=1))
    return pl.pallas_call(
        lambda *refs: finish_body(*refs, offset=offset),
        out_shape=[
            jax.ShapeDtypeStruct(base.shape, base.dtype),
            jax.ShapeDtypeStruct((8, BLK), jnp.float32),
        ],
        in_specs=[SMEM_SPEC] * 2 + [VMEM_SPEC] * 3 + [ANY_SPEC],
        out_specs=[ANY_SPEC, VMEM_SPEC],
        input_output_aliases={5: 0},
        scratch_shapes=[
            pltpu.VMEM((cols, BLK, width), jnp.float32),
            pltpu.VMEM((cols, BLK, width), jnp.float32),
            pltpu.SemaphoreType.DMA((cols,)),
            pltpu.SemaphoreType.DMA((cols,)),
        ],
        compiler_params=pltpu.CompilerParams(vmem_limit_bytes=SMALL),
        cost_estimate=pl.CostEstimate(
            flops=4 * cols * BLK * BLK * width, bytes_accessed=10 * cols * BLK * width,
            transcendentals=0,
        ),
        name="finish",
    )(me, order, basis2, even, odd, base)


def merge_body(got_ref, mine_ref, after_ref, out_ref):
    total = got_ref[...].astype(jnp.float32) + mine_ref[...].astype(jnp.float32)
    out_ref[...] = total.astype(out_ref.dtype)


def merge(got, mine, after):
    return pl.pallas_call(
        merge_body,
        out_shape=jax.ShapeDtypeStruct(mine.shape, mine.dtype),
        in_specs=[VMEM_SPEC, VMEM_SPEC, ANY_SPEC],
        out_specs=VMEM_SPEC,
        compiler_params=pltpu.CompilerParams(vmem_limit_bytes=SMALL),
        cost_estimate=pl.CostEstimate(
            flops=mine.size, bytes_accessed=6 * mine.size, transcendentals=0
        ),
        name="merge",
    )(got, mine, after)


def pick_body(take_ref, got_ref, mine_ref, after_ref, *out_refs):
    each = out_refs[0].shape[0]
    for i, out_ref in enumerate(out_refs):
        part = pl.ds(i * each, each)
        out_ref[...] = jnp.where(take_ref[0] > 0, got_ref[part], mine_ref[part])


def pick(take, got, mine, after, parts):
    shape = (mine.shape[0] // parts, *mine.shape[1:])
    return pl.pallas_call(
        pick_body,
        out_shape=[jax.ShapeDtypeStruct(shape, mine.dtype)] * parts,
        in_specs=[SMEM_SPEC, VMEM_SPEC, VMEM_SPEC, ANY_SPEC],
        out_specs=[VMEM_SPEC] * parts,
        compiler_params=pltpu.CompilerParams(vmem_limit_bytes=SMALL),
        cost_estimate=pl.CostEstimate(
            flops=mine.size, bytes_accessed=6 * mine.size, transcendentals=0
        ),
        name="pick",
    )(take, got, mine, after)


def second_half_body(whole_ref, after_ref, out_ref):
    out_ref[...] = whole_ref[out_ref.shape[0] :]


def second_half(whole, after):
    shape = (whole.shape[0] // 2, *whole.shape[1:])
    return pl.pallas_call(
        second_half_body,
        out_shape=jax.ShapeDtypeStruct(shape, whole.dtype),
        in_specs=[VMEM_SPEC, ANY_SPEC],
        out_specs=VMEM_SPEC,
        compiler_params=pltpu.CompilerParams(vmem_limit_bytes=SMALL),
        cost_estimate=pl.CostEstimate(
            flops=0, bytes_accessed=2 * whole.size, transcendentals=0
        ),
        name="second_half",
    )(whole, after)


def line_sums(parts, axis, deliver):
    count = lax.axis_size(axis)
    half = count // 2
    me = lax.axis_index(axis)
    stages = []
    for hop in range(half - 1):
        stages.append(([(hop, hop + 1), (count - 1 - hop, count - 2 - hop)], False))
    stages.append(([(half - 1, half), (half, half - 1)], False))
    for hop in range(half - 1):
        left, right = half - 1 - hop, half + hop
        stages.append(([(left, left - 1), (right, right + 1)], True))
    state = list(parts)
    got = [lax.ppermute(part, axis, stages[0][0]) for part in parts]
    after = parts[0]
    for time in range(len(parts) + len(stages) - 1):
        for s, (pairs, outwards) in enumerate(stages):
            k = time - s
            if not 0 <= k < len(parts):
                continue
            last = s + 1 == len(stages)
            if outwards:
                take = (me == pairs[0][1]) | (me == pairs[1][1])
                take = take.astype(jnp.int32).reshape(1)
                if last:
                    after = deliver(k, take, got[k], state[k], after)
                else:
                    state[k] = jnp.where(take[0] > 0, got[k], state[k])
            else:
                state[k] = after = merge(got[k], state[k], after)
                if last:
                    take = jnp.zeros((1,), jnp.int32)
                    after = deliver(k, take, state[k], state[k], after)
            if not last:
                got[k] = lax.ppermute(state[k], axis, stages[s + 1][0])


def swap(piece, axis, offset):
    return lax.ppermute(piece, axis, [(c, c ^ offset) for c in range(lax.axis_size(axis))])


def local(model_dir, sens_blocks, blk_row, blk_col, blk_count, send_order, neighbors, face_weight):
    cell_count, width = model_dir.shape
    blocks = cell_count // BLK
    peers = lax.axis_size("cols")
    half = peers // 2
    per_peer = blocks // peers
    col = lax.axis_index("cols").astype(jnp.int32)
    me = col.reshape(1)
    offset = (col * cell_count - RIM).reshape(1)
    sens = sens_blocks[0]
    far = far_first(peers)

    *own, odd = analyze(me, send_order, model_dir.reshape(blocks, BLK, width), peers)
    partner = swap(odd, "cols", 1)
    direct = {j: swap(own[j], "cols", 2 * j) for j in far}
    passed = {
        j: swap(partner[j * (per_peer + 1) : (j + 1) * (per_peer + 1)], "cols", 2 * j)
        for j in far
    }
    waves = [own[0], partner, *[direct[j] for j in far], *[passed[j] for j in far]]
    smooth = smoothing(offset, model_dir, neighbors, face_weight, partner)

    even_rows, odd_rows = forward(
        me, blk_row, blk_col, blk_count, sens, waves, (smooth, blocks)
    )
    pair = (even_rows + swap(odd_rows, "cols", 1)).reshape(half, -1, BLK, width)
    to_send = pair.astype(jnp.bfloat16)
    shares = [swap(to_send[j], "cols", 2 * j) for j in far]
    total = pair[0] + sum(share.astype(jnp.float32) for share in shares)
    image_share = total.astype(jnp.bfloat16)
    even_image = jnp.concatenate(
        [image_share] + [swap(image_share, "cols", 2 * j) for j in far], axis=0
    )
    odd_image = swap(even_image, "cols", 1)
    smooth = edges(
        me, offset, model_dir, neighbors, face_weight, smooth, to_send, [partner, *[passed[j] for j in range(1, half)]]
    )

    partial_cols, image = adjoint(
        me, blk_row, blk_col, blk_count, sens, even_image, odd_image, smooth, blocks, peers
    )
    data_image = image.reshape(RB_DEV * BLK, width).astype(jnp.float32)
    normal = smooth.reshape(blocks, BLK, width)
    order = [*far, 0]
    waiting, tokens = [], []

    def end_one(place):
        nonlocal normal
        even, other, j = waiting.pop(place)
        if other is None:
            other = swap(second_half(even, tokens[-1]), "cols", 1)
        normal, token = finish(me, send_order, even, other, normal, 2 * j)
        tokens.append(token)

    def deliver(k, take, got, mine, after):
        j = order[k]
        if j == 0:
            even, other = pick(take, got, mine, after, 2)
            waiting.append((even, swap(other, "cols", 1), j))
            return even
        [total] = pick(take, got, mine, after, 1)
        even = swap(total, "cols", 2 * j)
        other = None if k == half - 2 else swap(even[per_peer:], "cols", 1)
        waiting.append((even, other, j))
        return total

    line_sums([partial_cols[j] for j in order], "rows", deliver)
    for _ in range(half - 2):
        end_one(0)
    while waiting:
        end_one(-1)
    return (data_image, normal.reshape(cell_count, width))


def solution(mesh):
    placed = (
        P("cols", None),
        P("rows", "cols", None, None),
        P("rows", "cols"),
        P("rows", "cols"),
        P("rows", "cols"),
        P("cols", None),
        P(None, "cols"),
        P(None, "cols"),
    )
    return jax.shard_map(
        local,
        mesh=mesh,
        in_specs=placed,
        out_specs=(P("rows", None), P("cols", None)),
        check_vma=False,
    )
```
